32 devices in a mesh: stream: 2 (over core), batch: 16 (over z, y, x).
Axes of the slice: x: 2, y: 2, z: 4, core: 2. Of those that a mesh axis runs over, the one named last changes fastest.
Arguments:
- tokens: bfloat16 [2, 16384, 768], P('stream', 'batch'), may hold values from -6 to 6
- lengths: int32 [2, 16, 8], P('stream', 'batch'), may hold values from 0 to 512, as said below
- attn_weight: float32 [4, 768, 768], P(None, 'batch', 'stream'), may hold values from -0.8660254 to 0.8660254
- attn_moment: float32 [4, 768, 768], P(None, 'batch', 'stream'), may hold values from -7168 to 7168
- attn_average: float32 [4, 768, 768], P(None, 'batch', 'stream'), may hold values from -0.21875 to 0.21875
- up_weight: float32 [768, 3072], P('batch', 'stream'), may hold values from -0.21875 to 0.21875
- up_moment: float32 [768, 3072], P('batch', 'stream'), may hold values from -3072 to 3072
- up_average: float32 [768, 3072], P('batch', 'stream'), may hold values from -0.21875 to 0.21875
- down_weight: float32 [3072, 768], P('batch', 'stream'), may hold values from -0.109375 to 0.109375
- down_moment: float32 [3072, 768], P('batch', 'stream'), may hold values from -4096 to 4096
- down_average: float32 [3072, 768], P('batch', 'stream'), may hold values from -0.109375 to 0.109375
- layer_vectors: float32 [8, 768], P('stream', 'batch'), may hold values from -0.4 to 1.4
- vector_moment: float32 [8, 768], P('stream', 'batch'), may hold values from -10240 to 10240
- vector_average: float32 [8, 768], P('stream', 'batch'), may hold values from -3 to 3
- up_bias: float32 [3072], P(('stream', 'batch')), may hold values from -0.625 to 0.625
- bias_moment: float32 [3072], P(('stream', 'batch')), may hold values from -4096 to 4096
- bias_average: float32 [3072], P(('stream', 'batch')), may hold values from -0.625 to 0.625
- pos_table: float32 [512, 768], P('stream', 'batch'), may hold values from -3 to 3
- pos_moment: float32 [512, 768], P('stream', 'batch'), may hold values from -5120 to 5120
- pos_average: float32 [512, 768], P('stream', 'batch'), may hold values from -3 to 3
Outputs:
- block_out: bfloat16 [2, 16384, 768], P('stream', 'batch')
- input_grad: float32 [2, 16384, 768], P('stream', 'batch')
- attn_grad: float32 [4, 768, 768], P(None, 'batch', 'stream')
- attn_moment_new: float32 [4, 768, 768], P(None, 'batch', 'stream')
- attn_weight_new: float32 [4, 768, 768], P(None, 'batch', 'stream')
- attn_average_new: float32 [4, 768, 768], P(None, 'batch', 'stream')
- up_grad: float32 [768, 3072], P('batch', 'stream')
- up_moment_new: float32 [768, 3072], P('batch', 'stream')
- up_weight_new: float32 [768, 3072], P('batch', 'stream')
- up_average_new: float32 [768, 3072], P('batch', 'stream')
- down_grad: float32 [3072, 768], P('batch', 'stream')
- down_moment_new: float32 [3072, 768], P('batch', 'stream')
- down_weight_new: float32 [3072, 768], P('batch', 'stream')
- down_average_new: float32 [3072, 768], P('batch', 'stream')
- vector_grad: float32 [8, 768], P('stream', 'batch')
- vector_moment_new: float32 [8, 768], P('stream', 'batch')
- vector_new: float32 [8, 768], P('stream', 'batch')
- vector_average_new: float32 [8, 768], P('stream', 'batch')
- bias_grad: float32 [3072], P(('stream', 'batch'))
- bias_moment_new: float32 [3072], P(('stream', 'batch'))
- bias_new: float32 [3072], P(('stream', 'batch'))
- bias_average_new: float32 [3072], P(('stream', 'batch'))
- pos_grad: float32 [512, 768], P('stream', 'batch')
- pos_moment_new: float32 [512, 768], P('stream', 'batch')
- pos_new: float32 [512, 768], P('stream', 'batch')
- pos_average_new: float32 [512, 768], P('stream', 'batch')
The draws below stay inside these ranges and needn't reach their ends.
Inputs may be any that keep to these rules, and one draw needn't show every extreme that they name: `lengths`: for each pair index the two towers have the same number c of used slots, either 2 or 8; the used slots come first, the others are 0; a used slot's length lies between half of and all of 1024 // c, and one used slot of every device is full; in every draw some pair index has c = 2 and some has c = 8.
All inputs are finite; a program needn't handle non-finite values.
Results may differ from the reference program's by a relative error of at most 0.0075.
The reference program's roundings to bfloat16 on the way count: a program that leaves them out, or rounds other values in their place, can miss the bound.
Values may be sent and summed in bfloat16 or wider, within the bound.
No kernel may reach another device: no remote copies, remote signals or barrier semaphores. Data moves between devices by JAX's collectives and lax.ppermute only.
A program may use at most 192 MiB of HBM per device.

```python
import math
import jax
import jax.numpy as jnp
from jax import lax

D = 768
HEADS = 12
HD = 64
FF = 3072
LONG = 512
SLOTS = 8
TOK_DEV = 1024
TOKENS = 16384
N_BATCH = 16


def draw_lengths(key, part):
    key = jax.random.fold_in(key, 11)
    keys = jax.random.split(key, 5)
    picked = jax.random.randint(keys[0], (N_BATCH,), 0, 2)
    first_full = jax.random.randint(keys[1], (), 0, N_BATCH)
    second = (first_full + jax.random.randint(keys[2], (), 1, N_BATCH)) % N_BATCH
    picked = picked.at[first_full].set(1).at[second].set(0)
    counted = jnp.where(picked == 1, SLOTS, 2).astype(jnp.int32)
    bucket = (TOK_DEV // counted)[None, :, None]
    lower = bucket // 2
    raw = jax.random.randint(keys[3], (2, N_BATCH, SLOTS), 0, 1 << 20)
    lengths = lower + raw % (bucket - lower + 1)
    chosen = jax.random.randint(keys[4], (2, N_BATCH), 0, 1 << 20) % counted[None, :]
    slot = jnp.arange(SLOTS, dtype=jnp.int32)[None, None, :]
    lengths = jnp.where(slot == chosen[:, :, None], bucket, lengths)
    lengths = jnp.where(slot < counted[None, :, None], lengths, 0)
    return lengths.astype(jnp.int32)


def draw_attn_weight(key, part):
    key = jax.random.fold_in(key, 37)
    noise = jnp.clip(jax.random.normal(key, (4, D, D), jnp.float32), -6.0, 6.0)
    factor = jnp.where(jnp.arange(4)[:, None, None] == 3, 4.0, 1.0)
    return (noise * factor * D ** (-0.5)).astype(jnp.float32)


def draw_layer_vectors(key, part):
    key = jax.random.fold_in(key, 53)
    noise = jnp.clip(jax.random.normal(key, (8, D), jnp.float32), -4.0, 4.0)
    rows = jnp.arange(8)[:, None]
    is_gain = (rows == 4) | (rows == 6)
    return jnp.where(is_gain, 1.0 + 0.1 * noise, 0.1 * noise).astype(jnp.float32)


def levels(stream_key, shape, shards, smallest, largest):
    loudness = 1.0
    for dim, parts in shards:
        steps = jax.random.uniform(jax.random.fold_in(jax.random.fold_in(stream_key, 6), dim), (parts,), jnp.float32, smallest / len(shards), largest / len(shards))
        loudness = loudness * jnp.repeat(jnp.exp(steps), shape[dim] // parts).reshape((-1,) + (1,) * (len(shape) - 1 - dim))
    return loudness


def gaussian(key, dims, width, reach, cuts=(), held_as=jnp.bfloat16):
    result = jax.random.normal(key, dims, jnp.float32) * width
    if len(cuts) > 0:
        result = levels(key, dims, cuts, -0.22, 0.18) * result
    return jnp.clip(result, min=-reach, max=reach).astype(held_as)


def setup_inputs(seed: int = 0) -> dict:
    streams_of = jax.random.split(jax.random.key(seed), 21)
    tokens = gaussian(streams_of[0], (2, TOKENS, D), 1.0, 6.0, ((0, 2), (1, 16)))
    lengths = draw_lengths(jax.random.fold_in(streams_of[20], 71), 0)
    attn_weight = draw_attn_weight(jax.random.fold_in(streams_of[20], 71), 0)
    attn_moment = gaussian(streams_of[3], (4, D, D), (2816 * (N_BATCH * SLOTS / D) ** 0.5), 7168.0, ((1, 16), (2, 2)), jnp.float32)
    attn_average = gaussian(streams_of[4], (4, D, D), D ** -0.5, 0.21875, ((1, 16), (2, 2)), jnp.float32)
    up_weight = gaussian(streams_of[5], (D, FF), D ** -0.5, 0.21875, ((0, 16), (1, 2)), jnp.float32)
    up_moment = gaussian(streams_of[6], (D, FF), (1280 * (N_BATCH * SLOTS / D) ** 0.5), 3072.0, ((0, 16), (1, 2)), jnp.float32)
    up_average = gaussian(streams_of[7], (D, FF), D ** -0.5, 0.21875, ((0, 16), (1, 2)), jnp.float32)
    down_weight = gaussian(streams_of[8], (FF, D), FF ** -0.5, 0.109375, ((0, 16), (1, 2)), jnp.float32)
    down_moment = gaussian(streams_of[9], (FF, D), (1920 * (N_BATCH * SLOTS / D) ** 0.5), 4096.0, ((0, 16), (1, 2)), jnp.float32)
    down_average = gaussian(streams_of[10], (FF, D), FF ** -0.5, 0.109375, ((0, 16), (1, 2)), jnp.float32)
    layer_vectors = draw_layer_vectors(jax.random.fold_in(streams_of[20], 71), 0)
    vector_moment = gaussian(streams_of[12], (8, D), (4608 * (N_BATCH * SLOTS / D) ** 0.5), 10240.0, ((0, 2), (1, 16)), jnp.float32)
    vector_average = gaussian(streams_of[13], (8, D), 0.5, 3.0, ((0, 2), (1, 16)), jnp.float32)
    up_bias = gaussian(streams_of[14], (FF,), 0.1, 0.625, ((0, 32),), jnp.float32)
    bias_moment = gaussian(streams_of[15], (FF,), (1664 * (N_BATCH * SLOTS / D) ** 0.5), 4096.0, ((0, 32),), jnp.float32)
    bias_average = gaussian(streams_of[16], (FF,), 0.1, 0.625, ((0, 32),), jnp.float32)
    pos_table = gaussian(streams_of[17], (LONG, D), 0.5, 3.0, ((0, 2), (1, 16)), jnp.float32)
    pos_moment = gaussian(streams_of[18], (LONG, D), (2304 * (N_BATCH * SLOTS / D) ** 0.5), 5120.0, ((0, 2), (1, 16)), jnp.float32)
    pos_average = gaussian(streams_of[19], (LONG, D), 0.5, 3.0, ((0, 2), (1, 16)), jnp.float32)
    return {"tokens": tokens, "lengths": lengths, "attn_weight": attn_weight, "attn_moment": attn_moment, "attn_average": attn_average, "up_weight": up_weight, "up_moment": up_moment, "up_average": up_average, "down_weight": down_weight, "down_moment": down_moment, "down_average": down_average, "layer_vectors": layer_vectors, "vector_moment": vector_moment, "vector_average": vector_average, "up_bias": up_bias, "bias_moment": bias_moment, "bias_average": bias_average, "pos_table": pos_table, "pos_moment": pos_moment, "pos_average": pos_average}


@jax.custom_vjp
def low(v):
    return lax.optimization_barrier(v.astype(jnp.bfloat16)).astype(jnp.float32)

@jax.custom_vjp
def low_back(v):
    return v

def low_keep(v):
    return (low(v), None)

def low_pass(kept, grad):
    return (grad,)

def back_keep(v):
    return (v, None)

def back_low(kept, grad):
    return (low(grad),)
low.defvjp(low_keep, low_pass)
low_back.defvjp(back_keep, back_low)
EPS_NORM = 1e-06
INV_TEMP = 100.0
LOSS_WEIGHT = 256.0
MOMENTUM = 0.5
AVERAGE = 0.5
RATE = 0.0001
POS_RATE = 0.01
NEGATIVE = -1e+30
ROOT_HALF = 0.7071067811865476

def hdot(left, right):
    return jnp.dot(left, right, precision=lax.Precision.HIGHEST)

def gelu_value(values):
    return 0.5 * values * (1.0 + lax.erf(values * ROOT_HALF))

def layer_norm(values, gain_row, shift_row):
    center = values - lax.optimization_barrier(jnp.mean(values, axis=-1, keepdims=True))
    inverse = lax.rsqrt(lax.optimization_barrier(jnp.mean(center * center, axis=-1, keepdims=True)) + EPS_NORM)
    return center * inverse * gain_row + shift_row

def layout(lengths_row):
    counted = jnp.sum((lengths_row > 0).astype(jnp.int32)).astype(jnp.int32)
    bucket = (TOK_DEV // counted).astype(jnp.int32)
    places = jnp.arange(TOK_DEV, dtype=jnp.int32)
    document = places // bucket
    position = places - document * bucket
    member = document[:, None] == jnp.arange(SLOTS, dtype=jnp.int32)[None, :]
    slot_length = lax.optimization_barrier(jnp.sum(jnp.where(member, lengths_row[None, :], 0), axis=1))
    present = position < slot_length
    allowed = (document[:, None] == document[None, :]) & present[None, :]
    return (position, present, member, allowed)

def block_forward(weights, inputs, lengths_row):
    attn_half, up_half, down_half, vectors, up_bias_half, pos_half = weights
    position, present, member, allowed = layout(lengths_row)
    score_scale = 1.0 / math.sqrt(HD)
    hidden0 = inputs + jnp.take(pos_half, position, axis=0)
    entry = low(hidden0)
    queries = low(low_back(hdot(entry, attn_half[0])) + vectors[0]).reshape(TOK_DEV, HEADS, HD)
    key_rows = low(low_back(hdot(entry, attn_half[1]))).reshape(TOK_DEV, HEADS, HD)
    value_rows = low(low_back(hdot(entry, attn_half[2])) + vectors[1]).reshape(TOK_DEV, HEADS, HD)
    scores = low_back(jnp.einsum('qhd,khd->hqk', queries, key_rows, precision=lax.Precision.HIGHEST) * score_scale)
    scores = jnp.where(allowed[None], scores, NEGATIVE)
    probs = jax.nn.softmax(scores, axis=-1)
    context = jnp.einsum('hqk,khd->qhd', low(probs), value_rows, precision=lax.Precision.HIGHEST).reshape(TOK_DEV, D)
    context = low(low_back(context))
    resid1 = hidden0 + low_back(hdot(context, attn_half[3])) + vectors[2]
    hidden1 = layer_norm(resid1, vectors[4], vectors[5])
    entry2 = low(hidden1)
    pre_act = low_back(hdot(entry2, up_half)) + up_bias_half
    active = low(gelu_value(pre_act))
    resid2 = hidden1 + low_back(hdot(active, down_half)) + vectors[3]
    hidden2 = layer_norm(resid2, vectors[6], vectors[7])
    inverse_len = 1.0 / jnp.maximum(lengths_row, 1).astype(jnp.float32)
    pool = jnp.where(member & present[:, None], inverse_len[None, :], 0.0)
    pooled = hdot(pool.T, hidden2)
    return (hidden2, pooled)

def contrast(rows, columns, row_live, column_live):
    logits = low_back(hdot(rows, columns.T) * INV_TEMP)
    logits = jnp.where(column_live[None, :], logits, NEGATIVE)
    spread_sum = jax.nn.logsumexp(logits, axis=1)
    diagonal = jnp.diagonal(logits)
    return jnp.sum(jnp.where(row_live, spread_sum - diagonal, 0.0))

def renew(grad, moment, weight, average, rate):
    moment_new = MOMENTUM * moment + grad
    weight_new = weight - rate * (grad + MOMENTUM * moment_new)
    average_new = AVERAGE * average + (1.0 - AVERAGE) * weight_new
    return (grad, moment_new, weight_new, average_new)

def reference(tokens, lengths, attn_weight, attn_moment, attn_average, up_weight, up_moment, up_average, down_weight, down_moment, down_average, layer_vectors, vector_moment, vector_average, up_bias, bias_moment, bias_average, pos_table, pos_moment, pos_average):
    params = (attn_weight, up_weight, down_weight, layer_vectors, up_bias, pos_table)
    inputs = tokens.astype(jnp.float32).reshape(2 * N_BATCH, TOK_DEV, D)
    lens_all = lengths.reshape(2 * N_BATCH, SLOTS)
    live = lengths.reshape(2, N_BATCH * SLOTS) > 0

    def objective(weights, values):
        halves = tuple((low(item) for item in weights))
        checked = jax.checkpoint(block_forward)

        def visit(item):
            return checked(halves, item[0], item[1])
        outputs, pooled_all = lax.map(visit, (values, lens_all))
        pooled = pooled_all.reshape(2, N_BATCH * SLOTS, D)
        units = low(pooled * lax.rsqrt(lax.optimization_barrier(jnp.sum(pooled * pooled, axis=-1, keepdims=True)) + EPS_NORM))
        total = contrast(units[0], units[1], live[0], live[1]) + contrast(units[1], units[0], live[1], live[0])
        return (LOSS_WEIGHT * total, outputs)
    loss_value, pullback, outputs = jax.vjp(objective, params, inputs, has_aux=True)
    grads, input_grad = pullback(jnp.ones((), jnp.float32))
    block_out = outputs.reshape(2, N_BATCH * TOK_DEV, D).astype(jnp.bfloat16)
    input_grad = input_grad.reshape(2, N_BATCH * TOK_DEV, D)
    attn_all = renew(grads[0], attn_moment, attn_weight, attn_average, RATE)
    up_all = renew(grads[1], up_moment, up_weight, up_average, RATE)
    down_all = renew(grads[2], down_moment, down_weight, down_average, RATE)
    vector_all = renew(grads[3], vector_moment, layer_vectors, vector_average, RATE)
    bias_all = renew(grads[4], bias_moment, up_bias, bias_average, RATE)
    pos_all = renew(grads[5], pos_moment, pos_table, pos_average, POS_RATE)
    return (block_out, input_grad, attn_all[0], attn_all[1], attn_all[2], attn_all[3], up_all[0], up_all[1], up_all[2], up_all[3], down_all[0], down_all[1], down_all[2], down_all[3], vector_all[0], vector_all[1], vector_all[2], vector_all[3], bias_all[0], bias_all[1], bias_all[2], bias_all[3], pos_all[0], pos_all[1], pos_all[2], pos_all[3])
```

```python
import math

import jax
import jax.numpy as jnp
from jax import lax
from jax.sharding import PartitionSpec as P

HEADS = 12


EPS_NORM = 1e-06
INV_TEMP = 100.0
LOSS_WEIGHT = 256.0
MOMENTUM = 0.5
AVERAGE = 0.5
RATE = 0.0001
POS_RATE = 0.01
NEGATIVE = -1e30
ROOT_HALF = 0.7071067811865476
ROOT_TWO_PI = 2.5066282746310002


def exchanged(block, axis, bit):
    count = lax.axis_size(axis)
    route = [(place, place ^ (1 << bit)) for place in range(count)]
    return lax.ppermute(block, axis, route)


def bit_at(axis, bit):
    return (lax.axis_index(axis) >> bit) & 1


def batch_bits():
    return lax.axis_size("batch").bit_length() - 1


def joined(mine, other, upper, dim):
    low = jnp.where(upper, other, mine)
    high = jnp.where(upper, mine, other)
    return jnp.stack([low, high], axis=dim)


def gather_pair(block):
    bits = batch_bits()
    for depth, bit in enumerate(range(bits - 1, 1, -1)):
        other = exchanged(block, "batch", bit)
        block = joined(block, other, bit_at("batch", bit) == 1, depth)
    halves = []
    depth = bits - 2
    first = jnp.take(block, 0, axis=depth)
    second = jnp.take(block, 1, axis=depth)
    first_other = exchanged(first, "batch", 1)
    second_other = exchanged(second, "batch", 0)
    first = joined(first, first_other, bit_at("batch", 1) == 1, depth)
    second = joined(second, second_other, bit_at("batch", 0) == 1, depth)
    first_other = exchanged(first, "batch", 0)
    second_other = exchanged(second, "batch", 1)
    first = joined(first, first_other, bit_at("batch", 0) == 1, depth + 1)
    second = joined(second, second_other, bit_at("batch", 1) == 1, depth)
    shape = (-1, block.shape[-1])
    return first.reshape(shape), second.reshape(shape)


def packed(values, wide):
    if not wide:
        return halved(values)
    plain, kept = values[..., :-wide], values[..., -wide:]
    coarse = lax.reduce_precision(kept, exponent_bits=8, mantissa_bits=7)
    return halved(jnp.concatenate([plain, coarse, kept - coarse], axis=-1))


def unpacked(block, wide):
    values = block.astype(jnp.float32)
    if not wide:
        return values
    plain, coarse, rest = values[..., : -2 * wide], values[..., -2 * wide : -wide], values[..., -wide:]
    return jnp.concatenate([plain, coarse + rest], axis=-1)


def fold(block, axis, bit, dim, wide=0):
    upper = bit_at(axis, bit)
    sent = packed(lax.dynamic_index_in_dim(block, 1 - upper, dim, keepdims=False), wide)
    kept = lax.dynamic_index_in_dim(block, upper, dim, keepdims=False)
    return kept + unpacked(exchanged(sent, axis, bit), wide)


def scatter_pair(first, second, wide=0):
    bits = batch_bits()
    shape = (2,) * bits + (first.shape[0] >> bits,)
    first, second = (part.reshape(shape + part.shape[1:]) for part in (first, second))
    first = fold(first, "batch", 0, bits - 1)
    second = fold(second, "batch", 1, bits - 2, wide)
    first = fold(first, "batch", 1, bits - 2)
    second = fold(second, "batch", 0, bits - 2, wide)
    block = jnp.concatenate([first, second], axis=-1)
    for bit in range(2, bits):
        block = fold(block, "batch", bit, bits - 1 - bit, wide)
    return block


def columns_split(block):
    half = block.shape[1] // 2
    return jnp.stack([block[:, :half], block[:, half:]])


def columns_joined(pair):
    return jnp.concatenate([pair[0], pair[1]], axis=1)


def both_cores(block):
    other = exchanged(block, "stream", 0)
    upper = lax.axis_index("stream") == 1
    return jnp.where(upper, other, block), jnp.where(upper, block, other)


def halved(values):
    return values.astype(jnp.bfloat16)


def matmul(left, right):
    return jnp.dot(left, right, preferred_element_type=jnp.float32)


def gelu_value(values):
    return 0.5 * values * (1.0 + lax.erf(values * ROOT_HALF))


def gelu_slope(values):
    return (
        0.5 * (1.0 + lax.erf(values * ROOT_HALF))
        + values * jnp.exp(-0.5 * values * values) / ROOT_TWO_PI
    )


def layout(lengths_row, token_count):
    slot_count = lengths_row.shape[0]
    counted = jnp.sum((lengths_row > 0).astype(jnp.int32))
    bucket = token_count // counted
    places = jnp.arange(token_count, dtype=jnp.int32)
    document = places // bucket
    position = places - document * bucket
    member = document[:, None] == jnp.arange(slot_count, dtype=jnp.int32)[None, :]
    slot_length = jnp.sum(jnp.where(member, lengths_row[None, :], 0), axis=1)
    present = position < slot_length
    return (counted, position, present, member)


def norm_forward(values, gain_row, shift_row):
    center = values - jnp.mean(values, axis=-1, keepdims=True)
    inverse = lax.rsqrt(jnp.mean(center * center, axis=-1, keepdims=True) + EPS_NORM)
    normed = center * inverse
    return (normed * gain_row + shift_row, normed, inverse)


def norm_backward(grad_out, normed, inverse, gain_row):
    scaled = grad_out * gain_row
    inner = (
        scaled
        - jnp.mean(scaled, axis=-1, keepdims=True)
        - normed * jnp.mean(scaled * normed, axis=-1, keepdims=True)
    )
    return (inner * inverse, jnp.sum(grad_out * normed, axis=0), jnp.sum(grad_out, axis=0))


def slot_forward(query_half, key_half, value_half, present, slots, score_scale):
    token_count, heads, size = query_half.shape
    bucket = token_count // slots
    queries = query_half.reshape(slots, bucket, heads, size)
    keys = key_half.reshape(slots, bucket, heads, size)
    values = value_half.reshape(slots, bucket, heads, size)
    scores = (
        jnp.einsum("sqhd,skhd->shqk", queries, keys, preferred_element_type=jnp.float32)
        * score_scale
    )
    scores = jnp.where(present.reshape(slots, 1, 1, bucket), scores, NEGATIVE)
    highest = jnp.max(scores, axis=-1, keepdims=True)
    weights = jnp.exp(scores - highest)
    totals = jnp.sum(weights, axis=-1, keepdims=True)
    probs_half = halved(weights / totals)
    context = jnp.einsum(
        "shqk,skhd->sqhd", probs_half, values, preferred_element_type=jnp.float32
    ).reshape(token_count, heads, size)
    logsum = (
        (highest[..., 0] + jnp.log(totals[..., 0])).transpose(0, 2, 1).reshape(token_count, heads)
    )
    return (context, logsum)


def slot_backward(query_half, key_half, value_half, present, logsum, grad_half, slots, score_scale):
    token_count, heads, size = query_half.shape
    bucket = token_count // slots
    queries = query_half.reshape(slots, bucket, heads, size)
    keys = key_half.reshape(slots, bucket, heads, size)
    values = value_half.reshape(slots, bucket, heads, size)
    grads = grad_half.reshape(slots, bucket, heads, size)
    kept = logsum.reshape(slots, bucket, heads).transpose(0, 2, 1)[..., None]
    scores = (
        jnp.einsum("sqhd,skhd->shqk", queries, keys, preferred_element_type=jnp.float32)
        * score_scale
    )
    scores = jnp.where(present.reshape(slots, 1, 1, bucket), scores, NEGATIVE)
    probs = jnp.exp(scores - kept)
    dprob = jnp.einsum("sqhd,skhd->shqk", grads, values, preferred_element_type=jnp.float32)
    rowdot = jnp.sum(probs * dprob, axis=-1, keepdims=True)
    dscore = halved(probs * (dprob - rowdot))
    dquery = (
        jnp.einsum("shqk,skhd->sqhd", dscore, keys, preferred_element_type=jnp.float32)
        * score_scale
    )
    dkey = (
        jnp.einsum("shqk,sqhd->skhd", dscore, queries, preferred_element_type=jnp.float32)
        * score_scale
    )
    dvalue = jnp.einsum("shqk,sqhd->skhd", halved(probs), grads, preferred_element_type=jnp.float32)
    shape = (token_count, heads * size)
    return (dquery.reshape(shape), dkey.reshape(shape), dvalue.reshape(shape))


def renew(grad, moment, weight, average, rate):
    moment_new = MOMENTUM * moment + grad
    weight_new = weight - rate * (grad + MOMENTUM * moment_new)
    average_new = AVERAGE * average + (1.0 - AVERAGE) * weight_new
    return (grad, moment_new, weight_new, average_new)


def local(
    tokens,
    lengths,
    attn_weight,
    attn_moment,
    attn_average,
    up_weight,
    up_moment,
    up_average,
    down_weight,
    down_moment,
    down_average,
    layer_vectors,
    vector_moment,
    vector_average,
    up_bias,
    bias_moment,
    bias_average,
    pos_table,
    pos_moment,
    pos_average,
):
    rows = up_weight.shape[0]
    live_row = (lengths[0, 0] > 0).astype(jnp.float32)
    misc = jnp.concatenate(
        [
            layer_vectors.T,
            up_bias.reshape(rows, 2),
            jnp.broadcast_to(live_row[None, :], (rows, live_row.shape[0])),
        ],
        axis=1,
    )
    misc = jnp.pad(misc, ((0, 0), (0, 128 - misc.shape[1])))
    entry_block = halved(
        jnp.concatenate(
            [attn_weight[0], attn_weight[1], attn_weight[2], pos_table.T, misc], axis=1
        )
    )
    middle_block = halved(
        jnp.concatenate(
            [up_weight, attn_weight[3], jnp.zeros((rows, 128), jnp.float32)], axis=1
        )
    )
    entry_both = both_cores(columns_joined(gather_pair(columns_split(entry_block))))
    middle_both = both_cores(columns_joined(gather_pair(columns_split(middle_block))))
    down_both = lax.all_gather(halved(down_weight), ("stream", "batch"), axis=0, tiled=True)
    quarter = attn_weight.shape[2]
    hidden_half = up_weight.shape[1]
    attn_full = [
        jnp.concatenate([part[:, k * quarter : (k + 1) * quarter] for part in entry_both], axis=1)
        for k in range(3)
    ]
    attn_full.append(
        jnp.concatenate(
            [part[:, hidden_half : hidden_half + quarter] for part in middle_both], axis=1
        )
    )
    up_full = jnp.concatenate([part[:, :hidden_half] for part in middle_both], axis=1)
    down_full = jnp.concatenate(
        [down_both[: down_both.shape[0] // 2], down_both[down_both.shape[0] // 2 :]], axis=1
    )
    pos_at = 3 * quarter
    misc_at = pos_at + pos_table.shape[0]
    pos_full = jnp.concatenate([part[:, pos_at:misc_at].T for part in entry_both], axis=0)
    vectors = jnp.concatenate(
        [part[:, misc_at : misc_at + 4].T for part in entry_both], axis=0
    ).astype(jnp.float32)
    bias_row = jnp.concatenate(
        [part[:, misc_at + 4 : misc_at + 6].reshape(-1) for part in entry_both]
    ).astype(jnp.float32)
    slots_at = misc_at + 6
    lives = [
        part[::rows, slots_at : slots_at + live_row.shape[0]].reshape(-1) > 0
        for part in entry_both
    ]
    inputs = tokens[0].astype(jnp.float32)
    lengths_row = lengths[0, 0]
    token_count, width = inputs.shape
    slot_count = lengths_row.shape[0]
    head_size = width // HEADS
    score_scale = 1.0 / math.sqrt(head_size)
    counted, position, present, member = layout(lengths_row, token_count)
    long_rows = token_count // 2
    short_rows = token_count // slot_count
    short_tiled = jnp.tile(pos_full[:short_rows], (long_rows // short_rows, 1))
    pos_rows = jnp.where(counted == 2, pos_full, short_tiled).astype(jnp.float32)
    hidden0 = (inputs.reshape(2, long_rows, width) + pos_rows[None]).reshape(token_count, width)
    entry = halved(hidden0)
    triple = [matmul(entry, attn_full[k]) for k in range(3)]
    query_half = halved(triple[0] + vectors[0]).reshape(token_count, HEADS, head_size)
    key_half = halved(triple[1]).reshape(token_count, HEADS, head_size)
    value_half = halved(triple[2] + vectors[1]).reshape(token_count, HEADS, head_size)
    context, logsum = lax.cond(
        counted == 2,
        lambda: slot_forward(query_half, key_half, value_half, present, 2, score_scale),
        lambda: slot_forward(query_half, key_half, value_half, present, slot_count, score_scale),
    )
    context_half = halved(context.reshape(token_count, width))
    resid1 = hidden0 + matmul(context_half, attn_full[3]) + vectors[2]
    hidden1, normed1, inverse1 = norm_forward(resid1, vectors[4], vectors[5])
    entry2 = halved(hidden1)
    pre_act = matmul(entry2, up_full) + bias_row
    active_half = halved(gelu_value(pre_act))
    resid2 = hidden1 + matmul(active_half, down_full) + vectors[3]
    hidden2, normed2, inverse2 = norm_forward(resid2, vectors[6], vectors[7])
    inverse_len = 1.0 / jnp.maximum(lengths_row, 1).astype(jnp.float32)
    pool = jnp.where(member & present[:, None], inverse_len[None, :], 0.0)
    pooled = jnp.dot(pool.T, hidden2, precision=lax.Precision.HIGHEST)
    inverse_norm = lax.rsqrt(jnp.sum(pooled * pooled, axis=-1, keepdims=True) + EPS_NORM)
    unit_half = halved(pooled * inverse_norm)
    batch_index = lax.axis_index("batch")
    pair_total = lax.axis_size("batch") * slot_count
    units = unit_half
    for depth, bit in enumerate(range(batch_bits() - 1, -1, -1)):
        units = joined(
            units, exchanged(units, "batch", bit), bit_at("batch", bit) == 1, depth
        )
    units = units.reshape(pair_total, width)
    others = exchanged(units, "stream", 0)
    upper = lax.axis_index("stream") == 1
    own_live = jnp.where(upper, lives[1], lives[0])
    other_live = jnp.where(upper, lives[0], lives[1])
    own_rows = batch_index * slot_count + jnp.arange(slot_count, dtype=jnp.int32)
    all_rows = jnp.arange(pair_total, dtype=jnp.int32)
    row_live = (lengths_row > 0).astype(jnp.float32)

    def loss_grad(rows, columns, rows_at, rows_live, columns_live):
        logits = (
            jnp.einsum("sd,md->sm", rows, columns, preferred_element_type=jnp.float32) * INV_TEMP
        )
        logits = jnp.where(columns_live[None, :], logits, NEGATIVE)
        highest = jnp.max(logits, axis=-1, keepdims=True)
        weights = jnp.exp(logits - highest)
        probs = weights / jnp.sum(weights, axis=-1, keepdims=True)
        target = (all_rows[None, :] == rows_at[:, None]).astype(jnp.float32)
        return halved(LOSS_WEIGHT * (probs - target) * rows_live[:, None])

    dlogit_own = loss_grad(unit_half, others, own_rows, row_live, other_live)
    dlogit_all = loss_grad(others, units, all_rows, other_live.astype(jnp.float32), own_live)
    dlogit_in = lax.dynamic_slice_in_dim(dlogit_all, batch_index * slot_count, slot_count, 1)
    dunit = INV_TEMP * (
        matmul(dlogit_own, others)
        + jnp.einsum("ms,md->sd", dlogit_in, others, preferred_element_type=jnp.float32)
    )
    along = jnp.sum(pooled * dunit, axis=-1, keepdims=True)
    dpooled = inverse_norm * dunit - inverse_norm * inverse_norm * inverse_norm * pooled * along
    dhidden2 = jnp.dot(pool, dpooled, precision=lax.Precision.HIGHEST)
    dresid2, dgain2, dshift2 = norm_backward(dhidden2, normed2, inverse2, vectors[6])
    dresid2_half = halved(dresid2)
    down_grad = jnp.einsum(
        "tf,td->fd", active_half, dresid2_half, preferred_element_type=jnp.float32
    )
    dactive = jnp.einsum("td,fd->tf", dresid2_half, down_full, preferred_element_type=jnp.float32)
    dpre = dactive * gelu_slope(pre_act)
    dpre_half = halved(dpre)
    up_grad = jnp.einsum("td,tf->df", entry2, dpre_half, preferred_element_type=jnp.float32)
    dhidden1 = dresid2 + jnp.einsum(
        "tf,df->td", dpre_half, up_full, preferred_element_type=jnp.float32
    )
    dresid1, dgain1, dshift1 = norm_backward(dhidden1, normed1, inverse1, vectors[4])
    dresid1_half = halved(dresid1)
    out_grad = jnp.einsum(
        "td,te->de", context_half, dresid1_half, preferred_element_type=jnp.float32
    )
    dcontext_half = halved(
        jnp.einsum("te,de->td", dresid1_half, attn_full[3], preferred_element_type=jnp.float32)
    ).reshape(token_count, HEADS, head_size)
    dquery, dkey, dvalue = lax.cond(
        counted == 2,
        lambda: slot_backward(
            query_half, key_half, value_half, present, logsum, dcontext_half, 2, score_scale
        ),
        lambda: slot_backward(
            query_half,
            key_half,
            value_half,
            present,
            logsum,
            dcontext_half,
            slot_count,
            score_scale,
        ),
    )
    dtriple_half = [halved(part) for part in (dquery, dkey, dvalue)]
    in_grads = [
        jnp.einsum("td,te->de", entry, part, preferred_element_type=jnp.float32)
        for part in dtriple_half
    ]
    dhidden0 = dresid1 + sum(
        jnp.einsum("te,de->td", part, attn_full[k], preferred_element_type=jnp.float32)
        for k, part in enumerate(dtriple_half)
    )
    long_sum = jnp.sum(dhidden0.reshape(2, long_rows, width), axis=0)
    short_sum = jnp.sum(long_sum.reshape(-1, short_rows, width), axis=0)
    short_full = jnp.pad(short_sum, ((0, long_rows - short_rows), (0, 0)))
    pos_columns = jnp.where(counted == 2, long_sum, short_full).T
    vector_columns = jnp.stack(
        [
            jnp.sum(dquery, axis=0),
            jnp.sum(dvalue, axis=0),
            jnp.sum(dresid1, axis=0),
            jnp.sum(dresid2, axis=0),
            dgain1,
            dshift1,
            dgain2,
            dshift2,
        ],
        axis=1,
    )
    bias_columns = jnp.sum(dpre, axis=0).reshape(2, width, 2)
    down_rows = down_weight.shape[0] // 2

    def down_part(s):
        part = down_grad[:, s * quarter : (s + 1) * quarter].reshape(-1, 2, down_rows, quarter)
        return (part[:, 0].reshape(-1, quarter), part[:, 1].reshape(-1, quarter))

    def middle_part(s):
        block = jnp.concatenate(
            [
                up_grad[:, s * hidden_half : (s + 1) * hidden_half],
                out_grad[:, s * quarter : (s + 1) * quarter],
                jnp.zeros((width, 128), jnp.float32),
            ],
            axis=1,
        )
        return (block[:, : block.shape[1] // 2], block[:, block.shape[1] // 2 :])

    def entry_part(s):
        columns = [part[:, s * quarter : (s + 1) * quarter] for part in in_grads]
        misc_grad = jnp.concatenate(
            [
                vector_columns[:, 4 * s : 4 * s + 4],
                bias_columns[s],
                jnp.zeros((width, 58), jnp.float32),
            ],
            axis=1,
        )
        pos_part = pos_columns[:, s * (long_rows // 2) : (s + 1) * (long_rows // 2)]
        return (
            jnp.concatenate(columns[:2], axis=1),
            jnp.concatenate([columns[2], pos_part, misc_grad], axis=1),
        )

    def reduced(part, wide=0):
        first, second = part(0), part(1)
        return scatter_pair(
            fold(jnp.stack([first[0], second[0]]), "stream", 0, 0),
            fold(jnp.stack([first[1], second[1]]), "stream", 0, 0, wide),
            wide,
        )

    down_sum = reduced(down_part)
    down_sum = jnp.concatenate([down_sum[:, :quarter], down_sum[:, quarter:]], axis=0)
    middle_sum = reduced(middle_part)
    entry_sum = reduced(entry_part, 64)
    attn_sum = jnp.stack(
        [entry_sum[:, k * quarter : (k + 1) * quarter] for k in range(3)]
        + [middle_sum[:, hidden_half : hidden_half + quarter]]
    )
    reduced = (
        attn_sum,
        middle_sum[:, :hidden_half],
        down_sum,
        entry_sum[:, misc_at : misc_at + 4].T,
        entry_sum[:, misc_at + 4 : misc_at + 6].reshape(-1),
        entry_sum[:, pos_at:misc_at].T,
    )
    attn_all = renew(reduced[0], attn_moment, attn_weight, attn_average, RATE)
    up_all = renew(reduced[1], up_moment, up_weight, up_average, RATE)
    down_all = renew(reduced[2], down_moment, down_weight, down_average, RATE)
    vector_all = renew(reduced[3], vector_moment, layer_vectors, vector_average, RATE)
    bias_all = renew(reduced[4].reshape(-1), bias_moment, up_bias, bias_average, RATE)
    pos_all = renew(reduced[5], pos_moment, pos_table, pos_average, POS_RATE)
    return (
        halved(hidden2)[None],
        dhidden0[None],
        attn_all[0],
        attn_all[1],
        attn_all[2],
        attn_all[3],
        up_all[0],
        up_all[1],
        up_all[2],
        up_all[3],
        down_all[0],
        down_all[1],
        down_all[2],
        down_all[3],
        vector_all[0],
        vector_all[1],
        vector_all[2],
        vector_all[3],
        bias_all[0],
        bias_all[1],
        bias_all[2],
        bias_all[3],
        pos_all[0],
        pos_all[1],
        pos_all[2],
        pos_all[3],
    )


def solution(mesh):
    in_specs = (
        P("stream", "batch", None),
        P("stream", "batch", None),
        P(None, "batch", "stream"),
        P(None, "batch", "stream"),
        P(None, "batch", "stream"),
        P("batch", "stream"),
        P("batch", "stream"),
        P("batch", "stream"),
        P("batch", "stream"),
        P("batch", "stream"),
        P("batch", "stream"),
        P("stream", "batch"),
        P("stream", "batch"),
        P("stream", "batch"),
        P(("stream", "batch")),
        P(("stream", "batch")),
        P(("stream", "batch")),
        P("stream", "batch"),
        P("stream", "batch"),
        P("stream", "batch"),
    )
    out_specs = (
        P("stream", "batch", None),
        P("stream", "batch", None),
        P(None, "batch", "stream"),
        P(None, "batch", "stream"),
        P(None, "batch", "stream"),
        P(None, "batch", "stream"),
        P("batch", "stream"),
        P("batch", "stream"),
        P("batch", "stream"),
        P("batch", "stream"),
        P("batch", "stream"),
        P("batch", "stream"),
        P("batch", "stream"),
        P("batch", "stream"),
        P("stream", "batch"),
        P("stream", "batch"),
        P("stream", "batch"),
        P("stream", "batch"),
        P(("stream", "batch")),
        P(("stream", "batch")),
        P(("stream", "batch")),
        P(("stream", "batch")),
        P("stream", "batch"),
        P("stream", "batch"),
        P("stream", "batch"),
        P("stream", "batch"),
    )
    return jax.shard_map(local, mesh=mesh, in_specs=in_specs, out_specs=out_specs, check_vma=False)
```

```python
import functools
import math

import jax
import jax.numpy as jnp
from jax import lax
from jax.experimental import pallas as pl
from jax.experimental.pallas import tpu as pltpu
from jax.sharding import PartitionSpec as P

HEADS = 12


EPS_NORM = 1e-06
INV_TEMP = 100.0
LOSS_WEIGHT = 256.0
MOMENTUM = 0.5
AVERAGE = 0.5
RATE = 0.0001
POS_RATE = 0.01
NEGATIVE = -1e30
ROOT_HALF = 0.7071067811865476
ROOT_TWO_PI = 2.5066282746310002
LANES = 128
VMEM = 56 << 20
NN = (((1,), (0,)), ((), ()))
NT = (((1,), (1,)), ((), ()))
TN = (((0,), (0,)), ((), ()))


def halved(values):
    return values.astype(jnp.bfloat16)


def matmul(left, right, dims=NN):
    return lax.dot_general(left, right, dims, preferred_element_type=jnp.float32)


def stacked(*shape, dtype=jnp.float32):
    return jax.ShapeDtypeStruct(shape, dtype)


def in_order(*values):
    return lax.optimization_barrier(values)


def exchanged(block, axis, mask):
    count = lax.axis_size(axis)
    return lax.ppermute(block, axis, [(place, place ^ mask) for place in range(count)])


def position():
    batch = lax.axis_index("batch")
    return jnp.stack([lax.axis_index("stream"), batch & 1, (batch >> 1) & 1, batch >> 2])


def gathered(block, cut):
    bits = lax.axis_size("batch").bit_length() - 1
    blocks, masks, bit = block[None], [0], bits
    while bit > 2:
        step = min(2, bit - 2)
        bit -= step
        offsets = [d << bit for d in range(1 << step)]
        blocks = jnp.concatenate(
            [blocks] + [exchanged(blocks, "batch", offset) for offset in offsets[1:]], axis=0
        )
        masks = [offset | mask for offset in offsets for mask in masks]
    first, second = blocks[:, :, :cut], blocks[:, :, cut:]
    first_masks, second_masks = masks, masks
    for one, two in ((2, 1), (1, 2)):
        first_in, second_in = exchanged(first, "batch", one), exchanged(second, "batch", two)
        first = jnp.concatenate([first, first_in], axis=0)
        second = jnp.concatenate([second, second_in], axis=0)
        first_masks = first_masks + [one | mask for mask in first_masks]
        second_masks = second_masks + [two | mask for mask in second_masks]
    return (first, first_masks), (second, second_masks)


def place_kernel(moves, count, at_ref, *refs):
    sources, targets = refs[:count], refs[count:]
    stream = at_ref[0]
    batch = at_ref[1] + 2 * at_ref[2] + 4 * at_ref[3]
    for source, entry, mask, columns, target, lead, other, start, span in moves:
        core = stream ^ other
        low = pl.multiple_of(start + core * span, LANES) if span else start
        at = (batch ^ mask, slice(None), pl.ds(low, columns[1] - columns[0]))
        if lead == "relative":
            at = (other,) + at
        elif lead == "stream":
            at = (core,) + at
        targets[target][at] = sources[source][entry, :, columns[0] : columns[1]]


def placed(at, sources, moves, shapes):
    held = pl.BlockSpec(memory_space=pltpu.VMEM)
    return pl.pallas_call(
        functools.partial(place_kernel, moves, len(sources)),
        in_specs=[pl.BlockSpec(memory_space=pltpu.SMEM)] + [held] * len(sources),
        out_specs=[held] * len(shapes),
        out_shape=shapes,
        compiler_params=pltpu.CompilerParams(vmem_limit_bytes=VMEM),
        cost_estimate=pl.CostEstimate(flops=0, bytes_accessed=10 << 20, transcendentals=0),
    )(at, *sources)


def spread(at, block, cut, pieces, shapes):
    halves = gathered(block, cut)
    sources, moves = [], []
    for other in range(2):
        for side, (part, masks) in enumerate(halves):
            sources.append(exchanged(part, "stream", 1) if other else part)
            base = cut * side
            for start, stop, target, lead, offset, span in pieces:
                low, high = max(start, base), min(stop, base + part.shape[2])
                if low >= high:
                    continue
                for entry, mask in enumerate(masks):
                    moves.append(
                        (len(sources) - 1, entry, mask, (low - base, high - base), target, lead,
                         other, offset + low - start, span)
                    )
    return placed(at, sources, moves, shapes)


def pack_kernel(sides, at_ref, *refs):
    ins, outs = refs[: -len(sides)], refs[-len(sides) :]
    place = 0
    for out, (count, wide, _) in zip(outs, sides, strict=True):
        column = 0
        for k in range(count):
            values = ins[place][...]
            place += 1
            width = values.shape[-1]
            values = values.reshape(out.shape[:-1] + (width,))
            if wide and k == count - 1:
                values = two_words(values)
            out[..., column : column + width] = halved(values)
            column += width


def two_words(values):
    half = values.shape[-1] // 2
    coarse = values.astype(jnp.bfloat16).astype(jnp.float32)
    lane = lax.broadcasted_iota(jnp.int32, values.shape, values.ndim - 1)
    rest = jnp.concatenate([(values - coarse)[..., half:], (values - coarse)[..., :half]], axis=-1)
    return jnp.where(lane < half, coarse, rest)


def one_word(block):
    half = block.shape[-1] // 2
    return block + jnp.concatenate([block[..., half:], block[..., :half]], axis=-1)


def received(block, wide):
    values = block.astype(jnp.float32)
    if not wide:
        return values
    return jnp.concatenate(
        [values[..., :-LANES], one_word(values[..., -LANES:])], axis=-1
    )


def sent(values, wide):
    if not wide:
        return halved(values)
    return jnp.concatenate(
        [halved(values[..., :-LANES]), halved(two_words(values[..., -LANES:]))], axis=-1
    )


def piece_spec(side, piece, flip, other):
    array, rows, row_at, columns, column_at = piece

    def index(z, at):
        place = z ^ (at[0] * (array.shape[0] // 2)) if flip else z
        bit = at[1 + side] ^ (1 if other else 0)
        return (place, 0, bit, row_at, column_at) if side == 0 else (place, bit, 0, row_at, column_at)

    block = (1, 2, 1, rows, columns) if side == 0 else (1, 1, 2, rows, columns)
    return pl.BlockSpec(block, index)


def fold_call(kernel, count, at, ins, in_specs, outs, out_specs):
    size = sum(math.prod(o.shape) for o in outs) * 8
    return pl.pallas_call(
        kernel,
        grid_spec=pltpu.PrefetchScalarGridSpec(
            num_scalar_prefetch=1, grid=(count,), in_specs=in_specs, out_specs=out_specs
        ),
        out_shape=outs,
        compiler_params=pltpu.CompilerParams(vmem_limit_bytes=VMEM),
        cost_estimate=pl.CostEstimate(flops=0, bytes_accessed=size, transcendentals=0),
    )(at, *ins)


class Fold:
    def __init__(self, at, sides, flip=False, wide=False):
        self.at, self.sides, self.flip, self.wide = at, sides, flip, (False, wide)
        self.count = sides[0][0][0].shape[0]
        self.rows = [side[0][1] for side in sides]
        self.columns = [sum(piece[3] for piece in side) for side in sides]

    def first(self):
        ins, in_specs, sides = [], [], []
        for side, pieces in enumerate(self.sides):
            for piece in pieces:
                ins.append(piece[0])
                in_specs.append(piece_spec(side, piece, self.flip, True))
            sides.append((len(pieces), self.wide[side], None))
        outs = [stacked(self.count, 2, r, c, dtype=jnp.bfloat16) for r, c in zip(self.rows, self.columns)]
        out_specs = [pl.BlockSpec((1,) + o.shape[1:], lambda z, at: (z, 0, 0, 0)) for o in outs]
        parts = fold_call(
            functools.partial(pack_kernel, sides), self.count, self.at, ins, in_specs, outs, out_specs
        )
        return [exchanged(part, "batch", 1 << side) for side, part in enumerate(parts)]

    def second_kernel(self, at_ref, *refs):
        place = 0
        outs = refs[-4:]
        for side, pieces in enumerate(self.sides):
            arrays = refs[place : place + len(pieces)]
            arrived = refs[place + len(pieces)]
            place += len(pieces) + 1
            bit = at_ref[2 - side]
            for which, out in ((1 - bit, outs[2 * side]), (bit, outs[2 * side + 1])):
                values = jnp.concatenate(
                    [a[0, which, 0] if side == 0 else a[0, 0, which] for a in arrays], axis=-1
                )
                values = values + received(arrived[0, which], self.wide[side])
                out[0] = sent(values, self.wide[side]) if out.dtype == jnp.bfloat16 else values

    def second(self, arrived):
        ins, in_specs, outs = [], [], []
        for side, pieces in enumerate(self.sides):
            for piece in pieces:
                ins.append(piece[0])
                in_specs.append(piece_spec(side, piece, self.flip, False))
            ins.append(arrived[side])
            in_specs.append(pl.BlockSpec((1,) + arrived[side].shape[1:], lambda z, at: (z, 0, 0, 0)))
            shape = (self.count, self.rows[side], self.columns[side])
            outs += [stacked(*shape, dtype=jnp.bfloat16), stacked(*shape)]
        out_specs = [pl.BlockSpec((1,) + o.shape[1:], lambda z, at: (z, 0, 0)) for o in outs]
        out = fold_call(self.second_kernel, self.count, self.at, ins, in_specs, outs, out_specs)
        return [exchanged(out[0], "batch", 2), exchanged(out[2], "batch", 1)], [out[1], out[3]]

    def third_kernel(self, radix, at_ref, keep0, keep1, in0, in1, *outs):
        mine = at_ref[3] % radix
        for d, out in enumerate(outs):
            which = mine ^ d
            column = 0
            for side, (keep, arrived) in enumerate(((keep0, in0), (keep1, in1))):
                wide = self.wide[side]
                values = keep[which] + received(arrived[which], wide)
                width = values.shape[-1]
                out[0, :, column : column + width] = values if d == 0 else sent(values, wide)
                column += width

    def third(self, arrived, kept):
        radix = min(4, self.count)
        ins = kept + arrived
        in_specs = [pl.BlockSpec((radix,) + a.shape[1:], lambda z, at: (z, 0, 0)) for a in ins]
        shape = (self.count // radix, self.rows[0], sum(self.columns))
        outs = [stacked(*shape)] + [stacked(*shape, dtype=jnp.bfloat16)] * (radix - 1)
        out_specs = [pl.BlockSpec((1,) + o.shape[1:], lambda z, at: (z, 0, 0)) for o in outs]
        out = fold_call(
            functools.partial(self.third_kernel, radix), self.count // radix, self.at, ins, in_specs, outs, out_specs
        )
        terms = [out[0]] + [exchanged(part, "batch", 4 * d) for d, part in enumerate(out) if d > 0]
        total = None
        for term in terms:
            value = received(term, self.wide[1]) if term.dtype == jnp.bfloat16 else term
            total = value if total is None else total + value
        bit = 2 + radix.bit_length() - 1
        while total.shape[0] > 1:
            total = total.reshape((total.shape[0] // 2, 2) + total.shape[1:])
            upper = (lax.axis_index("batch") >> bit) & 1
            away = sent(lax.dynamic_index_in_dim(total, 1 - upper, 1, keepdims=False), False)
            total = lax.dynamic_index_in_dim(total, upper, 1, keepdims=False)
            total = total + exchanged(away, "batch", 1 << bit).astype(jnp.float32)
            bit += 1
        return total[0]


def attend_kernel(at, key_code, query_code, q_ref, k_ref, v_ref, context_ref, prob_ref, bias):
    half = pl.program_id(1)

    @pl.when(pl.program_id(0) == 0)
    def _():
        bias[half] = jnp.where(key_code[...] == query_code[...], 0.0, NEGATIVE)

    rows, lanes = q_ref.shape
    size = lanes // 2
    first = lax.broadcasted_iota(jnp.int32, (rows, lanes), 1) < size
    keys = k_ref[...]
    none = jnp.zeros_like(keys)
    masked = (jnp.where(first, keys, none), jnp.where(first, none, keys))
    values = v_ref[...].T
    queries = q_ref[...] * jnp.bfloat16(1.0 / math.sqrt(size))
    outs = []
    for h in range(2):
        scores = matmul(masked[h], queries, NT) + bias[half]
        weights = jnp.exp(scores - jnp.max(scores, axis=0, keepdims=True))
        probs = halved(weights * (1.0 / jnp.sum(weights, axis=0, keepdims=True)))
        prob_ref[0, 0, h] = probs
        outs.append(matmul(values[h * size : (h + 1) * size], probs))
    context_ref[...] = halved(jnp.concatenate(outs, axis=0).T)


def natural(pairs, i, at):
    return ((i // (pairs // 2)) ^ at[0]) * (pairs // 2) + i % (pairs // 2)


def attend(at, key_code, query_code, triples):
    tokens, wide = triples.shape[1:]
    width = wide // 3 * 2
    rows, pairs = tokens // 2, width // LANES
    own = pairs // 2

    def part(p):
        return pl.BlockSpec((None, rows, LANES), lambda i, j, at: (i // own, j, p * own + i % own))

    return pl.pallas_call(
        attend_kernel,
        grid_spec=pltpu.PrefetchScalarGridSpec(
            num_scalar_prefetch=1,
            grid=(pairs, 2),
            in_specs=[
                pl.BlockSpec((rows, 1), lambda i, j, at: (j, 0)),
                pl.BlockSpec((1, rows), lambda i, j, at: (0, j)),
                part(0),
                part(1),
                part(2),
            ],
            out_specs=[
                pl.BlockSpec((rows, LANES), lambda i, j, at: (j, natural(pairs, i, at))),
                pl.BlockSpec((1, 1, 2, rows, rows), lambda i, j, at: (i, j, 0, 0, 0)),
            ],
            scratch_shapes=[pltpu.VMEM((2, rows, rows), jnp.float32)],
        ),
        out_shape=[
            stacked(tokens, width, dtype=jnp.bfloat16),
            stacked(pairs, 2, 2, rows, rows, dtype=jnp.bfloat16),
        ],
        compiler_params=pltpu.CompilerParams(vmem_limit_bytes=VMEM),
        cost_estimate=pl.CostEstimate(
            flops=16 * pairs * rows * rows * LANES, bytes_accessed=40 << 20, transcendentals=0
        ),
    )(at, key_code, query_code, triples, triples, triples)


def attend_back_kernel(at, q_ref, k_ref, v_ref, context_ref, grad_ref, prob_ref, out_ref, sum_ref):
    rows, lanes = q_ref.shape
    size = lanes // 2
    scale = jnp.bfloat16(1.0 / math.sqrt(size))
    first = lax.broadcasted_iota(jnp.int32, (rows, lanes), 1) < size
    queries = q_ref[...] * scale
    keys = (k_ref[...] * scale).T
    values, grads = v_ref[...], grad_ref[...]
    none = jnp.zeros_like(values)
    masked = (jnp.where(first, values, none), jnp.where(first, none, values))
    products = (grads.astype(jnp.float32) * context_ref[...].astype(jnp.float32)).T
    dquery, dkey, dvalue = [], [], []
    for h in range(2):
        here = slice(h * size, (h + 1) * size)
        rowdot = jnp.sum(products[here], axis=0, keepdims=True)
        probs = prob_ref[0, 0, h]
        dprob = matmul(masked[h], grads, NT)
        dscore = halved(probs.astype(jnp.float32) * (dprob - rowdot))
        dkey.append(matmul(dscore, queries))
        dvalue.append(matmul(probs, grads))
        dquery.append(matmul(keys[here], dscore))
    dquery = jnp.concatenate(dquery, axis=0).T
    dkey = jnp.where(first, dkey[0], dkey[1])
    dvalue = jnp.where(first, dvalue[0], dvalue[1])
    for p, part in enumerate((dquery, dkey, dvalue)):
        out_ref[p] = halved(part)

    @pl.when(pl.program_id(1) == 0)
    def _():
        sum_ref[...] = jnp.zeros_like(sum_ref)

    sum_ref[0] += jnp.sum(dquery, axis=0, keepdims=True)
    sum_ref[1] += jnp.sum(dvalue, axis=0, keepdims=True)


def attend_back(at, triples, context, grad, probs):
    tokens, width = context.shape
    rows, pairs = tokens // 2, width // LANES
    own = pairs // 2

    def part(p):
        return pl.BlockSpec((None, rows, LANES), lambda i, j, at: (i // own, j, p * own + i % own))

    whole = pl.BlockSpec((rows, LANES), lambda i, j, at: (j, natural(pairs, i, at)))
    return pl.pallas_call(
        attend_back_kernel,
        grid_spec=pltpu.PrefetchScalarGridSpec(
            num_scalar_prefetch=1,
            grid=(pairs, 2),
            in_specs=[
                part(0),
                part(1),
                part(2),
                whole,
                whole,
                pl.BlockSpec((1, 1, 2, rows, rows), lambda i, j, at: (i, j, 0, 0, 0)),
            ],
            out_specs=[
                pl.BlockSpec((3, rows, LANES), lambda i, j, at: (0, j, i)),
                pl.BlockSpec((2, 1, LANES), lambda i, j, at: (0, 0, i)),
            ],
        ),
        out_shape=[stacked(3, tokens, width, dtype=jnp.bfloat16), stacked(2, 1, width)],
        compiler_params=pltpu.CompilerParams(vmem_limit_bytes=VMEM),
        cost_estimate=pl.CostEstimate(
            flops=32 * pairs * rows * rows * LANES, bytes_accessed=40 << 20, transcendentals=0
        ),
    )(at, triples, triples, triples, context, grad, probs)


def gelu_value(values):
    return 0.5 * values * (1.0 + lax.erf(values * ROOT_HALF))


def gelu_slope(values):
    return (
        0.5 * (1.0 + lax.erf(values * ROOT_HALF))
        + values * jnp.exp(-0.5 * values * values) / ROOT_TWO_PI
    )


def layout(lengths_row, token_count):
    slot_count = lengths_row.shape[0]
    counted = jnp.sum((lengths_row > 0).astype(jnp.int32))
    bucket = token_count // counted
    places = jnp.arange(token_count, dtype=jnp.int32)
    document = places // bucket
    position = places - document * bucket
    member = document[:, None] == jnp.arange(slot_count, dtype=jnp.int32)[None, :]
    slot_length = jnp.sum(jnp.where(member, lengths_row[None, :], 0), axis=1)
    present = position < slot_length
    return (counted, document, present, member)


def norm_forward(values, gain_row, shift_row):
    center = values - jnp.mean(values, axis=-1, keepdims=True)
    inverse = lax.rsqrt(jnp.mean(center * center, axis=-1, keepdims=True) + EPS_NORM)
    normed = center * inverse
    return (normed * gain_row + shift_row, normed, inverse)


def norm_backward(grad_out, normed, inverse, gain_row):
    scaled = grad_out * gain_row
    inner = (
        scaled
        - jnp.mean(scaled, axis=-1, keepdims=True)
        - normed * jnp.mean(scaled * normed, axis=-1, keepdims=True)
    )
    return (inner * inverse, jnp.sum(grad_out * normed, axis=0), jnp.sum(grad_out, axis=0))


def renew(grad, moment, weight, average, rate):
    moment_new = MOMENTUM * moment + grad
    weight_new = weight - rate * (grad + MOMENTUM * moment_new)
    average_new = AVERAGE * average + (1.0 - AVERAGE) * weight_new
    return (grad, moment_new, weight_new, average_new)


def local(
    tokens,
    lengths,
    attn_weight,
    attn_moment,
    attn_average,
    up_weight,
    up_moment,
    up_average,
    down_weight,
    down_moment,
    down_average,
    layer_vectors,
    vector_moment,
    vector_average,
    up_bias,
    bias_moment,
    bias_average,
    pos_table,
    pos_moment,
    pos_average,
):
    at = position()
    stream = at[0]
    devices = lax.axis_size("batch")
    rows, hidden_half = up_weight.shape
    quarter = attn_weight.shape[2]
    width = 2 * quarter
    pos_half = pos_table.shape[0]
    lengths_row = lengths[0, 0]
    slot_count = lengths_row.shape[0]
    live_row = (lengths_row > 0).astype(jnp.float32)

    misc = jnp.concatenate(
        [
            layer_vectors.T,
            up_bias.reshape(rows, 2),
            jnp.broadcast_to(live_row[None, :], (rows, slot_count)),
        ],
        axis=1,
    )
    misc = jnp.pad(misc, ((0, 0), (0, LANES - misc.shape[1])))
    entry_block = halved(
        jnp.concatenate([attn_weight[0], attn_weight[1], attn_weight[2], pos_table.T, misc], axis=1)
    )
    middle_block = halved(
        jnp.concatenate([up_weight, attn_weight[3], jnp.zeros((rows, LANES), jnp.float32)], axis=1)
    )
    triple = 3 * quarter
    pos_stop = triple + pos_half
    qkv_blocks, pos_blocks, misc_blocks = spread(
        at,
        entry_block,
        width,
        (
            (0, triple, 0, "relative", 0, 0),
            (triple, pos_stop, 1, "", 0, pos_half),
            (pos_stop, pos_stop + LANES, 2, "stream", 0, 0),
        ),
        [
            stacked(2, devices, rows, triple, dtype=jnp.bfloat16),
            stacked(devices, rows, 2 * pos_half, dtype=jnp.bfloat16),
            stacked(2, devices, rows, LANES, dtype=jnp.bfloat16),
        ],
    )
    up_blocks, out_blocks = spread(
        at,
        middle_block,
        (hidden_half + quarter + LANES) // 2,
        (
            (0, hidden_half, 0, "relative", 0, 0),
            (hidden_half, hidden_half + quarter, 1, "", 0, quarter),
        ),
        [
            stacked(2, devices, rows, hidden_half, dtype=jnp.bfloat16),
            stacked(devices, rows, width, dtype=jnp.bfloat16),
        ],
    )
    down_both = lax.all_gather(halved(down_weight), ("stream", "batch"), axis=0, tiled=True)
    qkv = qkv_blocks.reshape(2, width, triple)
    up = up_blocks.reshape(2, width, hidden_half)
    out_full = out_blocks.reshape(width, width)
    pos_full = pos_blocks.reshape(width, 2 * pos_half).T
    misc_full = misc_blocks.reshape(2, width, LANES)
    vectors = jnp.concatenate([misc_full[s, :, :4].T for s in range(2)], axis=0).astype(jnp.float32)
    biases = misc_full[:, :, 4:6].reshape(2, -1).astype(jnp.float32)
    lives = misc_full[:, ::rows, 6 : 6 + slot_count].reshape(2, -1) > 0
    upper = stream == 1

    def own_first(values):
        half = values.shape[-1] // 2
        return jnp.where(upper, jnp.roll(values, half, axis=-1), values)

    inputs = tokens[0].astype(jnp.float32)
    token_count = inputs.shape[0]
    counted, document, present, member = layout(lengths_row, token_count)
    key_code = jnp.where(present, document, -1).astype(jnp.float32)[:, None]
    query_code = document.astype(jnp.float32)[None, :]
    long_rows = token_count // 2
    short_rows = token_count // slot_count
    short_tiled = jnp.tile(pos_full[:short_rows], (long_rows // short_rows, 1))
    pos_rows = jnp.where(counted == 2, pos_full, short_tiled).astype(jnp.float32)
    hidden0 = (inputs.reshape(2, long_rows, width) + pos_rows[None]).reshape(token_count, width)
    entry = halved(hidden0)
    query_bias, value_bias = own_first(vectors[0]), own_first(vectors[1])
    triples = []
    for k in range(2):
        here = slice(k * quarter, (k + 1) * quarter)
        shift = jnp.concatenate(
            [query_bias[here], jnp.zeros((quarter,), jnp.float32), value_bias[here]]
        )
        triples.append(halved(matmul(entry, qkv[k]) + shift))
    triples = jnp.stack(triples)
    context_half, probs = attend(at, key_code, query_code, triples)
    resid1 = hidden0 + matmul(context_half, out_full) + vectors[2]
    hidden1, normed1, inverse1 = norm_forward(resid1, vectors[4], vectors[5])
    entry2 = halved(hidden1)
    biases_own = own_first(biases.reshape(1, -1)).reshape(2, -1)
    pre_act = [matmul(entry2, up[k]) + biases_own[k] for k in range(2)]
    active = [halved(gelu_value(part)) for part in pre_act]
    down_rows = down_both.shape[0] // 4
    down_full = jnp.concatenate(
        [down_both[: 2 * down_rows], down_both[2 * down_rows :]], axis=1
    ).reshape(2, down_rows, width)
    down = [
        lax.dynamic_index_in_dim(down_full, stream ^ k, 0, keepdims=False) for k in range(2)
    ]
    resid2 = hidden1 + (matmul(active[0], down[0]) + matmul(active[1], down[1])) + vectors[3]
    hidden2, normed2, inverse2 = norm_forward(resid2, vectors[6], vectors[7])
    inverse_len = 1.0 / jnp.maximum(lengths_row, 1).astype(jnp.float32)
    pool = jnp.where(member & present[:, None], inverse_len[None, :], 0.0)
    pooled = jnp.dot(pool.T, hidden2, precision=lax.Precision.HIGHEST)
    inverse_norm = lax.rsqrt(jnp.sum(pooled * pooled, axis=-1, keepdims=True) + EPS_NORM)
    unit_half = halved(pooled * inverse_norm)

    batch_index = lax.axis_index("batch")
    pair_total = devices * slot_count
    units = unit_half[None]
    for bit in range(devices.bit_length() - 2, -1, -1):
        other = exchanged(units, "batch", 1 << bit)
        is_high = (batch_index >> bit) & 1 == 1
        low, high = jnp.where(is_high, other, units), jnp.where(is_high, units, other)
        units = jnp.stack([low, high], axis=1).reshape(-1, slot_count, width)
    bits = devices.bit_length() - 1
    units = units.reshape((2,) * bits + (slot_count, width)).reshape(pair_total, width)
    others = exchanged(units, "stream", 1)
    own_live = jnp.where(upper, lives[1], lives[0])
    other_live = jnp.where(upper, lives[0], lives[1])
    own_rows = batch_index * slot_count + jnp.arange(slot_count, dtype=jnp.int32)
    all_rows = jnp.arange(pair_total, dtype=jnp.int32)

    def loss_grad(lines, columns, lines_at, lines_live, columns_live):
        logits = matmul(lines, columns, NT) * INV_TEMP
        logits = jnp.where(columns_live[None, :], logits, NEGATIVE)
        highest = jnp.max(logits, axis=-1, keepdims=True)
        weights = jnp.exp(logits - highest)
        spread_probs = weights / jnp.sum(weights, axis=-1, keepdims=True)
        target = (all_rows[None, :] == lines_at[:, None]).astype(jnp.float32)
        return halved(LOSS_WEIGHT * (spread_probs - target) * lines_live[:, None])

    dlogit_own = loss_grad(unit_half, others, own_rows, live_row, other_live)
    dlogit_all = loss_grad(others, units, all_rows, other_live.astype(jnp.float32), own_live)
    dlogit_in = lax.dynamic_slice_in_dim(dlogit_all, batch_index * slot_count, slot_count, 1)
    dunit = INV_TEMP * (matmul(dlogit_own, others) + matmul(dlogit_in, others, TN))
    along = jnp.sum(pooled * dunit, axis=-1, keepdims=True)
    dpooled = inverse_norm * dunit - inverse_norm * inverse_norm * inverse_norm * pooled * along

    dhidden2 = jnp.dot(pool, dpooled, precision=lax.Precision.HIGHEST)
    dresid2, dgain2, dshift2 = norm_backward(dhidden2, normed2, inverse2, vectors[6])
    dresid2_half = halved(dresid2)

    def columns_of(values, k):
        return lax.dynamic_slice_in_dim(values, (stream ^ k) * quarter, quarter, 1)

    def blocks(values):
        return values.reshape(devices // 4, 2, 2, values.shape[0] // devices, values.shape[1])

    active_all = jnp.concatenate(active, axis=1)
    down_away = halved(matmul(active_all, columns_of(dresid2_half, 1), TN))
    down_away = jnp.roll(down_away, down_rows, axis=0)
    down_in = exchanged(down_away, "stream", 1)
    down_own = matmul(active_all, columns_of(dresid2_half, 0), TN) + down_in.astype(jnp.float32)
    by_rows = down_weight.shape[0] % 32 == 0
    half_rows = down_weight.shape[0] // 2
    down_blocked = blocks(down_own)
    if by_rows:
        down_sides = [[(down_blocked, half_rows, k, quarter, 0)] for k in range(2)]
    else:
        down_sides = [
            [(down_blocked, 2 * half_rows, 0, LANES, k) for k in ks] for ks in ((0, 1), (2,))
        ]
    down_fold = Fold(at, down_sides, flip=True)
    down_first = down_fold.first()

    dpre = [
        matmul(dresid2_half, down[k], NT) * gelu_slope(pre_act[k]) for k in range(2)
    ]
    dpre_half = [halved(part) for part in dpre]
    dpre_half[1], down_first = in_order(dpre_half[1], down_first)
    down_second, down_kept = down_fold.second(down_first)
    up_away = halved(matmul(entry2, dpre_half[1], TN))
    up_in = exchanged(up_away, "stream", 1)
    up_own = matmul(entry2, dpre_half[0], TN) + up_in.astype(jnp.float32)
    dhidden1 = dresid2 + (matmul(dpre_half[0], up[0], NT) + matmul(dpre_half[1], up[1], NT))
    dresid1, dgain1, dshift1 = norm_backward(dhidden1, normed1, inverse1, vectors[4])
    dresid1_half = halved(dresid1)
    dresid1_half, down_second, up_own = in_order(dresid1_half, down_second, up_own)
    down_sum = down_fold.third(down_second, down_kept)
    out_away = halved(matmul(context_half, columns_of(dresid1_half, 1), TN))
    out_in = exchanged(out_away, "stream", 1)
    out_own = matmul(context_half, columns_of(dresid1_half, 0), TN) + out_in.astype(jnp.float32)
    third = hidden_half // 3
    up_blocked, out_blocked = blocks(up_own), blocks(out_own)
    middle_fold = Fold(
        at,
        [
            [(up_blocked, rows, 0, third, 0), (up_blocked, rows, 0, third, 1)],
            [(up_blocked, rows, 0, third, 2), (out_blocked, rows, 0, quarter, 0)],
        ],
    )
    middle_first = middle_fold.first()
    dcontext_half = halved(matmul(dresid1_half, out_full, NT))
    dtriple, dsums = attend_back(at, triples, context_half, dcontext_half, probs)
    dtriple, down_sum, middle_first = in_order(dtriple, down_sum, middle_first)
    middle_second, middle_kept = middle_fold.second(middle_first)
    qkv_away = jnp.concatenate(
        [halved(matmul(entry, dtriple[p, :, quarter:], TN)) for p in range(3)], axis=1
    )
    qkv_in = exchanged(qkv_away, "stream", 1)
    dhidden0 = dresid1
    for k in range(2):
        for p in range(3):
            here = slice(k * quarter, (k + 1) * quarter)
            weight = qkv[k][:, p * quarter : (p + 1) * quarter]
            dhidden0 = dhidden0 + matmul(dtriple[p, :, here], weight, NT)
    qkv_own = jnp.concatenate(
        [matmul(entry, dtriple[p, :, :quarter], TN) for p in range(3)], axis=1
    ) + qkv_in.astype(jnp.float32)
    long_sum = jnp.sum(dhidden0.reshape(2, long_rows, width), axis=0)
    short_sum = jnp.sum(long_sum.reshape(-1, short_rows, width), axis=0)
    short_full = jnp.pad(short_sum, ((0, long_rows - short_rows), (0, 0)))
    pos_columns = jnp.where(counted == 2, long_sum, short_full).T
    vector_columns = jnp.stack(
        [
            own_first(dsums[0, 0]),
            own_first(dsums[1, 0]),
            jnp.sum(dresid1, axis=0),
            jnp.sum(dresid2, axis=0),
            dgain1,
            dshift1,
            dgain2,
            dshift2,
        ],
        axis=1,
    )
    bias_rows = [jnp.sum(part, axis=0).reshape(width, 2) for part in dpre]

    def misc_part(k):
        picked = lax.dynamic_slice_in_dim(vector_columns, (stream ^ k) * 4, 4, 1)
        values = jnp.concatenate([picked, bias_rows[k]], axis=1)
        return jnp.pad(values, ((0, 0), (0, LANES - values.shape[1])))

    def pos_part(k):
        return lax.dynamic_slice_in_dim(pos_columns, (stream ^ k) * pos_half, pos_half, 1)

    misc_away = misc_part(1)
    coarse = lax.reduce_precision(misc_away[:, : LANES // 2], exponent_bits=8, mantissa_bits=7)
    rest = misc_away[:, : LANES // 2] - coarse
    last_in = exchanged(
        halved(jnp.concatenate([pos_part(1), coarse, rest], axis=1)), "stream", 1
    ).astype(jnp.float32)
    pos_own = pos_part(0) + last_in[:, :pos_half]
    misc_own = misc_part(0) + one_word(last_in[:, pos_half:])
    qkv_blocked = blocks(qkv_own)
    entry_fold = Fold(
        at,
        [
            [(qkv_blocked, rows, 0, quarter, 0), (qkv_blocked, rows, 0, quarter, 1)],
            [
                (qkv_blocked, rows, 0, quarter, 2),
                (blocks(pos_own), rows, 0, pos_half, 0),
                (blocks(misc_own), rows, 0, LANES, 0),
            ],
        ],
        wide=True,
    )
    entry_first = entry_fold.first()
    entry_second, entry_kept = entry_fold.second(entry_first)
    middle_sum = middle_fold.third(middle_second, middle_kept)
    entry_sum = entry_fold.third(entry_second, entry_kept)

    down_grad = down_sum
    if by_rows:
        down_grad = jnp.concatenate([down_sum[:, :quarter], down_sum[:, quarter:]], axis=0)
    attn_grad = jnp.stack(
        [entry_sum[:, k * quarter : (k + 1) * quarter] for k in range(3)]
        + [middle_sum[:, hidden_half : hidden_half + quarter]]
    )
    attn_all = renew(attn_grad, attn_moment, attn_weight, attn_average, RATE)
    up_all = renew(middle_sum[:, :hidden_half], up_moment, up_weight, up_average, RATE)
    down_all = renew(down_grad, down_moment, down_weight, down_average, RATE)
    vector_grad = entry_sum[:, pos_stop : pos_stop + 4].T
    vector_all = renew(vector_grad, vector_moment, layer_vectors, vector_average, RATE)
    bias_grad = entry_sum[:, pos_stop + 4 : pos_stop + 6].reshape(-1)
    bias_all = renew(bias_grad, bias_moment, up_bias, bias_average, RATE)
    pos_grad = entry_sum[:, triple:pos_stop].T
    pos_all = renew(pos_grad, pos_moment, pos_table, pos_average, POS_RATE)
    return (
        halved(hidden2)[None],
        dhidden0[None],
        *attn_all,
        *up_all,
        *down_all,
        *vector_all,
        *bias_all,
        *pos_all,
    )


def solution(mesh):
    tokens_at, weight_at = P("stream", "batch", None), P("batch", "stream")
    attn_at, rows_at, bias_at = P(None, "batch", "stream"), P("stream", "batch"), P(("stream", "batch"))
    kinds = (attn_at, weight_at, weight_at, rows_at, bias_at, rows_at)
    in_specs = (tokens_at, tokens_at) + tuple(kind for kind in kinds for _ in range(3))
    out_specs = (tokens_at, tokens_at) + tuple(kind for kind in kinds for _ in range(4))
    return jax.shard_map(local, mesh=mesh, in_specs=in_specs, out_specs=out_specs, check_vma=False)
```

```python
import functools
import math

import jax
import jax.numpy as jnp
from jax import lax
from jax.experimental import pallas as pl
from jax.experimental.pallas import tpu as pltpu
from jax.sharding import PartitionSpec as P

HEADS = 12


EPS_NORM = 1e-06
INV_TEMP = 100.0
LOSS_WEIGHT = 256.0
MOMENTUM = 0.5
AVERAGE = 0.5
RATE = 0.0001
POS_RATE = 0.01
NEGATIVE = -1e30
ROOT_HALF = 0.7071067811865476
ROOT_TWO_PI = 2.5066282746310002
LANES = 128
SLOT_COUNT, LENGTHS = 4, 5
CHUNK, BLOCKS = 256, 3
COST = pl.CostEstimate(flops=1000, bytes_accessed=1000, transcendentals=0)
LONG_COST = pl.CostEstimate(flops=10**12, bytes_accessed=10**9, transcendentals=0)
ANYWHERE = pl.BlockSpec(memory_space=pl.ANY)
NN = (((1,), (0,)), ((), ()))
NT = (((1,), (1,)), ((), ()))
TN = (((0,), (0,)), ((), ()))


def halved(values):
    return values.astype(jnp.bfloat16)


def matmul(left, right, dims=NN):
    return lax.dot_general(left, right, dims, preferred_element_type=jnp.float32)


def stacked(*shape, dtype=jnp.float32):
    return jax.ShapeDtypeStruct(shape, dtype)


def after(value, *earlier):
    return lax.optimization_barrier((value, earlier))[0]


def exchanged(block, axis, mask):
    count = lax.axis_size(axis)
    return lax.ppermute(block, axis, [(place, place ^ mask) for place in range(count)])


def scalars(lengths_row):
    batch = lax.axis_index("batch")
    places = [lax.axis_index("stream"), batch & 1, (batch >> 1) & 1, batch >> 2]
    counted = jnp.sum((lengths_row > 0).astype(jnp.int32))
    return jnp.concatenate([jnp.stack(places + [counted]), lengths_row]).astype(jnp.int32)


class Gather:
    def __init__(self, block, cut):
        self.cut = cut
        self.bits = lax.axis_size("batch").bit_length() - 1
        self.blocks, self.masks = block[None], [0]

    def far(self, *earlier):
        bit = self.bits
        while bit > 2:
            step = min(2, bit - 2)
            bit -= step
            offsets = [d << bit for d in range(1 << step)]
            arrived = [exchanged(self.blocks, "batch", offset) for offset in offsets[1:]]
            own = after(self.blocks, *earlier) if earlier else self.blocks
            self.blocks = jnp.concatenate([own] + arrived, axis=0)
            self.masks = [offset | mask for offset in offsets for mask in self.masks]
        self.sides = [self.blocks[:, :, : self.cut], self.blocks[:, :, self.cut :]]
        self.masks = [self.masks, self.masks]

    def near(self, flips, *earlier):
        for side, flip in enumerate(flips):
            part = self.sides[side]
            own = after(part, *earlier) if earlier else part
            self.sides[side] = jnp.concatenate([own, exchanged(part, "batch", flip)], axis=0)
            self.masks[side] = self.masks[side] + [flip | mask for mask in self.masks[side]]

    def placed(self, at, pieces, shapes):
        sources, moves = [], []
        for other in range(2):
            for side, part in enumerate(self.sides):
                sources.append(exchanged(part, "stream", 1) if other else part)
                base = self.cut * side
                for start, stop, target, lead, offset, span in pieces:
                    low, high = max(start, base), min(stop, base + part.shape[2])
                    if low >= high:
                        continue
                    for entry, mask in enumerate(self.masks[side]):
                        moves.append(
                            (len(sources) - 1, entry, mask, (low - base, high - base), target, lead,
                             other, offset + low - start, span)
                        )
        return placed(at, sources, moves, shapes)


def place_kernel(moves, count, at_ref, *refs):
    sources, targets = refs[:count], refs[count:]
    stream = at_ref[0]
    batch = at_ref[1] + 2 * at_ref[2] + 4 * at_ref[3]
    for source, entry, mask, columns, target, lead, other, start, span in moves:
        core = stream ^ other
        low = pl.multiple_of(start + core * span, LANES) if span else start
        at = (batch ^ mask, slice(None), pl.ds(low, columns[1] - columns[0]))
        if lead == "relative":
            at = (other,) + at
        elif lead == "stream":
            at = (core,) + at
        targets[target][at] = sources[source][entry, :, columns[0] : columns[1]]


def placed(at, sources, moves, shapes):
    held = pl.BlockSpec(memory_space=pltpu.VMEM)
    return pl.pallas_call(
        functools.partial(place_kernel, moves, len(sources)),
        in_specs=[pl.BlockSpec(memory_space=pltpu.SMEM)] + [held] * len(sources),
        out_specs=[held] * len(shapes),
        out_shape=shapes,
        compiler_params=pltpu.CompilerParams(vmem_limit_bytes=20 << 20),
        cost_estimate=COST,
    )(at, *sources)


def two_words(values):
    half = values.shape[-1] // 2
    coarse = values.astype(jnp.bfloat16).astype(jnp.float32)
    lane = lax.broadcasted_iota(jnp.int32, values.shape, values.ndim - 1)
    rest = jnp.concatenate([(values - coarse)[..., half:], (values - coarse)[..., :half]], axis=-1)
    return jnp.where(lane < half, coarse, rest)


def one_word(block):
    half = block.shape[-1] // 2
    return block + jnp.concatenate([block[..., half:], block[..., :half]], axis=-1)


def received(block, wide):
    values = block.astype(jnp.float32)
    if not wide:
        return values
    return jnp.concatenate(
        [values[..., :-LANES], one_word(values[..., -LANES:])], axis=-1
    )


def sent(values, wide):
    if not wide:
        return halved(values)
    return jnp.concatenate(
        [halved(values[..., :-LANES]), halved(two_words(values[..., -LANES:]))], axis=-1
    )


def piece_specs(side, piece, away):
    array, arrived, rows, row_at, columns, column_at, flip = piece

    def spec(column, turn):
        def index(z, at):
            place = z ^ (turn(at[0]) * (array.shape[0] // 2)) if flip else z
            bit = at[1 + side] ^ (1 if away else 0)
            return (place, 0, bit, row_at, column) if side == 0 else (place, bit, 0, row_at, column)

        return pl.BlockSpec((1, 2, 1, rows, columns) if side == 0 else (1, 1, 2, rows, columns), index)

    return [spec(column_at, lambda core: core), spec(column_at, lambda core: 1 - core)]


def fold_call(kernel, count, at, ins, in_specs, outs, out_specs):
    size = sum(math.prod(o.shape) for o in outs) * 8
    return pl.pallas_call(
        kernel,
        grid_spec=pltpu.PrefetchScalarGridSpec(
            num_scalar_prefetch=1, grid=(count,), in_specs=in_specs, out_specs=out_specs
        ),
        out_shape=outs,
        compiler_params=pltpu.CompilerParams(vmem_limit_bytes=16 << 20),
        cost_estimate=COST,
    )(at, *ins)


class Fold:
    def __init__(self, at, sides, wide=False):
        self.at, self.sides, self.wide = at, sides, (False, wide)
        self.count = sides[0][0][0].shape[0]
        self.rows = [side[0][2] for side in sides]
        self.columns = [sum(piece[4] for piece in side) for side in sides]

    def piece_values(self, refs, side, pick):
        columns = []
        for k in range(len(self.sides[side])):
            wide = self.wide[side] and k == len(self.sides[side]) - 1
            arrived = pick(refs[2 * k + 1]).astype(jnp.float32)
            columns.append(pick(refs[2 * k]) + (one_word(arrived) if wide else arrived))
        return jnp.concatenate(columns, axis=-1)

    def first_kernel(self, at_ref, *refs):
        place = 0
        for side, pieces in enumerate(self.sides):
            out = refs[side - 2]
            for which in range(2):
                values = self.piece_values(
                    refs[place:], side, lambda r: r[0, which, 0] if side == 0 else r[0, 0, which]
                )
                out[0, which] = sent(values, self.wide[side])
            place += 2 * len(pieces)

    def first(self):
        ins, in_specs = [], []
        for side, pieces in enumerate(self.sides):
            for piece in pieces:
                ins += piece[:2]
                in_specs += piece_specs(side, piece, True)
        outs = [stacked(self.count, 2, r, c, dtype=jnp.bfloat16) for r, c in zip(self.rows, self.columns)]
        out_specs = [pl.BlockSpec((1,) + o.shape[1:], lambda z, at: (z, 0, 0, 0)) for o in outs]
        return fold_call(self.first_kernel, self.count, self.at, ins, in_specs, outs, out_specs)

    def first_sent(self, parts):
        return [exchanged(part, "batch", 1 << side) for side, part in enumerate(parts)]

    def second_kernel(self, at_ref, *refs):
        place = 0
        outs = refs[-4:]
        for side, pieces in enumerate(self.sides):
            arrays = refs[place : place + 2 * len(pieces)]
            arrived = refs[place + 2 * len(pieces)]
            place += 2 * len(pieces) + 1
            bit = at_ref[2 - side]
            for which, out in ((1 - bit, outs[2 * side]), (bit, outs[2 * side + 1])):
                values = self.piece_values(
                    arrays, side, lambda r: r[0, which, 0] if side == 0 else r[0, 0, which]
                )
                values = values + received(arrived[0, which], self.wide[side])
                out[0] = sent(values, self.wide[side]) if out.dtype == jnp.bfloat16 else values

    def second(self, arrived):
        ins, in_specs, outs = [], [], []
        for side, pieces in enumerate(self.sides):
            for piece in pieces:
                ins += piece[:2]
                in_specs += piece_specs(side, piece, False)
            ins.append(arrived[side])
            in_specs.append(pl.BlockSpec((1,) + arrived[side].shape[1:], lambda z, at: (z, 0, 0, 0)))
            shape = (self.count, self.rows[side], self.columns[side])
            outs += [stacked(*shape, dtype=jnp.bfloat16), stacked(*shape)]
        out_specs = [pl.BlockSpec((1,) + o.shape[1:], lambda z, at: (z, 0, 0)) for o in outs]
        return fold_call(self.second_kernel, self.count, self.at, ins, in_specs, outs, out_specs)

    def second_sent(self, out):
        return [exchanged(out[0], "batch", 2), exchanged(out[2], "batch", 1)], [out[1], out[3]]

    def third_kernel(self, radix, at_ref, keep0, keep1, in0, in1, *outs):
        mine = at_ref[3] % radix
        for d, out in enumerate(outs):
            which = mine ^ d
            column = 0
            for side, (keep, arrived) in enumerate(((keep0, in0), (keep1, in1))):
                wide = self.wide[side]
                values = keep[which] + received(arrived[which], wide)
                width = values.shape[-1]
                out[0, :, column : column + width] = values if d == 0 else sent(values, wide)
                column += width

    def third(self, arrived, kept):
        radix = min(4, self.count)
        ins = kept + arrived
        in_specs = [pl.BlockSpec((radix,) + a.shape[1:], lambda z, at: (z, 0, 0)) for a in ins]
        shape = (self.count // radix, self.rows[0], sum(self.columns))
        outs = [stacked(*shape)] + [stacked(*shape, dtype=jnp.bfloat16)] * (radix - 1)
        out_specs = [pl.BlockSpec((1,) + o.shape[1:], lambda z, at: (z, 0, 0)) for o in outs]
        return fold_call(
            functools.partial(self.third_kernel, radix), self.count // radix, self.at, ins, in_specs, outs, out_specs
        )

    def third_sent(self, out):
        radix = min(4, self.count)
        terms = [out[0]] + [exchanged(part, "batch", 4 * d) for d, part in enumerate(out) if d > 0]
        total = None
        for term in terms:
            value = received(term, self.wide[1]) if term.dtype == jnp.bfloat16 else term
            total = value if total is None else total + value
        bit = 2 + radix.bit_length() - 1
        while total.shape[0] > 1:
            total = total.reshape((total.shape[0] // 2, 2) + total.shape[1:])
            upper = (lax.axis_index("batch") >> bit) & 1
            away = sent(lax.dynamic_index_in_dim(total, 1 - upper, 1, keepdims=False), False)
            total = lax.dynamic_index_in_dim(total, upper, 1, keepdims=False)
            total = total + exchanged(away, "batch", 1 << bit).astype(jnp.float32)
            bit += 1
        return total[0]


def attend_kernel(at, q_ref, k_ref, v_ref, context_ref, turned_ref, prob_ref, bias):
    half = pl.program_id(1)

    @pl.when(pl.program_id(0) == 0)
    def _():
        span = q_ref.shape[0]
        key = lax.broadcasted_iota(jnp.int32, (span, 1), 0) + half * span
        query = lax.broadcasted_iota(jnp.int32, (1, span), 1) + half * span
        bits = (2 * span).bit_length() - 1
        key_slot = (key * at[SLOT_COUNT]) >> bits
        query_slot = (query * at[SLOT_COUNT]) >> bits
        length = jnp.zeros((span, 1), jnp.int32)
        for slot in range(at.shape[0] - LENGTHS):
            length += jnp.where(key_slot == slot, at[LENGTHS + slot], 0)
        present = key - key_slot * bucket_of(at, 2 * span) < length
        code = jnp.where(present, key_slot, -1)
        bias[half] = jnp.where(code == query_slot, 0.0, NEGATIVE)

    rows, lanes = q_ref.shape
    size = lanes // 2
    first = lax.broadcasted_iota(jnp.int32, (rows, lanes), 1) < size
    keys = k_ref[...]
    none = jnp.zeros_like(keys)
    masked = (jnp.where(first, keys, none), jnp.where(first, none, keys))
    values = v_ref[...].T
    queries = q_ref[...] * jnp.bfloat16(1.0 / math.sqrt(size))
    outs = []
    for h in range(2):
        scores = matmul(masked[h], queries, NT) + bias[half]
        weights = jnp.exp(scores - jnp.max(scores, axis=0, keepdims=True))
        probs = halved(weights * (1.0 / jnp.sum(weights, axis=0, keepdims=True)))
        prob_ref[0, 0, h] = probs
        outs.append(matmul(values[h * size : (h + 1) * size], probs))
    context = jnp.concatenate(outs, axis=0)
    turned_ref[...] = halved(context)
    context_ref[...] = halved(context.T)


def natural(pairs, i, at):
    return ((i // (pairs // 2)) ^ at[0]) * (pairs // 2) + i % (pairs // 2)


def attend(at, triples):
    tokens, wide = triples.shape[1:]
    width = wide // 3 * 2
    rows, pairs = tokens // 2, width // LANES
    own = pairs // 2

    def part(p):
        return pl.BlockSpec((None, rows, LANES), lambda i, j, at: (i // own, j, p * own + i % own))

    return pl.pallas_call(
        attend_kernel,
        grid_spec=pltpu.PrefetchScalarGridSpec(
            num_scalar_prefetch=1,
            grid=(pairs, 2),
            in_specs=[
                part(0),
                part(1),
                part(2),
            ],
            out_specs=[
                pl.BlockSpec((rows, LANES), lambda i, j, at: (j, natural(pairs, i, at))),
                pl.BlockSpec((LANES, rows), lambda i, j, at: (natural(pairs, i, at), j)),
                pl.BlockSpec((1, 1, 2, rows, rows), lambda i, j, at: (i, j, 0, 0, 0)),
            ],
            scratch_shapes=[pltpu.VMEM((2, rows, rows), jnp.float32)],
        ),
        out_shape=[
            stacked(tokens, width, dtype=jnp.bfloat16),
            stacked(width, tokens, dtype=jnp.bfloat16),
            stacked(pairs, 2, 2, rows, rows, dtype=jnp.bfloat16),
        ],
        compiler_params=pltpu.CompilerParams(vmem_limit_bytes=56 << 20),
        cost_estimate=COST,
    )(at, triples, triples, triples)


def attend_back_kernel(at, q_ref, k_ref, v_ref, context_ref, grad_ref, prob_ref, out_ref, sum_ref):
    rows, lanes = q_ref.shape
    size = lanes // 2
    scale = jnp.bfloat16(1.0 / math.sqrt(size))
    first = lax.broadcasted_iota(jnp.int32, (rows, lanes), 1) < size
    queries = q_ref[...] * scale
    keys = (k_ref[...] * scale).T
    values, grads = v_ref[...], grad_ref[...]
    none = jnp.zeros_like(values)
    masked = (jnp.where(first, values, none), jnp.where(first, none, values))
    products = (grads.astype(jnp.float32) * context_ref[...].astype(jnp.float32)).T
    dquery, dkey, dvalue = [], [], []
    for h in range(2):
        here = slice(h * size, (h + 1) * size)
        rowdot = jnp.sum(products[here], axis=0, keepdims=True)
        probs = prob_ref[0, 0, h]
        dprob = matmul(masked[h], grads, NT)
        dscore = halved(probs.astype(jnp.float32) * (dprob - rowdot))
        dkey.append(matmul(dscore, queries))
        dvalue.append(matmul(probs, grads))
        dquery.append(matmul(keys[here], dscore))
    dquery = jnp.concatenate(dquery, axis=0).T
    dkey = jnp.where(first, dkey[0], dkey[1])
    dvalue = jnp.where(first, dvalue[0], dvalue[1])
    pair = pl.program_id(2)
    quarter = out_ref.shape[2] // 3
    low = pl.multiple_of(pair * lanes, lanes)
    for p, part in enumerate((dquery, dkey, dvalue)):
        out_ref[0, :, pl.ds(p * quarter + low, lanes)] = halved(part)

    @pl.when((pl.program_id(1) == 0) & (pair == 0))
    def _():
        sum_ref[...] = jnp.zeros_like(sum_ref)

    sum_ref[0, 0, :, pl.ds(low, lanes)] += jnp.sum(dquery, axis=0, keepdims=True)
    sum_ref[0, 1, :, pl.ds(low, lanes)] += jnp.sum(dvalue, axis=0, keepdims=True)


def attend_back(at, triples, context, grad, probs):
    tokens, width = context.shape
    rows, pairs = tokens // 2, width // LANES
    own = pairs // 2

    def part(p):
        return pl.BlockSpec((None, rows, LANES), lambda r, j, i, at: (r, j, p * own + i))

    whole = pl.BlockSpec((rows, LANES), lambda r, j, i, at: (j, natural(pairs, r * own + i, at)))
    return pl.pallas_call(
        attend_back_kernel,
        grid_spec=pltpu.PrefetchScalarGridSpec(
            num_scalar_prefetch=1,
            grid=(2, 2, own),
            in_specs=[
                part(0),
                part(1),
                part(2),
                whole,
                whole,
                pl.BlockSpec((1, 1, 2, rows, rows), lambda r, j, i, at: (r * own + i, j, 0, 0, 0)),
            ],
            out_specs=[
                pl.BlockSpec((1, rows, triples.shape[2]), lambda r, j, i, at: (r, j, 0)),
                pl.BlockSpec((1, 2, 1, width // 2), lambda r, j, i, at: (r, 0, 0, 0)),
            ],
        ),
        out_shape=[stacked(*triples.shape, dtype=jnp.bfloat16), stacked(2, 2, 1, width // 2)],
        compiler_params=pltpu.CompilerParams(vmem_limit_bytes=56 << 20),
        cost_estimate=LONG_COST,
    )(at, triples, triples, triples, context, grad, probs)


def bucket_of(at, token_count):
    return jnp.where(at[SLOT_COUNT] == 2, token_count // 2, token_count // (at.shape[0] - LENGTHS))


def group_slot(at, group, token_count):
    slots = at.shape[0] - LENGTHS
    span = token_count // slots
    slot = (group * at[SLOT_COUNT]) // slots
    place = lax.broadcasted_iota(jnp.int32, (span, 1), 0) + group * span
    live = place - slot * bucket_of(at, token_count) < at[LENGTHS + slot]
    return slot, live.astype(jnp.float32)


def whole_block(array):
    return pl.BlockSpec(array.shape, lambda *_: (0,) * len(array.shape))


def kernel_call(kernel, grid, at, ins, in_specs, outs, out_specs, scratch=(), long=False, vmem=56):
    return pl.pallas_call(
        kernel,
        grid_spec=pltpu.PrefetchScalarGridSpec(
            num_scalar_prefetch=1, grid=grid, in_specs=in_specs, out_specs=out_specs,
            scratch_shapes=scratch,
        ),
        out_shape=outs,
        compiler_params=pltpu.CompilerParams(vmem_limit_bytes=vmem << 20),
        cost_estimate=LONG_COST if long else COST,
    )(at, *ins)


def entry_kernel(at, tokens, pos, weight, shift, hidden0, entry, triples, table):
    step = pl.program_id(0)
    rows = tokens.shape[0]

    @pl.when(step == 0)
    def _():
        long = pos[...].astype(jnp.float32).T
        count = long.shape[0]
        span = 2 * count // (at.shape[0] - LENGTHS)
        short = jnp.concatenate([long[:span]] * (count // span), axis=0)
        table[...] = jnp.where(at[SLOT_COUNT] == 2, long, short)

    half_steps = pl.num_programs(0) // 2
    here = pl.ds(pl.multiple_of((step % half_steps) * rows, rows), rows)
    values = tokens[...].astype(jnp.float32) + table[here]
    hidden0[...] = values
    values = halved(values)
    entry[...] = values.T
    for other in range(2):
        triples[other] = halved(matmul(values, weight[other]) + shift[other])


def entered(at, tokens, pos, qkv, shift):
    token_count, width = tokens.shape
    triple = qkv.shape[2]
    outs = [
        stacked(token_count, width),
        stacked(width, token_count, dtype=jnp.bfloat16),
        stacked(2, token_count, triple, dtype=jnp.bfloat16),
    ]
    return kernel_call(
        entry_kernel,
        (token_count // CHUNK,),
        at,
        [tokens, pos, qkv, shift],
        tiles(tokens) + [held(pos), held(qkv), held(shift)],
        outs,
        tiles(outs[0], outs[1]) + [pl.BlockSpec((2, CHUNK, triple), lambda i, at: (0, i, 0))],
        [pltpu.VMEM((token_count // 2, width), jnp.float32)],
    )


BO, B2, G1, E1, G2, E2 = 2, 3, 4, 5, 6, 7


def normal(values):
    center = values - jnp.mean(values, axis=-1, keepdims=True)
    inverse = lax.rsqrt(jnp.mean(center * center, axis=-1, keepdims=True) + EPS_NORM)
    return center * inverse, inverse


def held(array):
    return pl.BlockSpec(
        array.shape, lambda *_: (0,) * len(array.shape), pipeline_mode=pl.Buffered(buffer_count=1)
    )


def tiles(*arrays):
    return [
        pl.BlockSpec((CHUNK, a.shape[1]), lambda i, at: (i, 0))
        if a.shape[0] == arrays[0].shape[0]
        else pl.BlockSpec((a.shape[0], CHUNK), lambda i, at: (0, i))
        for a in arrays
    ]


def weight_copies(at, up, down, up_held, down_held, sems):
    half, quarter = down.shape[1] // 2, down.shape[2]
    copies = [pltpu.make_async_copy(up, up_held, sems.at[0])]
    for other in range(2):
        start = pl.multiple_of((other ^ at[0]) * half, half)
        for k in range(2):
            copies.append(
                pltpu.make_async_copy(
                    down.at[k, pl.ds(start, half)],
                    down_held.at[pl.ds(other * half, half), pl.ds(k * quarter, quarter)],
                    sems.at[1 + 2 * other + k],
                )
            )
    return copies[:1], copies[1:]


def weight_scratch(up, down):
    return [
        pltpu.VMEM(up.shape, jnp.bfloat16),
        pltpu.VMEM((down.shape[1], 2 * down.shape[2]), jnp.bfloat16),
        pltpu.SemaphoreType.DMA((5,)),
    ]


def at_first(copies, act):
    @pl.when(pl.program_id(0) == 0)
    def _():
        for copy in copies:
            act(copy)


def forward_kernel(
    at, hidden0, context, out_weight, vectors, up, up_bias, down,
    entry2, normed1, inverse1, active, slope, normed2, inverse2, block_out, pooled, units,
    up_held, down_held, sems, acts,
):
    step = pl.program_id(0)
    up_copies, down_copies = weight_copies(at, up, down, up_held, down_held, sems)
    at_first(up_copies + down_copies, lambda copy: copy.start())
    rows, width = hidden0.shape
    token_count = rows * pl.num_programs(0)
    resid = hidden0[...] + matmul(context[...], out_weight[...]) + vectors[BO : BO + 1]
    normed, inverse = normal(resid)
    hidden1 = normed * vectors[G1 : G1 + 1] + vectors[E1 : E1 + 1]
    normed1[...], inverse1[...] = halved(normed), inverse
    entry = halved(hidden1)
    entry2[...] = entry.T
    at_first(up_copies, lambda copy: copy.wait())
    half = up.shape[2]
    span = half // BLOCKS
    for other in range(2):
        for block in range(BLOCKS):
            here = slice(block * span, (block + 1) * span)
            there = slice(other * half + block * span, other * half + (block + 1) * span)
            values = matmul(entry, up_held[other, :, here]) + up_bias[other, :, here]
            cumulative = 0.5 + 0.5 * lax.erf(values * ROOT_HALF)
            acted = halved(values * cumulative)
            acts[:, there] = acted
            active[there] = acted.T
            density = jnp.exp(-0.5 * values * values) * (1.0 / ROOT_TWO_PI)
            slope[:, there] = halved(cumulative + values * density)
    at_first(down_copies, lambda copy: copy.wait())
    total = hidden1 + vectors[B2 : B2 + 1] + matmul(acts[...], down_held[...])
    normed, inverse = normal(total)
    hidden2 = normed * vectors[G2 : G2 + 1] + vectors[E2 : E2 + 1]
    normed2[...], inverse2[...] = halved(normed), inverse
    block_out[...] = halved(hidden2)

    @pl.when(step == 0)
    def _():
        pooled[...] = jnp.zeros_like(pooled)

    slots = pooled.shape[0]
    span = token_count // slots
    for group in range(rows // span):
        slot, live = group_slot(at, step * (rows // span) + group, token_count)
        part = hidden2[group * span : (group + 1) * span] * live
        pooled[pl.ds(slot, 1)] += jnp.sum(part, axis=0, keepdims=True)

    @pl.when(step == pl.num_programs(0) - 1)
    def _():
        row = lax.broadcasted_iota(jnp.int32, (slots, LANES), 0)
        length = jnp.zeros((slots, LANES), jnp.int32)
        for slot in range(slots):
            length += jnp.where(row == slot, at[LENGTHS + slot], 0)
        mean = pooled[...] * (1.0 / jnp.maximum(length[:, :1], 1).astype(jnp.float32))
        pooled[...] = mean
        squares = jnp.sum(mean * mean, axis=-1, keepdims=True)
        units[:, :width] = halved(mean * lax.rsqrt(squares + EPS_NORM))
        first = lax.broadcasted_iota(jnp.int32, (slots, LANES), 1) == 0
        units[:, width:] = halved(jnp.where(first & (length > 0), 1.0, 0.0))


def forward(at, hidden0, context, out_weight, vectors, up, up_bias, down):
    token_count, width = hidden0.shape
    slots = at.shape[0] - LENGTHS
    hidden = 2 * up.shape[2]
    half = functools.partial(stacked, dtype=jnp.bfloat16)
    outs = [
        half(width, token_count),
        half(token_count, width),
        stacked(token_count, 1),
        half(hidden, token_count),
        half(token_count, hidden),
        half(token_count, width),
        stacked(token_count, 1),
        half(token_count, width),
        stacked(slots, width),
        half(slots, width + LANES),
    ]
    return kernel_call(
        forward_kernel,
        (token_count // CHUNK,),
        at,
        [hidden0, context, out_weight, vectors, up, up_bias, down],
        tiles(hidden0, context)
        + [held(out_weight), held(vectors), ANYWHERE, held(up_bias), ANYWHERE],
        outs,
        tiles(hidden0, *outs[:8])[1:] + [whole_block(out) for out in outs[8:]],
        weight_scratch(up, down) + [pltpu.VMEM((CHUNK, hidden), jnp.bfloat16)],
        vmem=56,
    )


def norm_back(grad, normed, inverse, gain):
    scaled = grad * gain
    inner = (
        scaled
        - jnp.mean(scaled, axis=-1, keepdims=True)
        - normed * jnp.mean(scaled * normed, axis=-1, keepdims=True)
    )
    return inner * inverse


def loss_kernel(
    at, units, others, pooled, normed2, inverse2, vectors,
    dresid, dresid_half, sums, dpool,
):
    slots, width = pooled.shape
    count = units.shape[0]
    step = pl.program_id(0)

    @pl.when(step == 0)
    def _():
        own, own_flags = units[:, :width], units[:, width:]
        other, other_flags = others[:, :width], others[:, width:]
        lane = lax.broadcasted_iota(jnp.int32, (slots, LANES), 1)
        one_hot = halved(jnp.where(lane == 0, 1.0, 0.0))
        own_row = matmul(one_hot, own_flags, NT)[:1] > 0
        other_row = matmul(one_hot, other_flags, NT)[:1] > 0

        def shares(lines, columns, live):
            logits = matmul(lines, columns, NT) * INV_TEMP
            logits = jnp.where(live, logits, NEGATIVE)
            weights = jnp.exp(logits - jnp.max(logits, axis=-1, keepdims=True))
            return weights / jnp.sum(weights, axis=-1, keepdims=True)

        row = lax.broadcasted_iota(jnp.int32, (slots, count), 0)
        column = lax.broadcasted_iota(jnp.int32, (slots, count), 1)
        target = jnp.where(row == column, 1.0, 0.0)
        row_live = own_flags[:slots, :1].astype(jnp.float32)
        dlogit = halved(LOSS_WEIGHT * (shares(own[:slots], other, other_row) - target) * row_live)
        near = shares(other, own, own_row)[:, :LANES]
        row = lax.broadcasted_iota(jnp.int32, (count, LANES), 0)
        column = lax.broadcasted_iota(jnp.int32, (count, LANES), 1)
        target = jnp.where(row == column, 1.0, 0.0)
        other_live = other_flags[:, :1].astype(jnp.float32)
        dnear = LOSS_WEIGHT * (near - target) * other_live
        dnear = halved(jnp.where(column < slots, dnear, 0.0))
        dunit = INV_TEMP * (matmul(dlogit, other) + matmul(dnear, other, TN)[:slots])
        mean = pooled[...]
        inverse = lax.rsqrt(jnp.sum(mean * mean, axis=-1, keepdims=True) + EPS_NORM)
        along = jnp.sum(mean * dunit, axis=-1, keepdims=True)
        grad = inverse * dunit - inverse * inverse * inverse * mean * along
        slot_row = lax.broadcasted_iota(jnp.int32, (slots, 1), 0)
        length = jnp.zeros((slots, 1), jnp.int32)
        for slot in range(slots):
            length += jnp.where(slot_row == slot, at[LENGTHS + slot], 0)
        dpool[...] = grad * (1.0 / jnp.maximum(length, 1).astype(jnp.float32))
        sums[...] = jnp.zeros_like(sums)

    gain = vectors[G2 : G2 + 1]
    token_count = normed2.shape[0] * pl.num_programs(0)
    span = token_count // slots
    groups = normed2.shape[0] // span
    for group in range(groups):
        here = pl.ds(group * span, span)
        slot, live = group_slot(at, step * groups + group, token_count)
        dhidden = dpool[pl.ds(slot, 1)] * live
        normed = normed2[here].astype(jnp.float32)
        values = norm_back(dhidden, normed, inverse2[here], gain)
        dresid[here] = values
        dresid_half[here] = halved(values)
        for k, terms in enumerate((values, dhidden * normed, dhidden)):
            sums[k : k + 1] += jnp.sum(terms, axis=0, keepdims=True)


def loss_back(at, units, others, pooled, normed2, inverse2, vectors):
    token_count, width = normed2.shape
    half = functools.partial(stacked, dtype=jnp.bfloat16)
    ins = [units, others, pooled, normed2, inverse2, vectors]
    outs = [
        stacked(token_count, width),
        half(token_count, width),
        stacked(3, width),
    ]
    return kernel_call(
        loss_kernel,
        (token_count // CHUNK,),
        at,
        ins,
        [held(a) for a in ins[:3]] + tiles(*ins[3:5]) + [held(vectors)],
        outs,
        tiles(*outs[:2]) + [whole_block(outs[2])],
        [pltpu.VMEM(pooled.shape, jnp.float32)],
    )


def backward_kernel(
    at, dresid2, dresid2_half, slope, up, down, normed1, inverse1, vectors,
    dpre, dpre_sum, dresid, dresid_half, sums,
    up_held, down_held, sems,
):
    up_copies, down_copies = weight_copies(at, up, down, up_held, down_held, sems)
    at_first(down_copies + up_copies, lambda copy: copy.start())

    @pl.when(pl.program_id(0) == 0)
    def _():
        dpre_sum[...] = jnp.zeros_like(dpre_sum)
        sums[...] = jnp.zeros_like(sums)

    at_first(down_copies, lambda copy: copy.wait())
    half = up.shape[2]
    span = half // BLOCKS
    grad = dresid2_half[...]
    for block in range(2 * BLOCKS):
        here = slice(block * span, (block + 1) * span)
        dactive = matmul(grad, down_held[here], NT)
        values = dactive * slope[:, here].astype(jnp.float32)
        dpre_sum[:, here] += jnp.sum(values, axis=0, keepdims=True)
        dpre[:, here] = halved(values)
    at_first(up_copies, lambda copy: copy.wait())
    dhidden = dresid2[...]
    for other in range(2):
        dhidden += matmul(dpre[:, other * half : (other + 1) * half], up_held[other], NT)
    normed = normed1[...].astype(jnp.float32)
    values = norm_back(dhidden, normed, inverse1[...], vectors[G1 : G1 + 1])
    dresid[...] = values
    rounded = halved(values)
    dresid_half[...] = rounded
    for k, terms in enumerate((values, dhidden * normed, dhidden)):
        sums[k : k + 1] += jnp.sum(terms, axis=0, keepdims=True)


def backward(at, dresid2, dresid2_half, slope, up, down, normed1, inverse1, vectors):
    token_count, width = dresid2.shape
    hidden = 2 * up.shape[2]
    half = functools.partial(stacked, dtype=jnp.bfloat16)
    outs = [
        half(token_count, hidden),
        stacked(1, hidden),
        stacked(token_count, width),
        half(token_count, width),
        stacked(3, width),
    ]
    out_specs = tiles(outs[0], *outs[2:4])
    return kernel_call(
        backward_kernel,
        (token_count // CHUNK,),
        at,
        [dresid2, dresid2_half, slope, up, down, normed1, inverse1, vectors],
        tiles(dresid2, dresid2_half, slope) + [ANYWHERE, ANYWHERE] + tiles(normed1, inverse1)
        + [held(vectors)],
        outs,
        out_specs[:1] + [whole_block(outs[1])] + out_specs[1:] + [whole_block(outs[4])],
        weight_scratch(up, down),
        vmem=56,
        long=True,
    )


def leave_kernel(at, dresid1, dtriples, qkv, lines, input_grad, last_own, last_away, total):
    step = pl.program_id(0)
    rows = dresid1.shape[0]
    values = dresid1[...]
    for other in range(2):
        values = values + matmul(dtriples[other], qkv[other], NT)
    input_grad[...] = values
    half_steps = pl.num_programs(0) // 2
    here = pl.ds(pl.multiple_of((step % half_steps) * rows, rows), rows)

    @pl.when(step < half_steps)
    def _():
        total[here] = values

    @pl.when(step >= half_steps)
    def _():
        total[here] += values

    @pl.when(step == pl.num_programs(0) - 1)
    def _():
        count = total.shape[0]
        long = total[...]
        span = 2 * count // (at.shape[0] - LENGTHS)
        short = sum(long[k * span : (k + 1) * span] for k in range(count // span))
        short = jnp.concatenate([short, jnp.zeros((count - span, long.shape[1]), jnp.float32)], axis=0)
        columns = jnp.where(at[SLOT_COUNT] == 2, long, short).T
        left, right = columns[:, : count // 2], columns[:, count // 2 :]
        last_own[:, : count // 2] = jnp.where(at[0] == 0, left, right)
        last_away[:, : count // 2] = halved(jnp.where(at[0] == 0, right, left))
        last_own[:, count // 2 :] = lines[0].T
        last_away[:, count // 2 :] = halved(two_words(lines[1].T))


def left(at, dresid1, dtriples, qkv, lines):
    token_count, width = dresid1.shape
    triple = qkv.shape[2]
    columns = token_count // 4 + LANES
    outs = [
        stacked(token_count, width),
        stacked(width, columns),
        stacked(width, columns, dtype=jnp.bfloat16),
    ]
    return kernel_call(
        leave_kernel,
        (token_count // CHUNK,),
        at,
        [dresid1, dtriples, qkv, lines],
        tiles(dresid1)
        + [pl.BlockSpec((2, CHUNK, triple), lambda i, at: (0, i, 0)), held(qkv), held(lines)],
        outs,
        tiles(outs[0]) + [whole_block(out) for out in outs[1:]],
        [pltpu.VMEM((token_count // 2, width), jnp.float32)],
        long=True,
    )


def product_kernel(natural_order, at, left_ref, right_ref, own, away):
    values = left_ref[...]
    if len(right_ref.shape) == 3:
        first, second = matmul(values, right_ref[0]), matmul(values, right_ref[1])
    else:
        both = matmul(values, right_ref[...])
        first, second = both[:, : both.shape[1] // 2], both[:, both.shape[1] // 2 :]
    if natural_order:
        first, second = jnp.where(at[0] == 0, first, second), jnp.where(at[0] == 0, second, first)
    own[...], away[...] = first, halved(second)


def product(at, left_array, right_array, natural_order=False):
    rows, depth = left_array.shape
    columns = right_array.size // depth // 2
    tile = rows // 6 if rows > 1024 else rows // 3
    outs = [stacked(rows, columns), stacked(rows, columns, dtype=jnp.bfloat16)]
    return kernel_call(
        functools.partial(product_kernel, natural_order),
        (rows // tile,),
        at,
        [left_array, right_array],
        [pl.BlockSpec((tile, depth), lambda i, at: (i, 0)), held(right_array)],
        outs,
        [pl.BlockSpec((tile, columns), lambda i, at: (i, 0))] * 2,
        long=True,
        vmem=56,
    )


def renew(grad, moment, weight, average, rate):
    moment_new = MOMENTUM * moment + grad
    weight_new = weight - rate * (grad + MOMENTUM * moment_new)
    average_new = AVERAGE * average + (1.0 - AVERAGE) * weight_new
    return (grad, moment_new, weight_new, average_new)


def local(
    tokens,
    lengths,
    attn_weight,
    attn_moment,
    attn_average,
    up_weight,
    up_moment,
    up_average,
    down_weight,
    down_moment,
    down_average,
    layer_vectors,
    vector_moment,
    vector_average,
    up_bias,
    bias_moment,
    bias_average,
    pos_table,
    pos_moment,
    pos_average,
):
    at = scalars(lengths[0, 0])
    stream = at[0]
    upper = stream == 1
    devices = lax.axis_size("batch")
    rows, hidden_half = up_weight.shape
    quarter = attn_weight.shape[2]
    width = 2 * quarter
    pos_half = pos_table.shape[0]
    slot_count = lengths.shape[2]

    misc = jnp.concatenate([layer_vectors.T, up_bias.reshape(2, rows).T], axis=1)
    misc = jnp.pad(misc, ((0, 0), (0, LANES - misc.shape[1])))
    entry_block = halved(
        jnp.concatenate([attn_weight[0], attn_weight[1], attn_weight[2], pos_table.T, misc], axis=1)
    )
    middle_block = halved(
        jnp.concatenate([up_weight, attn_weight[3], jnp.zeros((rows, LANES), jnp.float32)], axis=1)
    )
    triple = 3 * quarter
    pos_stop = triple + pos_half
    entry_gather = Gather(entry_block, width)
    entry_gather.far()
    entry_gather.near((2, 1))
    down_both = lax.all_gather(
        after(halved(down_weight), *entry_gather.sides), ("stream", "batch"), axis=0, tiled=True
    )
    middle_gather = Gather(
        after(middle_block, *entry_gather.sides), (hidden_half + quarter + LANES) // 2
    )
    middle_gather.far()
    entry_gather.near((1, 2), middle_gather.blocks)
    qkv_blocks, pos_blocks, misc_blocks = entry_gather.placed(
        at,
        (
            (0, triple, 0, "relative", 0, 0),
            (triple, pos_stop, 1, "", 0, pos_half),
            (pos_stop, pos_stop + LANES, 2, "stream", 0, 0),
        ),
        [
            stacked(2, devices, rows, triple, dtype=jnp.bfloat16),
            stacked(devices, rows, 2 * pos_half, dtype=jnp.bfloat16),
            stacked(2, devices, rows, LANES, dtype=jnp.bfloat16),
        ],
    )
    qkv = qkv_blocks.reshape(2, width, triple)
    pos_full = pos_blocks.reshape(width, 2 * pos_half)
    misc_full = misc_blocks.reshape(2, width, LANES)[:, :, :6].astype(jnp.float32)
    vectors = misc_full[:, :, :4].transpose(0, 2, 1).reshape(8, width)
    biases = misc_full[:, :, 4:].reshape(2, devices, rows, 2).transpose(0, 1, 3, 2)
    biases = biases.reshape(2, 1, hidden_half)

    def own_first(pair):
        return jnp.where(upper, pair[::-1], pair)

    shift = own_first(vectors[:2].reshape(2, 2, quarter).transpose(1, 0, 2))
    shift = jnp.stack([shift[:, 0], jnp.zeros((2, quarter), jnp.float32), shift[:, 1]], axis=1)
    hidden0, entry, triples = entered(
        at, tokens[0], pos_full, qkv, shift.reshape(2, 1, triple)
    )
    middle_gather.near((2, 1), triples)
    context_half, context_turned, probs = attend(after(at, *middle_gather.sides), triples)
    middle_gather.near((1, 2), context_half)
    up_blocks, out_blocks = middle_gather.placed(
        after(at, context_half),
        (
            (0, hidden_half, 0, "relative", 0, 0),
            (hidden_half, hidden_half + quarter, 1, "", 0, quarter),
        ),
        [
            stacked(2, devices, rows, hidden_half, dtype=jnp.bfloat16),
            stacked(devices, rows, width, dtype=jnp.bfloat16),
        ],
    )
    up = up_blocks.reshape(2, width, hidden_half)
    out_full = out_blocks.reshape(width, width)
    down = down_both.reshape(2, 2 * hidden_half, quarter)
    (entry2, normed1, inverse1, active, slope, normed2, inverse2, block_out, pooled, units) = forward(
        at, hidden0, context_half, out_full, vectors, up, own_first(biases), down
    )

    units = units[None]
    bit = 0
    while 1 << bit < devices:
        step = min(2, devices.bit_length() - 1 - bit)
        arrived = [exchanged(units, "batch", d << bit) for d in range(1, 1 << step)]
        units = jnp.concatenate([units] + arrived, axis=0)
        bit += step
    units = units.reshape(-1, units.shape[2])
    others = exchanged(units, "stream", 1)
    dresid2, dresid2_half, sums2 = loss_back(
        at, units, others, pooled, normed2, inverse2, vectors
    )

    def blocks(values):
        return values.reshape(devices // 4, 2, 2, values.shape[0] // devices, values.shape[1])

    down_own, down_away = product(at, active, dresid2_half, True)
    down_in = exchanged(down_away, "stream", 1)
    by_rows = down_weight.shape[0] % 32 == 0
    half_rows = down_weight.shape[0] // 2
    down_pair = (blocks(down_own), blocks(down_in))
    if by_rows:
        down_sides = [[down_pair + (half_rows, k, quarter, 0, True)] for k in range(2)]
    else:
        down_sides = [
            [down_pair + (2 * half_rows, 0, LANES, k, True) for k in ks] for ks in ((0, 1), (2,))
        ]
    down_fold = Fold(at, down_sides)
    down_parts = down_fold.first()
    down_first = down_fold.first_sent(down_parts)
    dpre, dpre_sum, dresid1, dresid1_half, sums1 = backward(
        after(at, *down_parts), dresid2, dresid2_half, slope, up, down, normed1, inverse1, vectors
    )
    down_fold.at = after(at, dresid1_half, *down_first)
    down_parts = down_fold.second(down_first)
    down_second, down_kept = down_fold.second_sent(down_parts)
    up_own, up_away = product(after(at, *down_parts), entry2, dpre)
    up_in = exchanged(up_away, "stream", 1)
    out_own, out_away = product(
        after(at, up_away, *down_second), context_turned, dresid1_half, True
    )
    out_in = exchanged(out_away, "stream", 1)
    down_fold.at = after(at, out_own, *down_second)
    down_parts = down_fold.third(down_second, down_kept)
    down_sum = down_fold.third_sent(down_parts)
    third = hidden_half // 3
    up_pair = (blocks(up_own), blocks(up_in))
    out_pair = (blocks(out_own), blocks(out_in))
    middle_fold = Fold(
        after(at, *down_parts),
        [
            [up_pair + (rows, 0, third, 0, False), up_pair + (rows, 0, third, 1, False)],
            [up_pair + (rows, 0, third, 2, False), out_pair + (rows, 0, quarter, 0, False)],
        ],
    )
    middle_parts = middle_fold.first()
    middle_first = middle_fold.first_sent(middle_parts)
    dcontext_half = halved(matmul(after(dresid1_half, *middle_parts), out_full, NT))
    dtriples, dsums = attend_back(at, triples, context_half, dcontext_half, probs)
    middle_fold.at = after(at, dtriples, *middle_first)
    middle_parts = middle_fold.second(middle_first)
    middle_second, middle_kept = middle_fold.second_sent(middle_parts)
    qkv_own, qkv_away = product(after(at, *middle_parts), entry, dtriples)
    qkv_in = exchanged(qkv_away, "stream", 1)
    dsums = own_first(dsums[:, :, 0]).transpose(1, 0, 2).reshape(2, width)
    lines = own_first(
        jnp.concatenate([dsums, sums1[:1], sums2[:1], sums1[1:], sums2[1:]], axis=0).reshape(2, 4, width)
    )
    bias_lines = dpre_sum.reshape(2, devices, 2, rows).transpose(0, 2, 1, 3).reshape(2, 2, width)
    lines = jnp.concatenate(
        [lines, bias_lines, jnp.zeros((2, LANES - 6, width), jnp.float32)], axis=1
    )
    input_grad, last_own, last_away = left(
        after(at, qkv_away, *middle_second), dresid1, dtriples, qkv, lines
    )
    last_in = exchanged(last_away, "stream", 1)
    middle_fold.at = after(at, input_grad, *middle_second)
    middle_parts = middle_fold.third(middle_second, middle_kept)
    middle_sum = middle_fold.third_sent(middle_parts)
    qkv_pair = (blocks(qkv_own), blocks(qkv_in))
    last_pair = (blocks(last_own), blocks(last_in))
    entry_fold = Fold(
        after(at, *middle_parts),
        [
            [qkv_pair + (rows, 0, quarter, 0, False), qkv_pair + (rows, 0, quarter, 1, False)],
            [
                qkv_pair + (rows, 0, quarter, 2, False),
                last_pair + (rows, 0, pos_half, 0, False),
                last_pair + (rows, 0, LANES, pos_half // LANES, False),
            ],
        ],
        wide=True,
    )
    entry_first = entry_fold.first_sent(entry_fold.first())
    entry_second, entry_kept = entry_fold.second_sent(entry_fold.second(entry_first))
    entry_sum = entry_fold.third_sent(entry_fold.third(entry_second, entry_kept))

    down_grad = down_sum
    if by_rows:
        down_grad = jnp.concatenate([down_sum[:, :quarter], down_sum[:, quarter:]], axis=0)
    attn_grad = jnp.stack(
        [entry_sum[:, k * quarter : (k + 1) * quarter] for k in range(3)]
        + [middle_sum[:, hidden_half : hidden_half + quarter]]
    )
    attn_all = renew(attn_grad, attn_moment, attn_weight, attn_average, RATE)
    up_all = renew(middle_sum[:, :hidden_half], up_moment, up_weight, up_average, RATE)
    down_all = renew(down_grad, down_moment, down_weight, down_average, RATE)
    vector_grad = entry_sum[:, pos_stop : pos_stop + 4].T
    vector_all = renew(vector_grad, vector_moment, layer_vectors, vector_average, RATE)
    bias_grad = entry_sum[:, pos_stop + 4 : pos_stop + 6].T.reshape(-1)
    bias_all = renew(bias_grad, bias_moment, up_bias, bias_average, RATE)
    pos_grad = entry_sum[:, triple:pos_stop].T
    pos_all = renew(pos_grad, pos_moment, pos_table, pos_average, POS_RATE)
    return (
        block_out[None],
        input_grad[None],
        *attn_all,
        *up_all,
        *down_all,
        *vector_all,
        *bias_all,
        *pos_all,
    )


def solution(mesh):
    tokens_at, weight_at = P("stream", "batch", None), P("batch", "stream")
    attn_at, rows_at, bias_at = P(None, "batch", "stream"), P("stream", "batch"), P(("stream", "batch"))
    kinds = (attn_at, weight_at, weight_at, rows_at, bias_at, rows_at)
    in_specs = (tokens_at, tokens_at) + tuple(kind for kind in kinds for _ in range(3))
    out_specs = (tokens_at, tokens_at) + tuple(kind for kind in kinds for _ in range(4))
    return jax.shard_map(local, mesh=mesh, in_specs=in_specs, out_specs=out_specs, check_vma=False)
```

```python
import functools
import math

import jax
import jax.numpy as jnp
from jax import lax
from jax.experimental import pallas as pl
from jax.experimental.pallas import tpu as pltpu
from jax.sharding import PartitionSpec as P

HEADS = 12


EPS_NORM = 1e-06
INV_TEMP = 100.0
LOSS_WEIGHT = 256.0
MOMENTUM = 0.5
AVERAGE = 0.5
RATE = 0.0001
POS_RATE = 0.01
NEGATIVE = -1e30
ROOT_HALF = 0.7071067811865476
ROOT_TWO_PI = 2.5066282746310002
LANES = 128
SLOT_COUNT, LENGTHS = 4, 5
CHUNK, BLOCKS = 256, 3
COST = pl.CostEstimate(flops=1000, bytes_accessed=1000, transcendentals=0)
LONG_COST = pl.CostEstimate(flops=10**12, bytes_accessed=10**9, transcendentals=0)
ANYWHERE = pl.BlockSpec(memory_space=pl.ANY)
HERE = pl.BlockSpec(memory_space=pltpu.VMEM)
FORWARD_VMEM, BACKWARD_VMEM, PRODUCT_VMEM, OTHER_VMEM = 22, 20, 14, 20
NN = (((1,), (0,)), ((), ()))
NT = (((1,), (1,)), ((), ()))
TN = (((0,), (0,)), ((), ()))


def halved(values):
    return values.astype(jnp.bfloat16)


def matmul(left, right, dims=NN):
    return lax.dot_general(left, right, dims, preferred_element_type=jnp.float32)


def stacked(*shape, dtype=jnp.float32):
    return jax.ShapeDtypeStruct(shape, dtype)


def far_off(*shape, dtype=jnp.bfloat16):
    return pltpu.HBM(shape, dtype)


def after(value, *earlier):
    return lax.optimization_barrier((value, earlier))[0]


def exchanged(block, axis, mask):
    count = lax.axis_size(axis)
    return lax.ppermute(block, axis, [(place, place ^ mask) for place in range(count)])


def scalars(lengths_row):
    batch = lax.axis_index("batch")
    places = [lax.axis_index("stream"), batch & 1, (batch >> 1) & 1, batch >> 2]
    counted = jnp.sum((lengths_row > 0).astype(jnp.int32))
    return jnp.concatenate([jnp.stack(places + [counted]), lengths_row]).astype(jnp.int32)


class Gather:
    def __init__(self, block, cut):
        self.cut = cut
        self.bits = lax.axis_size("batch").bit_length() - 1
        self.blocks, self.masks = block[None], [0]

    def far(self, *earlier):
        bit = self.bits
        while bit > 2:
            step = min(2, bit - 2)
            bit -= step
            offsets = [d << bit for d in range(1 << step)]
            arrived = [exchanged(self.blocks, "batch", offset) for offset in offsets[1:]]
            own = after(self.blocks, *earlier) if earlier else self.blocks
            self.blocks = jnp.concatenate([own] + arrived, axis=0)
            self.masks = [offset | mask for offset in offsets for mask in self.masks]
        self.sides = [self.blocks[:, :, : self.cut], self.blocks[:, :, self.cut :]]
        self.masks = [self.masks, self.masks]

    def near(self, flips, *earlier):
        for side, flip in enumerate(flips):
            part = self.sides[side]
            own = after(part, *earlier) if earlier else part
            self.sides[side] = jnp.concatenate([own, exchanged(part, "batch", flip)], axis=0)
            self.masks[side] = self.masks[side] + [flip | mask for mask in self.masks[side]]

    def placed(self, at, pieces, shapes, down=None):
        sources, moves = [], []
        for other in range(2):
            for side, part in enumerate(self.sides):
                sources.append(exchanged(part, "stream", 1) if other else part)
                base = self.cut * side
                for start, stop, target, lead, offset, span in pieces:
                    low, high = max(start, base), min(stop, base + part.shape[2])
                    if low >= high:
                        continue
                    for entry, mask in enumerate(self.masks[side]):
                        moves.append(
                            (len(sources) - 1, entry, mask, (low - base, high - base), target, lead,
                             other, offset + low - start, span)
                        )
        return placed(at, sources, moves, shapes, down)


def far_away(array):
    return pltpu.with_memory_space_constraint(array, pltpu.HBM)


def near_by(array):
    return pltpu.with_memory_space_constraint(array, pltpu.VMEM)


def place_kernel(moves, count, with_down, at_ref, *refs):
    sources, rest = refs[:count], refs[count:]
    stream = at_ref[0]
    copies = []
    if with_down:
        down, targets, down_held, sems = rest[0], rest[1:-2], rest[-2], rest[-1]
        half, quarter = down.shape[1] // 2, down.shape[2]
        for other in range(2):
            start = pl.multiple_of((other ^ stream) * half, half)
            for k in range(2):
                copies.append(
                    pltpu.make_async_copy(
                        down.at[k, pl.ds(start, half)],
                        down_held.at[pl.ds(other * half, half), pl.ds(k * quarter, quarter)],
                        sems.at[2 * other + k],
                    )
                )
        for copy in copies:
            copy.start()
    else:
        targets = rest
    batch = at_ref[1] + 2 * at_ref[2] + 4 * at_ref[3]
    for source, entry, mask, columns, target, lead, other, start, span in moves:
        core = stream ^ other
        low = pl.multiple_of(start + core * span, LANES) if span else start
        at = (batch ^ mask, slice(None), pl.ds(low, columns[1] - columns[0]))
        if lead == "relative":
            at = (other,) + at
        elif lead == "stream":
            at = (core,) + at
        targets[target][at] = sources[source][entry, :, columns[0] : columns[1]]
    for copy in copies:
        copy.wait()


def placed(at, sources, moves, shapes, down=None):
    held_here = pl.BlockSpec(memory_space=pltpu.VMEM)
    ins, in_specs, out_specs = list(sources), [held_here] * len(sources), [held_here] * len(shapes)
    scratch = []
    if down is not None:
        ins.append(far_away(down))
        in_specs.append(ANYWHERE)
        shapes = list(shapes) + [pltpu.VMEM((down.shape[1], 2 * down.shape[2]), down.dtype)]
        out_specs.append(held_here)
        scratch.append(pltpu.SemaphoreType.DMA((4,)))
    return pl.pallas_call(
        functools.partial(place_kernel, moves, len(sources), down is not None),
        in_specs=[pl.BlockSpec(memory_space=pltpu.SMEM)] + in_specs,
        out_specs=out_specs,
        out_shape=shapes,
        scratch_shapes=scratch,
        compiler_params=pltpu.CompilerParams(vmem_limit_bytes=24 << 20),
        cost_estimate=COST,
    )(at, *ins)


def two_words(values):
    half = values.shape[-1] // 2
    coarse = values.astype(jnp.bfloat16).astype(jnp.float32)
    lane = lax.broadcasted_iota(jnp.int32, values.shape, values.ndim - 1)
    rest = jnp.concatenate([(values - coarse)[..., half:], (values - coarse)[..., :half]], axis=-1)
    return jnp.where(lane < half, coarse, rest)


def one_word(block):
    half = block.shape[-1] // 2
    return block + jnp.concatenate([block[..., half:], block[..., :half]], axis=-1)


def received(block, wide):
    values = block.astype(jnp.float32)
    if not wide:
        return values
    return jnp.concatenate(
        [values[..., :-LANES], one_word(values[..., -LANES:])], axis=-1
    )


def sent(values, wide):
    if not wide:
        return halved(values)
    return jnp.concatenate(
        [halved(values[..., :-LANES]), halved(two_words(values[..., -LANES:]))], axis=-1
    )


def piece_spec(piece):
    array, _, rows, row_at, columns, column_at, _ = piece
    return pl.BlockSpec(
        (array.shape[0], 2, 2, rows, columns),
        lambda _, at: (0, 0, 0, row_at, column_at),
        pipeline_mode=pl.Buffered(buffer_count=1),
    )


def fold_call(kernel, count, at, ins, in_specs, outs, out_specs, long=False):
    size = sum(math.prod(o.shape) for o in outs) * 8
    return pl.pallas_call(
        kernel,
        grid_spec=pltpu.PrefetchScalarGridSpec(
            num_scalar_prefetch=1, grid=(count,), in_specs=in_specs, out_specs=out_specs
        ),
        out_shape=outs,
        compiler_params=pltpu.CompilerParams(vmem_limit_bytes=26 << 20),
        cost_estimate=LONG_COST if long else COST,
    )(at, *ins)


class Fold:
    def __init__(self, at, sides, wide=False):
        self.at, self.sides, self.wide = at, sides, (False, wide)
        self.count = sides[0][0][0].shape[0]
        self.rows = [side[0][2] for side in sides]
        self.columns = [sum(piece[4] for piece in side) for side in sides]

    def piece_values(self, refs, side, z, bit, which, core):
        columns = []
        for k, piece in enumerate(self.sides[side]):
            values = []
            for turn, ref in ((core, refs[2 * k]), (1 - core, refs[2 * k + 1])):
                place = z ^ (turn * (self.count // 2)) if piece[6] else z
                entry = ref[place, which, bit] if side == 0 else ref[place, bit, which]
                values.append(entry.astype(jnp.float32))
            wide = self.wide[side] and k == len(self.sides[side]) - 1
            columns.append(values[0] + (one_word(values[1]) if wide else values[1]))
        return jnp.concatenate(columns, axis=-1)

    def first_kernel(self, at_ref, *refs):
        place = 0
        for side, pieces in enumerate(self.sides):
            goes, stays = refs[2 * side - 4], refs[2 * side - 3]
            bit = at_ref[1 + side]
            for z in range(self.count):
                for which in range(2):
                    values = self.piece_values(refs[place:], side, z, 1 - bit, which, at_ref[0])
                    goes[z, which] = sent(values, self.wide[side])
                    stays[z, which] = self.piece_values(
                        refs[place:], side, z, bit, which, at_ref[0]
                    )
            place += 2 * len(pieces)

    def first(self):
        ins, in_specs, outs = [], [], []
        for side, pieces in enumerate(self.sides):
            for piece in pieces:
                ins += piece[:2]
                in_specs += [piece_spec(piece)] * 2
            shape = (self.count, 2, self.rows[side], self.columns[side])
            outs += [stacked(*shape, dtype=jnp.bfloat16), far_off(*shape, dtype=jnp.float32)]
        return fold_call(self.first_kernel, 1, self.at, ins, in_specs, outs, [whole_block(o) for o in outs])

    def first_sent(self, parts):
        self.stays = parts[1::2]
        return [exchanged(part, "batch", 1 << side) for side, part in enumerate(parts[::2])]

    def second_kernel(self, at_ref, *refs):
        outs = refs[-4:]
        for side in range(2):
            stays, arrived = refs[2 * side], refs[2 * side + 1]
            bit = at_ref[2 - side]
            for z in range(self.count):
                for which, out in ((1 - bit, outs[2 * side]), (bit, outs[2 * side + 1])):
                    values = stays[z, which] + received(arrived[z, which], self.wide[side])
                    out[z] = sent(values, self.wide[side]) if out.dtype == jnp.bfloat16 else values

    def second(self, arrived):
        ins, outs = [], []
        for side in range(2):
            ins += [far_away(self.stays[side]), arrived[side]]
            shape = (self.count, self.rows[side], self.columns[side])
            outs += [stacked(*shape, dtype=jnp.bfloat16), far_off(*shape, dtype=jnp.float32)]
        return fold_call(
            self.second_kernel, 1, self.at, ins, [whole_block(a) for a in ins], outs,
            [whole_block(out) for out in outs],
        )

    def second_sent(self, out):
        return [exchanged(out[0], "batch", 2), exchanged(out[2], "batch", 1)], [out[1], out[3]]

    def third_kernel(self, radix, at_ref, keep0, keep1, in0, in1, *outs):
        mine = at_ref[3] % radix
        for d, out in enumerate(outs):
            which = mine ^ d
            column = 0
            for side, (keep, arrived) in enumerate(((keep0, in0), (keep1, in1))):
                wide = self.wide[side]
                values = keep[which] + received(arrived[which], wide)
                width = values.shape[-1]
                out[0, :, column : column + width] = values if d == 0 else sent(values, wide)
                column += width

    def third(self, arrived, kept):
        radix = min(4, self.count)
        ins = [far_away(part) for part in kept] + arrived
        in_specs = [pl.BlockSpec((radix,) + a.shape[1:], lambda z, at: (z, 0, 0)) for a in ins]
        shape = (self.count // radix, self.rows[0], sum(self.columns))
        outs = [far_off(*shape, dtype=jnp.float32)] + [stacked(*shape, dtype=jnp.bfloat16)] * (radix - 1)
        out_specs = [pl.BlockSpec((1,) + o.shape[1:], lambda z, at: (z, 0, 0)) for o in outs]
        return fold_call(
            functools.partial(self.third_kernel, radix), self.count // radix, self.at, ins, in_specs, outs, out_specs, True
        )

    def third_sent(self, out, *earlier):
        radix = min(4, self.count)
        arrived = [exchanged(part, "batch", 4 * d) for d, part in enumerate(out) if d > 0]
        terms = [out[0]] + [after(part, *earlier) if earlier else part for part in arrived]
        total = None
        for term in terms:
            value = received(term, self.wide[1]) if term.dtype == jnp.bfloat16 else term
            total = value if total is None else total + value
        bit = 2 + radix.bit_length() - 1
        while total.shape[0] > 1:
            total = total.reshape((total.shape[0] // 2, 2) + total.shape[1:])
            upper = (lax.axis_index("batch") >> bit) & 1
            away = sent(lax.dynamic_index_in_dim(total, 1 - upper, 1, keepdims=False), False)
            total = lax.dynamic_index_in_dim(total, upper, 1, keepdims=False)
            total = total + exchanged(away, "batch", 1 << bit).astype(jnp.float32)
            bit += 1
        return total[0]


def attend_kernel(at, q_ref, k_ref, v_ref, context_ref, turned_ref, prob_ref, bias):
    half = pl.program_id(1)

    @pl.when(pl.program_id(0) == 0)
    def _():
        span = q_ref.shape[0]
        key = lax.broadcasted_iota(jnp.int32, (span, 1), 0) + half * span
        query = lax.broadcasted_iota(jnp.int32, (1, span), 1) + half * span
        bits = (2 * span).bit_length() - 1
        key_slot = (key * at[SLOT_COUNT]) >> bits
        query_slot = (query * at[SLOT_COUNT]) >> bits
        length = jnp.zeros((span, 1), jnp.int32)
        for slot in range(at.shape[0] - LENGTHS):
            length += jnp.where(key_slot == slot, at[LENGTHS + slot], 0)
        present = key - key_slot * bucket_of(at, 2 * span) < length
        code = jnp.where(present, key_slot, -1)
        bias[half] = jnp.where(code == query_slot, 0.0, NEGATIVE)

    rows, lanes = q_ref.shape
    size = lanes // 2
    first = lax.broadcasted_iota(jnp.int32, (rows, lanes), 1) < size
    keys = k_ref[...]
    none = jnp.zeros_like(keys)
    masked = (jnp.where(first, keys, none), jnp.where(first, none, keys))
    values = v_ref[...].T
    queries = q_ref[...] * jnp.bfloat16(1.0 / math.sqrt(size))
    products = [matmul(masked[h], queries, NT) for h in range(2)]
    probs = []
    for h in range(2):
        scores = products[h] + bias[half]
        weights = jnp.exp(scores - jnp.max(scores, axis=0, keepdims=True))
        probs.append(halved(weights * (1.0 / jnp.sum(weights, axis=0, keepdims=True))))
        prob_ref[0, 0, h] = probs[h]
    outs = [matmul(values[h * size : (h + 1) * size], probs[h]) for h in range(2)]
    context = jnp.concatenate(outs, axis=0)
    turned_ref[...] = halved(context)
    context_ref[...] = halved(context.T)


def natural(pairs, i, at):
    return ((i // (pairs // 2)) ^ at[0]) * (pairs // 2) + i % (pairs // 2)


def attend(at, triples):
    tokens, wide = triples.shape[1:]
    width = wide // 3 * 2
    rows, pairs = tokens // 2, width // LANES
    own = pairs // 2

    def part(p):
        return pl.BlockSpec((None, rows, LANES), lambda i, j, at: (i // own, j, p * own + i % own))

    return pl.pallas_call(
        attend_kernel,
        grid_spec=pltpu.PrefetchScalarGridSpec(
            num_scalar_prefetch=1,
            grid=(pairs, 2),
            in_specs=[
                part(0),
                part(1),
                part(2),
            ],
            out_specs=[
                pl.BlockSpec((rows, LANES), lambda i, j, at: (j, natural(pairs, i, at))),
                pl.BlockSpec((LANES, rows), lambda i, j, at: (natural(pairs, i, at), j)),
                pl.BlockSpec((1, 1, 2, rows, rows), lambda i, j, at: (i, j, 0, 0, 0)),
            ],
            scratch_shapes=[pltpu.VMEM((2, rows, rows), jnp.float32)],
        ),
        out_shape=[
            far_off(tokens, width),
            far_off(width, tokens),
            far_off(pairs, 2, 2, rows, rows),
        ],
        compiler_params=pltpu.CompilerParams(vmem_limit_bytes=24 << 20),
        cost_estimate=COST,
    )(at, *[far_away(triples)] * 3)


def attend_back_kernel(at, q_ref, k_ref, v_ref, context_ref, grad_ref, prob_ref, out_ref, sum_ref):
    rows, lanes = q_ref.shape
    size = lanes // 2
    scale = jnp.bfloat16(1.0 / math.sqrt(size))
    first = lax.broadcasted_iota(jnp.int32, (rows, lanes), 1) < size
    queries = q_ref[...] * scale
    keys = (k_ref[...] * scale).T
    values, grads = v_ref[...], grad_ref[...]
    none = jnp.zeros_like(values)
    masked = (jnp.where(first, values, none), jnp.where(first, none, values))
    products = (grads.astype(jnp.float32) * context_ref[...].astype(jnp.float32)).T
    dquery, dkey, dvalue = [], [], []
    for h in range(2):
        here = slice(h * size, (h + 1) * size)
        rowdot = jnp.sum(products[here], axis=0, keepdims=True)
        probs = prob_ref[0, 0, h]
        dprob = matmul(masked[h], grads, NT)
        dscore = halved(probs.astype(jnp.float32) * (dprob - rowdot))
        dkey.append(matmul(dscore, queries))
        dvalue.append(matmul(probs, grads))
        dquery.append(matmul(keys[here], dscore))
    dquery = jnp.concatenate(dquery, axis=0).T
    dkey = jnp.where(first, dkey[0], dkey[1])
    dvalue = jnp.where(first, dvalue[0], dvalue[1])
    pair = pl.program_id(2)
    quarter = out_ref.shape[2] // 3
    low = pl.multiple_of(pair * lanes, lanes)
    for p, part in enumerate((dquery, dkey, dvalue)):
        out_ref[0, :, pl.ds(p * quarter + low, lanes)] = halved(part)

    @pl.when((pl.program_id(1) == 0) & (pair == 0))
    def _():
        sum_ref[...] = jnp.zeros_like(sum_ref)

    sum_ref[0, 0, :, pl.ds(low, lanes)] += jnp.sum(dquery, axis=0, keepdims=True)
    sum_ref[0, 1, :, pl.ds(low, lanes)] += jnp.sum(dvalue, axis=0, keepdims=True)


def attend_back(at, triples, context, grad, probs):
    tokens, width = context.shape
    rows, pairs = tokens // 2, width // LANES
    own = pairs // 2

    def part(p):
        return pl.BlockSpec((None, rows, LANES), lambda r, j, i, at: (r, j, p * own + i))

    whole = pl.BlockSpec((rows, LANES), lambda r, j, i, at: (j, natural(pairs, r * own + i, at)))
    return pl.pallas_call(
        attend_back_kernel,
        grid_spec=pltpu.PrefetchScalarGridSpec(
            num_scalar_prefetch=1,
            grid=(2, 2, own),
            in_specs=[
                part(0),
                part(1),
                part(2),
                whole,
                whole,
                pl.BlockSpec((1, 1, 2, rows, rows), lambda r, j, i, at: (r * own + i, j, 0, 0, 0)),
            ],
            out_specs=[
                pl.BlockSpec((1, rows, triples.shape[2]), lambda r, j, i, at: (r, j, 0)),
                pl.BlockSpec((1, 2, 1, width // 2), lambda r, j, i, at: (r, 0, 0, 0)),
            ],
        ),
        out_shape=[pltpu.VMEM(triples.shape, jnp.bfloat16), stacked(2, 2, 1, width // 2)],
        compiler_params=pltpu.CompilerParams(vmem_limit_bytes=24 << 20),
        cost_estimate=LONG_COST,
    )(at, *[far_away(triples)] * 3, context, grad, probs)


def bucket_of(at, token_count):
    return jnp.where(at[SLOT_COUNT] == 2, token_count // 2, token_count // (at.shape[0] - LENGTHS))


def group_slot(at, group, token_count):
    slots = at.shape[0] - LENGTHS
    span = token_count // slots
    slot = (group * at[SLOT_COUNT]) // slots
    place = lax.broadcasted_iota(jnp.int32, (span, 1), 0) + group * span
    live = place - slot * bucket_of(at, token_count) < at[LENGTHS + slot]
    return slot, live.astype(jnp.float32)


def whole_block(array):
    return pl.BlockSpec(array.shape, lambda *_: (0,) * len(array.shape))


def kernel_call(kernel, grid, at, ins, in_specs, outs, out_specs, scratch=(), long=False, vmem=OTHER_VMEM):
    return pl.pallas_call(
        kernel,
        grid_spec=pltpu.PrefetchScalarGridSpec(
            num_scalar_prefetch=1, grid=grid, in_specs=in_specs, out_specs=out_specs,
            scratch_shapes=scratch,
        ),
        out_shape=outs,
        compiler_params=pltpu.CompilerParams(vmem_limit_bytes=vmem << 20),
        cost_estimate=LONG_COST if long else COST,
    )(at, *ins)


def entry_kernel(
    at, tokens, pos, weight, misc, hidden0, entry, triples, vectors, bias_lines, table, shift
):
    step = pl.program_id(0)
    rows, width = tokens.shape
    quarter = width // 2

    @pl.when(step == 0)
    def _():
        long = pos[...].astype(jnp.float32).T
        count = long.shape[0]
        span = 2 * count // (at.shape[0] - LENGTHS)
        short = jnp.concatenate([long[:span]] * (count // span), axis=0)
        table[...] = jnp.where(at[SLOT_COUNT] == 2, long, short)
        for core in range(2):
            lines = misc[core].astype(jnp.float32).T
            vectors[4 * core : 4 * core + 4] = lines[:4]
            bias_lines[2 * core : 2 * core + 2] = lines[4:6]
        shift[...] = jnp.zeros_like(shift)
        for other in range(2):
            here = pl.ds(pl.multiple_of((other ^ at[0]) * quarter, quarter), quarter)
            shift[other, :, :quarter] = vectors[BQ : BQ + 1, here]
            shift[other, :, 2 * quarter :] = vectors[BV : BV + 1, here]

    half_steps = pl.num_programs(0) // 2
    here = pl.ds(pl.multiple_of((step % half_steps) * rows, rows), rows)
    values = tokens[...].astype(jnp.float32) + table[here]
    hidden0[...] = values
    values = halved(values)
    entry[...] = values.T
    for other in range(2):
        triples[other] = halved(matmul(values, weight[other]) + shift[other])


def entered(at, tokens, pos, qkv, misc):
    token_count, width = tokens.shape
    triple = qkv.shape[2]
    outs = [
        far_off(token_count, width, dtype=jnp.float32),
        far_off(width, token_count),
        far_off(2, token_count, triple),
        stacked(8, width),
        stacked(4, width),
    ]
    return kernel_call(
        entry_kernel,
        (token_count // CHUNK,),
        at,
        [far_away(tokens), near_by(pos), near_by(qkv), near_by(misc)],
        tiles(tokens) + [HERE, HERE, HERE],
        outs,
        tiles(outs[0], outs[1])
        + [pl.BlockSpec((2, CHUNK, triple), lambda i, at: (0, i, 0))]
        + [whole_block(out) for out in outs[3:]],
        [
            pltpu.VMEM((token_count // 2, width), jnp.float32),
            pltpu.VMEM((2, 1, triple), jnp.float32),
        ],
    )


BQ, BV, BO, B2, G1, E1, G2, E2 = range(8)


def normal(values):
    center = values - jnp.mean(values, axis=-1, keepdims=True)
    inverse = lax.rsqrt(jnp.mean(center * center, axis=-1, keepdims=True) + EPS_NORM)
    return center * inverse, inverse


def held(array):
    return pl.BlockSpec(
        array.shape, lambda *_: (0,) * len(array.shape), pipeline_mode=pl.Buffered(buffer_count=1)
    )


def tiles(*arrays):
    return [
        pl.BlockSpec((CHUNK, a.shape[1]), lambda i, at: (i, 0))
        if a.shape[0] == arrays[0].shape[0]
        else pl.BlockSpec((a.shape[0], CHUNK), lambda i, at: (0, i))
        for a in arrays
    ]


def forward_kernel(
    at, hidden0, context, out_weight, vectors, up, up_bias, down,
    entry2, normed1, inverse1, active, slope, normed2, inverse2, block_out, pooled, units, acts,
):
    step = pl.program_id(0)
    rows, width = hidden0.shape
    token_count = rows * pl.num_programs(0)
    resid = hidden0[...] + matmul(context[...], out_weight[...]) + vectors[BO : BO + 1]
    normed, inverse = normal(resid)
    hidden1 = normed * vectors[G1 : G1 + 1] + vectors[E1 : E1 + 1]
    normed1[...], inverse1[...] = halved(normed), inverse
    entry = halved(hidden1)
    entry2[...] = entry.T
    half = up.shape[2]
    span = half // BLOCKS
    for other in range(2):
        for block in range(BLOCKS):
            here = slice(block * span, (block + 1) * span)
            there = slice(other * half + block * span, other * half + (block + 1) * span)
            values = matmul(entry, up[other, :, here]) + up_bias[other, :, here]
            cumulative = 0.5 + 0.5 * lax.erf(values * ROOT_HALF)
            acted = halved(values * cumulative)
            acts[:, there] = acted
            active[there] = acted.T
            density = jnp.exp(-0.5 * values * values) * (1.0 / ROOT_TWO_PI)
            slope[:, there] = halved(cumulative + values * density)
    total = hidden1 + vectors[B2 : B2 + 1] + matmul(acts[...], down[...])
    normed, inverse = normal(total)
    hidden2 = normed * vectors[G2 : G2 + 1] + vectors[E2 : E2 + 1]
    normed2[...], inverse2[...] = halved(normed), inverse
    block_out[...] = halved(hidden2)

    @pl.when(step == 0)
    def _():
        pooled[...] = jnp.zeros_like(pooled)

    slots = pooled.shape[0]
    span = token_count // slots
    for group in range(rows // span):
        slot, live = group_slot(at, step * (rows // span) + group, token_count)
        part = hidden2[group * span : (group + 1) * span] * live
        pooled[pl.ds(slot, 1)] += jnp.sum(part, axis=0, keepdims=True)

    @pl.when(step == pl.num_programs(0) - 1)
    def _():
        row = lax.broadcasted_iota(jnp.int32, (slots, LANES), 0)
        length = jnp.zeros((slots, LANES), jnp.int32)
        for slot in range(slots):
            length += jnp.where(row == slot, at[LENGTHS + slot], 0)
        mean = pooled[...] * (1.0 / jnp.maximum(length[:, :1], 1).astype(jnp.float32))
        pooled[...] = mean
        squares = jnp.sum(mean * mean, axis=-1, keepdims=True)
        units[:, :width] = halved(mean * lax.rsqrt(squares + EPS_NORM))
        first = lax.broadcasted_iota(jnp.int32, (slots, LANES), 1) == 0
        units[:, width:] = halved(jnp.where(first & (length > 0), 1.0, 0.0))


def forward(at, hidden0, context, out_weight, vectors, up, up_bias, down):
    token_count, width = hidden0.shape
    slots = at.shape[0] - LENGTHS
    hidden = 2 * up.shape[2]
    half = functools.partial(stacked, dtype=jnp.bfloat16)
    outs = [
        far_off(width, token_count),
        far_off(token_count, width),
        stacked(token_count, 1),
        pltpu.VMEM((hidden, token_count), jnp.bfloat16),
        pltpu.VMEM((token_count, hidden), jnp.bfloat16),
        far_off(token_count, width),
        stacked(token_count, 1),
        far_off(token_count, width),
        stacked(slots, width),
        half(slots, width + LANES),
    ]
    return kernel_call(
        forward_kernel,
        (token_count // CHUNK,),
        at,
        [far_away(hidden0), far_away(context), out_weight, vectors, near_by(up), up_bias, near_by(down)],
        tiles(hidden0, context)
        + [held(out_weight), held(vectors), HERE, held(up_bias), HERE],
        outs,
        tiles(hidden0, *outs[:8])[1:] + [whole_block(out) for out in outs[8:]],
        [pltpu.VMEM((CHUNK, hidden), jnp.bfloat16)],
        vmem=FORWARD_VMEM,
    )


def norm_back(grad, normed, inverse, gain):
    scaled = grad * gain
    inner = (
        scaled
        - jnp.mean(scaled, axis=-1, keepdims=True)
        - normed * jnp.mean(scaled * normed, axis=-1, keepdims=True)
    )
    return inner * inverse


def loss_kernel(
    at, units, others, pooled, normed2, inverse2, vectors,
    dresid, dresid_half, sums, dpool,
):
    slots, width = pooled.shape
    count = units.shape[0]
    step = pl.program_id(0)

    @pl.when(step == 0)
    def _():
        own, own_flags = units[:, :width], units[:, width:]
        other, other_flags = others[:, :width], others[:, width:]
        lane = lax.broadcasted_iota(jnp.int32, (slots, LANES), 1)
        one_hot = halved(jnp.where(lane == 0, 1.0, 0.0))
        own_row = matmul(one_hot, own_flags, NT)[:1] > 0
        other_row = matmul(one_hot, other_flags, NT)[:1] > 0

        def shares(lines, columns, live):
            logits = matmul(lines, columns, NT) * INV_TEMP
            logits = jnp.where(live, logits, NEGATIVE)
            weights = jnp.exp(logits - jnp.max(logits, axis=-1, keepdims=True))
            return weights / jnp.sum(weights, axis=-1, keepdims=True)

        row = lax.broadcasted_iota(jnp.int32, (slots, count), 0)
        column = lax.broadcasted_iota(jnp.int32, (slots, count), 1)
        target = jnp.where(row == column, 1.0, 0.0)
        row_live = own_flags[:slots, :1].astype(jnp.float32)
        dlogit = halved(LOSS_WEIGHT * (shares(own[:slots], other, other_row) - target) * row_live)
        near = shares(other, own, own_row)[:, :LANES]
        row = lax.broadcasted_iota(jnp.int32, (count, LANES), 0)
        column = lax.broadcasted_iota(jnp.int32, (count, LANES), 1)
        target = jnp.where(row == column, 1.0, 0.0)
        other_live = other_flags[:, :1].astype(jnp.float32)
        dnear = LOSS_WEIGHT * (near - target) * other_live
        dnear = halved(jnp.where(column < slots, dnear, 0.0))
        dunit = INV_TEMP * (matmul(dlogit, other) + matmul(dnear, other, TN)[:slots])
        mean = pooled[...]
        inverse = lax.rsqrt(jnp.sum(mean * mean, axis=-1, keepdims=True) + EPS_NORM)
        along = jnp.sum(mean * dunit, axis=-1, keepdims=True)
        grad = inverse * dunit - inverse * inverse * inverse * mean * along
        slot_row = lax.broadcasted_iota(jnp.int32, (slots, 1), 0)
        length = jnp.zeros((slots, 1), jnp.int32)
        for slot in range(slots):
            length += jnp.where(slot_row == slot, at[LENGTHS + slot], 0)
        dpool[...] = grad * (1.0 / jnp.maximum(length, 1).astype(jnp.float32))
        sums[...] = jnp.zeros_like(sums)

    gain = vectors[G2 : G2 + 1]
    token_count = normed2.shape[0] * pl.num_programs(0)
    span = token_count // slots
    groups = normed2.shape[0] // span
    for group in range(groups):
        here = pl.ds(group * span, span)
        slot, live = group_slot(at, step * groups + group, token_count)
        dhidden = dpool[pl.ds(slot, 1)] * live
        normed = normed2[here].astype(jnp.float32)
        values = norm_back(dhidden, normed, inverse2[here], gain)
        dresid[here] = values
        dresid_half[here] = halved(values)
        for k, terms in enumerate((values, dhidden * normed, dhidden)):
            sums[k : k + 1] += jnp.sum(terms, axis=0, keepdims=True)


def loss_back(at, units, others, pooled, normed2, inverse2, vectors):
    token_count, width = normed2.shape
    half = functools.partial(stacked, dtype=jnp.bfloat16)
    ins = [units, others, pooled, far_away(normed2), inverse2, vectors]
    outs = [
        far_off(token_count, width, dtype=jnp.float32),
        half(token_count, width),
        stacked(3, width),
    ]
    return kernel_call(
        loss_kernel,
        (token_count // CHUNK,),
        at,
        ins,
        [held(a) for a in ins[:3]] + tiles(*ins[3:5]) + [held(vectors)],
        outs,
        tiles(*outs[:2]) + [whole_block(outs[2])],
        [pltpu.VMEM(pooled.shape, jnp.float32)],
    )


def backward_kernel(
    at, dresid2, dresid2_half, slope, up, down, normed1, inverse1, vectors,
    dpre, dpre_sum, dresid, dresid_half, sums,
):
    @pl.when(pl.program_id(0) == 0)
    def _():
        dpre_sum[...] = jnp.zeros_like(dpre_sum)
        sums[...] = jnp.zeros_like(sums)

    half = up.shape[2]
    span = half // BLOCKS
    grad = dresid2_half[...]
    for block in range(2 * BLOCKS):
        here = slice(block * span, (block + 1) * span)
        dactive = matmul(grad, down[here], NT)
        values = dactive * slope[:, here].astype(jnp.float32)
        dpre_sum[:, here] += jnp.sum(values, axis=0, keepdims=True)
        dpre[:, here] = halved(values)
    dhidden = dresid2[...]
    for other in range(2):
        dhidden += matmul(dpre[:, other * half : (other + 1) * half], up[other], NT)
    normed = normed1[...].astype(jnp.float32)
    values = norm_back(dhidden, normed, inverse1[...], vectors[G1 : G1 + 1])
    dresid[...] = values
    rounded = halved(values)
    dresid_half[...] = rounded
    for k, terms in enumerate((values, dhidden * normed, dhidden)):
        sums[k : k + 1] += jnp.sum(terms, axis=0, keepdims=True)


def backward(at, dresid2, dresid2_half, slope, up, down, normed1, inverse1, vectors):
    token_count, width = dresid2.shape
    hidden = 2 * up.shape[2]
    half = functools.partial(stacked, dtype=jnp.bfloat16)
    outs = [
        pltpu.VMEM((token_count, hidden), jnp.bfloat16),
        stacked(1, hidden),
        far_off(token_count, width, dtype=jnp.float32),
        half(token_count, width),
        stacked(3, width),
    ]
    out_specs = tiles(outs[0], *outs[2:4])
    return kernel_call(
        backward_kernel,
        (token_count // CHUNK,),
        at,
        [far_away(dresid2), dresid2_half, near_by(slope), near_by(up), near_by(down), far_away(normed1), inverse1, vectors],
        tiles(dresid2, dresid2_half, slope) + [HERE, HERE] + tiles(normed1, inverse1)
        + [held(vectors)],
        outs,
        out_specs[:1] + [whole_block(outs[1])] + out_specs[1:] + [whole_block(outs[4])],
        vmem=BACKWARD_VMEM,
        long=True,
    )


def leave_kernel(
    at, dresid1, dtriples, qkv, dsums, sums1, sums2, dpre_sum, input_grad, last_own, last_away, total, turned,
):
    step = pl.program_id(0)
    rows = dresid1.shape[0]
    values = dresid1[...]
    for other in range(2):
        values = values + matmul(dtriples[other], qkv[other], NT)
    input_grad[...] = values
    half_steps = pl.num_programs(0) // 2
    here = pl.ds(pl.multiple_of((step % half_steps) * rows, rows), rows)

    @pl.when(step < half_steps)
    def _():
        total[here] = values

    @pl.when(step >= half_steps)
    def _():
        total[here] += values

    @pl.when(step == pl.num_programs(0) - 1)
    def _():
        count = total.shape[0]
        long = total[...]
        span = 2 * count // (at.shape[0] - LENGTHS)
        short = sum(long[k * span : (k + 1) * span] for k in range(count // span))
        short = jnp.concatenate([short, jnp.zeros((count - span, long.shape[1]), jnp.float32)], axis=0)
        columns = jnp.where(at[SLOT_COUNT] == 2, long, short).T
        left, right = columns[:, : count // 2], columns[:, count // 2 :]
        last_own[:, : count // 2] = jnp.where(at[0] == 0, left, right)
        last_away[:, : count // 2] = halved(jnp.where(at[0] == 0, right, left))
        width = long.shape[1]
        first = [jnp.concatenate([dsums[0, k], dsums[1, k]], axis=1) for k in range(2)]
        swapped = [jnp.concatenate([dsums[1, k], dsums[0, k]], axis=1) for k in range(2)]
        heads = [jnp.where(at[0] == 0, a, b) for a, b in zip(first, swapped)]
        vectors = [heads + [sums1[:1], sums2[:1]], [sums1[1:2], sums1[2:3], sums2[1:2], sums2[2:3]]]
        blank = jnp.zeros((LANES - 4, width), jnp.float32)
        vectors = [jnp.concatenate(rows + [blank], axis=0).T for rows in vectors]
        lane = lax.broadcasted_iota(jnp.int32, (width, LANES), 1)
        for other, (out, words) in enumerate(((last_own, False), (last_away, True))):
            row = dpre_sum[:, other * 2 * width : (other + 1) * 2 * width]
            turned[...] = jnp.broadcast_to(row, (LANES, 2 * width)).T
            lines = jnp.where(at[0] == other, vectors[0], vectors[1])
            for k in range(2):
                lines = jnp.where(lane == 4 + k, turned[pl.ds(k, width, 2)], lines)
            out[:, count // 2 :] = halved(two_words(lines)) if words else lines


def left(at, dresid1, dtriples, qkv, dsums, sums1, sums2, dpre_sum):
    token_count, width = dresid1.shape
    triple = qkv.shape[2]
    columns = token_count // 4 + LANES
    small = [dsums, sums1, sums2, dpre_sum]
    outs = [
        stacked(token_count, width),
        stacked(width, columns),
        stacked(width, columns, dtype=jnp.bfloat16),
    ]
    return kernel_call(
        leave_kernel,
        (token_count // CHUNK,),
        at,
        [far_away(dresid1), near_by(dtriples), qkv] + small,
        tiles(dresid1)
        + [pl.BlockSpec((2, CHUNK, triple), lambda i, at: (0, i, 0)), held(qkv)]
        + [held(a) for a in small],
        outs,
        tiles(outs[0]) + [whole_block(out) for out in outs[1:]],
        [
            pltpu.VMEM((token_count // 2, width), jnp.float32),
            pltpu.VMEM((2 * width, LANES), jnp.float32),
        ],
        long=True,
    )


def product_kernel(natural_order, at, left_ref, right_ref, own, away):
    values = left_ref[...]
    if len(right_ref.shape) == 3:
        first, second = matmul(values, right_ref[0]), matmul(values, right_ref[1])
    else:
        both = matmul(values, right_ref[...])
        first, second = both[:, : both.shape[1] // 2], both[:, both.shape[1] // 2 :]
    first, second = halved(first), halved(second)
    if natural_order:
        first, second = jnp.where(at[0] == 0, first, second), jnp.where(at[0] == 0, second, first)
    own[...], away[...] = first, second


def product(at, left_array, right_array, natural_order=False, near=None):
    rows, depth = left_array.shape
    columns = right_array.size // depth // 2
    tile = rows // 6 if rows > 1024 else rows // 3
    outs = [stacked(rows, columns, dtype=jnp.bfloat16)] * 2
    return kernel_call(
        functools.partial(product_kernel, natural_order),
        (rows // tile,),
        at,
        [near_by(left_array) if near == 0 else left_array, near_by(right_array) if near == 1 else right_array],
        [pl.BlockSpec((tile, depth), lambda i, at: (i, 0)), HERE if near == 1 else held(right_array)],
        outs,
        [pl.BlockSpec((tile, columns), lambda i, at: (i, 0))] * 2,
        long=True,
        vmem=PRODUCT_VMEM,
    )


def renew(grad, moment, weight, average, rate):
    moment_new = MOMENTUM * moment + grad
    weight_new = weight - rate * (grad + MOMENTUM * moment_new)
    average_new = AVERAGE * average + (1.0 - AVERAGE) * weight_new
    return (grad, moment_new, weight_new, average_new)


def local(
    tokens,
    lengths,
    attn_weight,
    attn_moment,
    attn_average,
    up_weight,
    up_moment,
    up_average,
    down_weight,
    down_moment,
    down_average,
    layer_vectors,
    vector_moment,
    vector_average,
    up_bias,
    bias_moment,
    bias_average,
    pos_table,
    pos_moment,
    pos_average,
):
    at = scalars(lengths[0, 0])
    stream = at[0]
    upper = stream == 1
    devices = lax.axis_size("batch")
    rows, hidden_half = up_weight.shape
    quarter = attn_weight.shape[2]
    width = 2 * quarter
    pos_half = pos_table.shape[0]
    slot_count = lengths.shape[2]

    misc = jnp.concatenate([layer_vectors.T, up_bias.reshape(rows, 2)], axis=1)
    misc = jnp.pad(misc, ((0, 0), (0, LANES - misc.shape[1])))
    entry_block = halved(
        jnp.concatenate([attn_weight[0], attn_weight[1], attn_weight[2], pos_table.T, misc], axis=1)
    )
    middle_block = halved(
        jnp.concatenate([up_weight, attn_weight[3], jnp.zeros((rows, LANES), jnp.float32)], axis=1)
    )
    triple = 3 * quarter
    pos_stop = triple + pos_half
    entry_gather = Gather(entry_block, width)
    entry_gather.far()
    down_both = lax.all_gather(
        after(halved(down_weight), entry_gather.blocks), ("stream", "batch"), axis=0, tiled=True
    )
    entry_gather.near((2, 1))
    middle_gather = Gather(
        after(middle_block, *entry_gather.sides), (hidden_half + quarter + LANES) // 2
    )
    middle_gather.far()
    entry_gather.near((1, 2), middle_gather.blocks)
    qkv_blocks, pos_blocks, misc_blocks = entry_gather.placed(
        at,
        (
            (0, triple, 0, "relative", 0, 0),
            (triple, pos_stop, 1, "", 0, pos_half),
            (pos_stop, pos_stop + LANES, 2, "stream", 0, 0),
        ),
        [
            pltpu.VMEM((2, devices, rows, triple), jnp.bfloat16),
            pltpu.VMEM((devices, rows, 2 * pos_half), jnp.bfloat16),
            pltpu.VMEM((2, devices, rows, LANES), jnp.bfloat16),
        ],
    )
    qkv = qkv_blocks.reshape(2, width, triple)
    pos_full = pos_blocks.reshape(width, 2 * pos_half)
    def own_first(pair):
        return jnp.where(upper, pair[::-1], pair)

    hidden0, entry, triples, vectors, bias_lines = entered(
        at, tokens[0], pos_full, qkv, misc_blocks.reshape(2, width, LANES)
    )
    biases = bias_lines.reshape(2, 2, width).transpose(0, 2, 1).reshape(2, 1, hidden_half)
    middle_gather.near((2, 1), triples)
    context_half, context_turned, probs = attend(after(at, *middle_gather.sides), triples)
    middle_gather.near((1, 2), context_half)
    up_blocks, out_blocks, down = middle_gather.placed(
        after(at, context_half),
        (
            (0, hidden_half, 0, "relative", 0, 0),
            (hidden_half, hidden_half + quarter, 1, "", 0, quarter),
        ),
        [
            pltpu.VMEM((2, devices, rows, hidden_half), jnp.bfloat16),
            stacked(devices, rows, width, dtype=jnp.bfloat16),
        ],
        down_both.reshape(2, 2 * hidden_half, quarter),
    )
    up = up_blocks.reshape(2, width, hidden_half)
    out_full = out_blocks.reshape(width, width)
    (entry2, normed1, inverse1, active, slope, normed2, inverse2, block_out, pooled, units) = forward(
        at, hidden0, context_half, out_full, vectors, up, own_first(biases), down
    )

    units = units[None]
    bit = 0
    while 1 << bit < devices:
        step = min(2, devices.bit_length() - 1 - bit)
        arrived = [exchanged(units, "batch", d << bit) for d in range(1, 1 << step)]
        units = jnp.concatenate([units] + arrived, axis=0)
        bit += step
    units = units.reshape(-1, units.shape[2])
    others = exchanged(units, "stream", 1)
    dresid2, dresid2_half, sums2 = loss_back(
        at, units, others, pooled, normed2, inverse2, vectors
    )

    def blocks(values):
        return values.reshape(devices // 4, 2, 2, values.shape[0] // devices, values.shape[1])

    down_own, down_away = product(at, active, dresid2_half, True, near=0)
    down_in = exchanged(down_away, "stream", 1)
    by_rows = down_weight.shape[0] % 32 == 0
    half_rows = down_weight.shape[0] // 2
    down_pair = (blocks(down_own), blocks(down_in))
    if by_rows:
        down_sides = [[down_pair + (half_rows, k, quarter, 0, True)] for k in range(2)]
    else:
        down_sides = [
            [down_pair + (2 * half_rows, 0, LANES, k, True) for k in ks] for ks in ((0, 1), (2,))
        ]
    down_fold = Fold(at, down_sides)
    down_parts = down_fold.first()
    down_first = down_fold.first_sent(down_parts)
    dpre, dpre_sum, dresid1, dresid1_half, sums1 = backward(
        after(at, *down_parts), dresid2, dresid2_half, slope, up, down, normed1, inverse1, vectors
    )
    down_fold.at = after(at, dresid1_half, *down_first)
    down_parts = down_fold.second(down_first)
    down_second, down_kept = down_fold.second_sent(down_parts)
    up_own, up_away = product(after(at, *down_parts), entry2, dpre, near=1)
    up_in = exchanged(up_away, "stream", 1)
    out_own, out_away = product(
        after(at, up_away, *down_second), context_turned, dresid1_half, True
    )
    out_in = exchanged(out_away, "stream", 1)
    down_fold.at = after(at, out_own, *down_second)
    down_parts = down_fold.third(down_second, down_kept)
    third = hidden_half // 3
    up_pair = (blocks(up_own), blocks(up_in))
    out_pair = (blocks(out_own), blocks(out_in))
    middle_fold = Fold(
        after(at, *down_parts),
        [
            [up_pair + (rows, 0, third, 0, False), up_pair + (rows, 0, third, 1, False)],
            [up_pair + (rows, 0, third, 2, False), out_pair + (rows, 0, quarter, 0, False)],
        ],
    )
    middle_parts = middle_fold.first()
    middle_first = middle_fold.first_sent(middle_parts)
    dcontext_half = halved(matmul(after(dresid1_half, *middle_parts), out_full, NT))
    dtriples, dsums = attend_back(at, triples, context_half, dcontext_half, probs)
    qkv_own, qkv_away = product(at, entry, dtriples, near=1)
    down_sum = down_fold.third_sent(down_parts, qkv_away)
    qkv_in = exchanged(qkv_away, "stream", 1)
    middle_fold.at = after(at, qkv_away, *middle_first)
    middle_parts = middle_fold.second(middle_first)
    middle_second, middle_kept = middle_fold.second_sent(middle_parts)
    input_grad, last_own, last_away = left(
        after(at, qkv_away, *middle_parts), dresid1, dtriples, qkv, dsums, sums1, sums2, dpre_sum
    )
    last_in = exchanged(last_away, "stream", 1)
    qkv_pair = (blocks(qkv_own), blocks(qkv_in))
    last_pair = (blocks(last_own), blocks(last_in))
    entry_fold = Fold(
        at,
        [
            [qkv_pair + (rows, 0, quarter, 0, False), qkv_pair + (rows, 0, quarter, 1, False)],
            [
                qkv_pair + (rows, 0, quarter, 2, False),
                last_pair + (rows, 0, pos_half, 0, False),
                last_pair + (rows, 0, LANES, pos_half // LANES, False),
            ],
        ],
        wide=True,
    )
    entry_parts = entry_fold.first()
    entry_first = entry_fold.first_sent(entry_parts)
    middle_fold.at = after(at, *entry_parts, *middle_second)
    middle_parts = middle_fold.third(middle_second, middle_kept)
    entry_fold.at = after(at, *middle_parts)
    entry_parts = entry_fold.second(entry_first)
    middle_sum = middle_fold.third_sent(middle_parts, *entry_parts)
    entry_second, entry_kept = entry_fold.second_sent(entry_parts)
    entry_sum = entry_fold.third_sent(entry_fold.third(entry_second, entry_kept))

    down_grad = down_sum
    if by_rows:
        down_grad = jnp.concatenate([down_sum[:, :quarter], down_sum[:, quarter:]], axis=0)
    attn_grad = jnp.stack(
        [entry_sum[:, k * quarter : (k + 1) * quarter] for k in range(3)]
        + [middle_sum[:, hidden_half : hidden_half + quarter]]
    )
    attn_all = renew(attn_grad, attn_moment, attn_weight, attn_average, RATE)
    up_all = renew(middle_sum[:, :hidden_half], up_moment, up_weight, up_average, RATE)
    down_all = renew(down_grad, down_moment, down_weight, down_average, RATE)
    vector_grad = entry_sum[:, pos_stop : pos_stop + 4].T
    vector_all = renew(vector_grad, vector_moment, layer_vectors, vector_average, RATE)
    bias_grad = entry_sum[:, pos_stop + 4 : pos_stop + 6].reshape(-1)
    bias_all = renew(bias_grad, bias_moment, up_bias, bias_average, RATE)
    pos_grad = entry_sum[:, triple:pos_stop].T
    pos_all = renew(pos_grad, pos_moment, pos_table, pos_average, POS_RATE)
    return (
        block_out[None],
        input_grad[None],
        *attn_all,
        *up_all,
        *down_all,
        *vector_all,
        *bias_all,
        *pos_all,
    )


def solution(mesh):
    tokens_at, weight_at = P("stream", "batch", None), P("batch", "stream")
    attn_at, rows_at, bias_at = P(None, "batch", "stream"), P("stream", "batch"), P(("stream", "batch"))
    kinds = (attn_at, weight_at, weight_at, rows_at, bias_at, rows_at)
    in_specs = (tokens_at, tokens_at) + tuple(kind for kind in kinds for _ in range(3))
    out_specs = (tokens_at, tokens_at) + tuple(kind for kind in kinds for _ in range(4))
    return jax.shard_map(local, mesh=mesh, in_specs=in_specs, out_specs=out_specs, check_vma=False)
```

```python
import functools
import math

import jax
import jax.numpy as jnp
from jax import lax
from jax.experimental import pallas as pl
from jax.experimental.pallas import tpu as pltpu
from jax.sharding import PartitionSpec as P

HEADS = 12


EPS_NORM = 1e-06
INV_TEMP = 100.0
LOSS_WEIGHT = 256.0
MOMENTUM = 0.5
AVERAGE = 0.5
RATE = 0.0001
POS_RATE = 0.01
NEGATIVE = -1e30
ROOT_HALF = 0.7071067811865476
ROOT_TWO_PI = 2.5066282746310002
LANES = 128
SLOT_COUNT, LENGTHS = 4, 5
CHUNK, BLOCKS = 256, 3
COST = pl.CostEstimate(flops=1000, bytes_accessed=1000, transcendentals=0)
LONG_COST = pl.CostEstimate(flops=10**12, bytes_accessed=10**9, transcendentals=0)
ANYWHERE = pl.BlockSpec(memory_space=pl.ANY)
HERE = pl.BlockSpec(memory_space=pltpu.VMEM)
FORWARD_VMEM, BACKWARD_VMEM, PRODUCT_VMEM, OTHER_VMEM = 22, 20, 14, 20
NN = (((1,), (0,)), ((), ()))
NT = (((1,), (1,)), ((), ()))
TN = (((0,), (0,)), ((), ()))


def halved(values):
    return values.astype(jnp.bfloat16)


def matmul(left, right, dims=NN):
    return lax.dot_general(left, right, dims, preferred_element_type=jnp.float32)


def stacked(*shape, dtype=jnp.float32):
    return jax.ShapeDtypeStruct(shape, dtype)


def far_off(*shape, dtype=jnp.bfloat16):
    return pltpu.HBM(shape, dtype)


def after(value, *earlier):
    return lax.optimization_barrier((value, earlier))[0]


def exchanged(block, axis, mask):
    count = lax.axis_size(axis)
    return lax.ppermute(block, axis, [(place, place ^ mask) for place in range(count)])


def scalars(lengths_row):
    batch = lax.axis_index("batch")
    places = [lax.axis_index("stream"), batch & 1, (batch >> 1) & 1, batch >> 2]
    counted = jnp.sum((lengths_row > 0).astype(jnp.int32))
    return jnp.concatenate([jnp.stack(places + [counted]), lengths_row]).astype(jnp.int32)


class Gather:
    def __init__(self, block, cut):
        self.cut = cut
        self.bits = lax.axis_size("batch").bit_length() - 1
        self.blocks, self.masks = block[None], [0]

    def far(self, *earlier):
        bit = self.bits
        while bit > 2:
            step = min(2, bit - 2)
            bit -= step
            offsets = [d << bit for d in range(1 << step)]
            arrived = [exchanged(self.blocks, "batch", offset) for offset in offsets[1:]]
            own = after(self.blocks, *earlier) if earlier else self.blocks
            self.blocks = jnp.concatenate([own] + arrived, axis=0)
            self.masks = [offset | mask for offset in offsets for mask in self.masks]
        self.sides = [self.blocks[:, :, : self.cut], self.blocks[:, :, self.cut :]]
        self.masks = [self.masks, self.masks]

    def near(self, flips, *earlier):
        for side, flip in enumerate(flips):
            part = self.sides[side]
            own = after(part, *earlier) if earlier else part
            self.sides[side] = jnp.concatenate([own, exchanged(part, "batch", flip)], axis=0)
            self.masks[side] = self.masks[side] + [flip | mask for mask in self.masks[side]]

    def placed(self, at, pieces, shapes, down=None):
        sources, moves = [], []
        for other in range(2):
            for side, part in enumerate(self.sides):
                sources.append(exchanged(part, "stream", 1) if other else part)
                base = self.cut * side
                for start, stop, target, lead, offset, span in pieces:
                    low, high = max(start, base), min(stop, base + part.shape[2])
                    if low >= high:
                        continue
                    for entry, mask in enumerate(self.masks[side]):
                        moves.append(
                            (len(sources) - 1, entry, mask, (low - base, high - base), target, lead,
                             other, offset + low - start, span)
                        )
        return placed(at, sources, moves, shapes, down)


def far_away(array):
    return pltpu.with_memory_space_constraint(array, pltpu.HBM)


def near_by(array):
    return pltpu.with_memory_space_constraint(array, pltpu.VMEM)


def place_kernel(moves, count, with_down, at_ref, *refs):
    sources, rest = refs[:count], refs[count:]
    stream = at_ref[0]
    copies = []
    if with_down:
        down, targets, down_held, sems = rest[0], rest[1:-2], rest[-2], rest[-1]
        half, quarter = down.shape[1] // 2, down.shape[2]
        for other in range(2):
            start = pl.multiple_of((other ^ stream) * half, half)
            for k in range(2):
                copies.append(
                    pltpu.make_async_copy(
                        down.at[k, pl.ds(start, half)],
                        down_held.at[pl.ds(other * half, half), pl.ds(k * quarter, quarter)],
                        sems.at[2 * other + k],
                    )
                )
        for copy in copies:
            copy.start()
    else:
        targets = rest
    batch = at_ref[1] + 2 * at_ref[2] + 4 * at_ref[3]
    for source, entry, mask, columns, target, lead, other, start, span in moves:
        core = stream ^ other
        low = pl.multiple_of(start + core * span, LANES) if span else start
        at = (batch ^ mask, slice(None), pl.ds(low, columns[1] - columns[0]))
        if lead == "relative":
            at = (other,) + at
        elif lead == "stream":
            at = (core,) + at
        targets[target][at] = sources[source][entry, :, columns[0] : columns[1]]
    for copy in copies:
        copy.wait()


def placed(at, sources, moves, shapes, down=None):
    held_here = pl.BlockSpec(memory_space=pltpu.VMEM)
    ins, in_specs, out_specs = list(sources), [held_here] * len(sources), [held_here] * len(shapes)
    scratch = []
    if down is not None:
        ins.append(far_away(down))
        in_specs.append(ANYWHERE)
        shapes = list(shapes) + [pltpu.VMEM((down.shape[1], 2 * down.shape[2]), down.dtype)]
        out_specs.append(held_here)
        scratch.append(pltpu.SemaphoreType.DMA((4,)))
    return pl.pallas_call(
        functools.partial(place_kernel, moves, len(sources), down is not None),
        in_specs=[pl.BlockSpec(memory_space=pltpu.SMEM)] + in_specs,
        out_specs=out_specs,
        out_shape=shapes,
        scratch_shapes=scratch,
        compiler_params=pltpu.CompilerParams(vmem_limit_bytes=24 << 20),
        cost_estimate=COST,
    )(at, *ins)


def two_words(values):
    half = values.shape[-1] // 2
    coarse = values.astype(jnp.bfloat16).astype(jnp.float32)
    lane = lax.broadcasted_iota(jnp.int32, values.shape, values.ndim - 1)
    rest = jnp.concatenate([(values - coarse)[..., half:], (values - coarse)[..., :half]], axis=-1)
    return jnp.where(lane < half, coarse, rest)


def one_word(block):
    half = block.shape[-1] // 2
    return block + jnp.concatenate([block[..., half:], block[..., :half]], axis=-1)


def received(block, wide):
    values = block.astype(jnp.float32)
    if not wide:
        return values
    return jnp.concatenate(
        [values[..., :-LANES], one_word(values[..., -LANES:])], axis=-1
    )


def sent(values, wide):
    if not wide:
        return halved(values)
    return jnp.concatenate(
        [halved(values[..., :-LANES]), halved(two_words(values[..., -LANES:]))], axis=-1
    )


def piece_spec(piece):
    array, _, rows, row_at, columns, column_at, _ = piece
    return pl.BlockSpec(
        (array.shape[0], 2, 2, rows, columns),
        lambda _, at: (0, 0, 0, row_at, column_at),
        pipeline_mode=pl.Buffered(buffer_count=1),
    )


def fold_call(kernel, count, at, ins, in_specs, outs, out_specs, long=False):
    size = sum(math.prod(o.shape) for o in outs) * 8
    return pl.pallas_call(
        kernel,
        grid_spec=pltpu.PrefetchScalarGridSpec(
            num_scalar_prefetch=1, grid=(count,), in_specs=in_specs, out_specs=out_specs
        ),
        out_shape=outs,
        compiler_params=pltpu.CompilerParams(vmem_limit_bytes=20 << 20),
        cost_estimate=LONG_COST if long else COST,
    )(at, *ins)


class Fold:
    def __init__(self, at, sides, wide=False):
        self.at, self.sides, self.wide = at, sides, (False, wide)
        self.count = sides[0][0][0].shape[0]
        self.rows = [side[0][2] for side in sides]
        self.columns = [sum(piece[4] for piece in side) for side in sides]

    def piece_values(self, refs, side, z, bit, which, core):
        columns = []
        for k, piece in enumerate(self.sides[side]):
            values = []
            for turn, ref in ((core, refs[2 * k]), (1 - core, refs[2 * k + 1])):
                place = z ^ (turn * (self.count // 2)) if piece[6] else z
                entry = ref[place, which, bit] if side == 0 else ref[place, bit, which]
                values.append(entry.astype(jnp.float32))
            wide = self.wide[side] and k == len(self.sides[side]) - 1
            columns.append(values[0] + (one_word(values[1]) if wide else values[1]))
        return jnp.concatenate(columns, axis=-1)

    def first_kernel(self, at_ref, *refs):
        place = 0
        for side, pieces in enumerate(self.sides):
            goes, stays = refs[2 * side - 4], refs[2 * side - 3]
            bit = at_ref[1 + side]
            for z in range(self.count):
                for which in range(2):
                    values = self.piece_values(refs[place:], side, z, 1 - bit, which, at_ref[0])
                    goes[z, which] = sent(values, self.wide[side])
                    stays[z, which] = self.piece_values(
                        refs[place:], side, z, bit, which, at_ref[0]
                    )
            place += 2 * len(pieces)

    def first(self):
        ins, in_specs, outs = [], [], []
        for side, pieces in enumerate(self.sides):
            for piece in pieces:
                ins += piece[:2]
                in_specs += [piece_spec(piece)] * 2
            shape = (self.count, 2, self.rows[side], self.columns[side])
            outs += [stacked(*shape, dtype=jnp.bfloat16), pltpu.VMEM(shape, jnp.float32)]
        return fold_call(self.first_kernel, 1, self.at, ins, in_specs, outs, [whole_block(o) for o in outs])

    def first_sent(self, parts):
        self.stays = parts[1::2]
        return [exchanged(part, "batch", 1 << side) for side, part in enumerate(parts[::2])]

    def second_kernel(self, at_ref, *refs):
        outs = refs[-4:]
        for side in range(2):
            stays, arrived = refs[2 * side], refs[2 * side + 1]
            bit = at_ref[2 - side]
            for z in range(self.count):
                for which, out in ((1 - bit, outs[2 * side]), (bit, outs[2 * side + 1])):
                    values = stays[z, which] + received(arrived[z, which], self.wide[side])
                    out[z] = sent(values, self.wide[side]) if out.dtype == jnp.bfloat16 else values

    def second(self, arrived):
        ins, outs = [], []
        for side in range(2):
            ins += [near_by(self.stays[side]), arrived[side]]
            shape = (self.count, self.rows[side], self.columns[side])
            outs += [stacked(*shape, dtype=jnp.bfloat16), pltpu.VMEM(shape, jnp.float32)]
        return fold_call(
            self.second_kernel, 1, self.at, ins, [whole_block(a) for a in ins], outs,
            [whole_block(out) for out in outs],
        )

    def second_sent(self, out):
        return [exchanged(out[0], "batch", 2), exchanged(out[2], "batch", 1)], [out[1], out[3]]

    def third_kernel(self, radix, at_ref, keep0, keep1, in0, in1, *outs):
        mine = at_ref[3] % radix
        for d, out in enumerate(outs):
            which = mine ^ d
            column = 0
            for side, (keep, arrived) in enumerate(((keep0, in0), (keep1, in1))):
                wide = self.wide[side]
                values = keep[which] + received(arrived[which], wide)
                width = values.shape[-1]
                out[0, :, column : column + width] = values if d == 0 else sent(values, wide)
                column += width

    def third(self, arrived, kept):
        radix = min(4, self.count)
        ins = [near_by(part) for part in kept] + arrived
        in_specs = [pl.BlockSpec((radix,) + a.shape[1:], lambda z, at: (z, 0, 0)) for a in ins]
        shape = (self.count // radix, self.rows[0], sum(self.columns))
        outs = [pltpu.VMEM(shape, jnp.float32)] + [stacked(*shape, dtype=jnp.bfloat16)] * (radix - 1)
        out_specs = [pl.BlockSpec((1,) + o.shape[1:], lambda z, at: (z, 0, 0)) for o in outs]
        return fold_call(
            functools.partial(self.third_kernel, radix), self.count // radix, self.at, ins, in_specs, outs, out_specs, True
        )

    def third_sent(self, out):
        return [exchanged(part, "batch", 4 * d) for d, part in enumerate(out) if d > 0]

    def total(self, kept, arrived, *earlier):
        radix = min(4, self.count)
        terms = [kept] + [after(part, *earlier) if earlier else part for part in arrived]
        total = None
        for term in terms:
            value = received(term, self.wide[1]) if term.dtype == jnp.bfloat16 else term
            total = value if total is None else total + value
        bit = 2 + radix.bit_length() - 1
        while total.shape[0] > 1:
            total = total.reshape((total.shape[0] // 2, 2) + total.shape[1:])
            upper = (lax.axis_index("batch") >> bit) & 1
            away = sent(lax.dynamic_index_in_dim(total, 1 - upper, 1, keepdims=False), False)
            total = lax.dynamic_index_in_dim(total, upper, 1, keepdims=False)
            total = total + exchanged(away, "batch", 1 << bit).astype(jnp.float32)
            bit += 1
        return total[0]


def attend_kernel(at, q_ref, k_ref, v_ref, context_ref, turned_ref, prob_ref, bias):
    half = pl.program_id(1)

    @pl.when(pl.program_id(0) == 0)
    def _():
        span = q_ref.shape[0]
        key = lax.broadcasted_iota(jnp.int32, (span, 1), 0) + half * span
        query = lax.broadcasted_iota(jnp.int32, (1, span), 1) + half * span
        bits = (2 * span).bit_length() - 1
        key_slot = (key * at[SLOT_COUNT]) >> bits
        query_slot = (query * at[SLOT_COUNT]) >> bits
        length = jnp.zeros((span, 1), jnp.int32)
        for slot in range(at.shape[0] - LENGTHS):
            length += jnp.where(key_slot == slot, at[LENGTHS + slot], 0)
        present = key - key_slot * bucket_of(at, 2 * span) < length
        code = jnp.where(present, key_slot, -1)
        bias[half] = jnp.where(code == query_slot, 0.0, NEGATIVE)

    rows, lanes = q_ref.shape
    size = lanes // 2
    first = lax.broadcasted_iota(jnp.int32, (rows, lanes), 1) < size
    keys = k_ref[...]
    none = jnp.zeros_like(keys)
    masked = (jnp.where(first, keys, none), jnp.where(first, none, keys))
    values = v_ref[...].T
    queries = q_ref[...] * jnp.bfloat16(1.0 / math.sqrt(size))
    products = [matmul(masked[h], queries, NT) for h in range(2)]
    probs = []
    for h in range(2):
        scores = products[h] + bias[half]
        weights = jnp.exp(scores - jnp.max(scores, axis=0, keepdims=True))
        probs.append(halved(weights * (1.0 / jnp.sum(weights, axis=0, keepdims=True))))
        prob_ref[0, 0, h] = probs[h]
    outs = [matmul(values[h * size : (h + 1) * size], probs[h]) for h in range(2)]
    context = jnp.concatenate(outs, axis=0)
    turned_ref[...] = halved(context)
    context_ref[...] = halved(context.T)


def natural(pairs, i, at):
    return ((i // (pairs // 2)) ^ at[0]) * (pairs // 2) + i % (pairs // 2)


def attend(at, triples):
    tokens, wide = triples.shape[1:]
    width = wide // 3 * 2
    rows, pairs = tokens // 2, width // LANES
    own = pairs // 2

    def part(p):
        return pl.BlockSpec((None, rows, LANES), lambda i, j, at: (i // own, j, p * own + i % own))

    return pl.pallas_call(
        attend_kernel,
        grid_spec=pltpu.PrefetchScalarGridSpec(
            num_scalar_prefetch=1,
            grid=(pairs, 2),
            in_specs=[
                part(0),
                part(1),
                part(2),
            ],
            out_specs=[
                pl.BlockSpec((rows, LANES), lambda i, j, at: (j, natural(pairs, i, at))),
                pl.BlockSpec((LANES, rows), lambda i, j, at: (natural(pairs, i, at), j)),
                pl.BlockSpec((1, 1, 2, rows, rows), lambda i, j, at: (i, j, 0, 0, 0)),
            ],
            scratch_shapes=[pltpu.VMEM((2, rows, rows), jnp.float32)],
        ),
        out_shape=[
            far_off(tokens, width),
            far_off(width, tokens),
            far_off(pairs, 2, 2, rows, rows),
        ],
        compiler_params=pltpu.CompilerParams(vmem_limit_bytes=14 << 20),
        cost_estimate=COST,
    )(at, *[far_away(triples)] * 3)


def attend_back_kernel(at, q_ref, k_ref, v_ref, context_ref, grad_ref, prob_ref, out_ref, sum_ref):
    rows, lanes = q_ref.shape
    size = lanes // 2
    scale = jnp.bfloat16(1.0 / math.sqrt(size))
    first = lax.broadcasted_iota(jnp.int32, (rows, lanes), 1) < size
    queries = q_ref[...] * scale
    keys = (k_ref[...] * scale).T
    values, grads = v_ref[...], grad_ref[...]
    none = jnp.zeros_like(values)
    masked = (jnp.where(first, values, none), jnp.where(first, none, values))
    products = (grads.astype(jnp.float32) * context_ref[...].astype(jnp.float32)).T
    dquery, dkey, dvalue = [], [], []
    for h in range(2):
        here = slice(h * size, (h + 1) * size)
        rowdot = jnp.sum(products[here], axis=0, keepdims=True)
        probs = prob_ref[0, 0, h]
        dprob = matmul(masked[h], grads, NT)
        dscore = halved(probs.astype(jnp.float32) * (dprob - rowdot))
        dkey.append(matmul(dscore, queries))
        dvalue.append(matmul(probs, grads))
        dquery.append(matmul(keys[here], dscore))
    dquery = jnp.concatenate(dquery, axis=0).T
    dkey = jnp.where(first, dkey[0], dkey[1])
    dvalue = jnp.where(first, dvalue[0], dvalue[1])
    pair = pl.program_id(2)
    quarter = out_ref.shape[2] // 3
    low = pl.multiple_of(pair * lanes, lanes)
    for p, part in enumerate((dquery, dkey, dvalue)):
        out_ref[0, :, pl.ds(p * quarter + low, lanes)] = halved(part)

    @pl.when((pl.program_id(1) == 0) & (pair == 0))
    def _():
        sum_ref[...] = jnp.zeros_like(sum_ref)

    sum_ref[0, 0, :, pl.ds(low, lanes)] += jnp.sum(dquery, axis=0, keepdims=True)
    sum_ref[0, 1, :, pl.ds(low, lanes)] += jnp.sum(dvalue, axis=0, keepdims=True)


def attend_back(at, triples, context, grad, probs):
    tokens, width = context.shape
    rows, pairs = tokens // 2, width // LANES
    own = pairs // 2

    def part(p):
        return pl.BlockSpec((None, rows, LANES), lambda r, j, i, at: (r, j, p * own + i))

    whole = pl.BlockSpec((rows, LANES), lambda r, j, i, at: (j, natural(pairs, r * own + i, at)))
    return pl.pallas_call(
        attend_back_kernel,
        grid_spec=pltpu.PrefetchScalarGridSpec(
            num_scalar_prefetch=1,
            grid=(2, 2, own),
            in_specs=[
                part(0),
                part(1),
                part(2),
                whole,
                whole,
                pl.BlockSpec((1, 1, 2, rows, rows), lambda r, j, i, at: (r * own + i, j, 0, 0, 0)),
            ],
            out_specs=[
                pl.BlockSpec((1, rows, triples.shape[2]), lambda r, j, i, at: (r, j, 0)),
                pl.BlockSpec((1, 2, 1, width // 2), lambda r, j, i, at: (r, 0, 0, 0)),
            ],
        ),
        out_shape=[pltpu.VMEM(triples.shape, jnp.bfloat16), stacked(2, 2, 1, width // 2)],
        compiler_params=pltpu.CompilerParams(vmem_limit_bytes=16 << 20),
        cost_estimate=LONG_COST,
    )(at, *[far_away(triples)] * 3, context, grad, probs)


def bucket_of(at, token_count):
    return jnp.where(at[SLOT_COUNT] == 2, token_count // 2, token_count // (at.shape[0] - LENGTHS))


def group_slot(at, group, token_count):
    slots = at.shape[0] - LENGTHS
    span = token_count // slots
    slot = (group * at[SLOT_COUNT]) // slots
    place = lax.broadcasted_iota(jnp.int32, (span, 1), 0) + group * span
    live = place - slot * bucket_of(at, token_count) < at[LENGTHS + slot]
    return slot, live.astype(jnp.float32)


def whole_block(array):
    return pl.BlockSpec(array.shape, lambda *_: (0,) * len(array.shape))


def kernel_call(kernel, grid, at, ins, in_specs, outs, out_specs, scratch=(), long=False, vmem=OTHER_VMEM):
    return pl.pallas_call(
        kernel,
        grid_spec=pltpu.PrefetchScalarGridSpec(
            num_scalar_prefetch=1, grid=grid, in_specs=in_specs, out_specs=out_specs,
            scratch_shapes=scratch,
        ),
        out_shape=outs,
        compiler_params=pltpu.CompilerParams(vmem_limit_bytes=vmem << 20),
        cost_estimate=LONG_COST if long else COST,
    )(at, *ins)


def entry_kernel(
    at, tokens, pos, weight, misc, hidden0, entry, triples, vectors, bias_lines, table, shift
):
    step = pl.program_id(0)
    rows, width = tokens.shape
    quarter = width // 2

    @pl.when(step == 0)
    def _():
        long = pos[...].astype(jnp.float32).T
        count = long.shape[0]
        span = 2 * count // (at.shape[0] - LENGTHS)
        short = jnp.concatenate([long[:span]] * (count // span), axis=0)
        table[...] = jnp.where(at[SLOT_COUNT] == 2, long, short)
        for core in range(2):
            lines = misc[core].astype(jnp.float32).T
            vectors[4 * core : 4 * core + 4] = lines[:4]
            bias_lines[2 * core : 2 * core + 2] = lines[4:6]
        shift[...] = jnp.zeros_like(shift)
        for other in range(2):
            here = pl.ds(pl.multiple_of((other ^ at[0]) * quarter, quarter), quarter)
            shift[other, :, :quarter] = vectors[BQ : BQ + 1, here]
            shift[other, :, 2 * quarter :] = vectors[BV : BV + 1, here]

    half_steps = pl.num_programs(0) // 2
    here = pl.ds(pl.multiple_of((step % half_steps) * rows, rows), rows)
    values = tokens[...].astype(jnp.float32) + table[here]
    hidden0[...] = values
    values = halved(values)
    entry[...] = values.T
    for other in range(2):
        triples[other] = halved(matmul(values, weight[other]) + shift[other])


def entered(at, tokens, pos, qkv, misc):
    token_count, width = tokens.shape
    triple = qkv.shape[2]
    outs = [
        far_off(token_count, width, dtype=jnp.float32),
        far_off(width, token_count),
        far_off(2, token_count, triple),
        stacked(8, width),
        stacked(4, width),
    ]
    return kernel_call(
        entry_kernel,
        (token_count // CHUNK,),
        at,
        [far_away(tokens), near_by(pos), near_by(qkv), near_by(misc)],
        tiles(tokens) + [HERE, HERE, HERE],
        outs,
        tiles(outs[0], outs[1])
        + [pl.BlockSpec((2, CHUNK, triple), lambda i, at: (0, i, 0))]
        + [whole_block(out) for out in outs[3:]],
        [
            pltpu.VMEM((token_count // 2, width), jnp.float32),
            pltpu.VMEM((2, 1, triple), jnp.float32),
        ],
    )


BQ, BV, BO, B2, G1, E1, G2, E2 = range(8)


def normal(values):
    center = values - jnp.mean(values, axis=-1, keepdims=True)
    inverse = lax.rsqrt(jnp.mean(center * center, axis=-1, keepdims=True) + EPS_NORM)
    return center * inverse, inverse


def held(array):
    return pl.BlockSpec(
        array.shape, lambda *_: (0,) * len(array.shape), pipeline_mode=pl.Buffered(buffer_count=1)
    )


def tiles(*arrays):
    return [
        pl.BlockSpec((CHUNK, a.shape[1]), lambda i, at: (i, 0))
        if a.shape[0] == arrays[0].shape[0]
        else pl.BlockSpec((a.shape[0], CHUNK), lambda i, at: (0, i))
        for a in arrays
    ]


def forward_kernel(
    at, hidden0, context, out_weight, vectors, up, up_bias, down,
    entry2, normed1, inverse1, active, slope, normed2, inverse2, block_out, pooled, units, acts,
):
    step = pl.program_id(0)
    rows, width = hidden0.shape
    token_count = rows * pl.num_programs(0)
    resid = hidden0[...] + matmul(context[...], out_weight[...]) + vectors[BO : BO + 1]
    normed, inverse = normal(resid)
    hidden1 = normed * vectors[G1 : G1 + 1] + vectors[E1 : E1 + 1]
    normed1[...], inverse1[...] = halved(normed), inverse
    entry = halved(hidden1)
    entry2[...] = entry.T
    half = up.shape[2]
    span = half // BLOCKS
    for other in range(2):
        for block in range(BLOCKS):
            here = slice(block * span, (block + 1) * span)
            there = slice(other * half + block * span, other * half + (block + 1) * span)
            values = matmul(entry, up[other, :, here]) + up_bias[other, :, here]
            cumulative = 0.5 + 0.5 * lax.erf(values * ROOT_HALF)
            acted = halved(values * cumulative)
            acts[:, there] = acted
            active[there] = acted.T
            density = jnp.exp(-0.5 * values * values) * (1.0 / ROOT_TWO_PI)
            slope[:, there] = halved(cumulative + values * density)
    total = hidden1 + vectors[B2 : B2 + 1] + matmul(acts[...], down[...])
    normed, inverse = normal(total)
    hidden2 = normed * vectors[G2 : G2 + 1] + vectors[E2 : E2 + 1]
    normed2[...], inverse2[...] = halved(normed), inverse
    block_out[...] = halved(hidden2)

    @pl.when(step == 0)
    def _():
        pooled[...] = jnp.zeros_like(pooled)

    slots = pooled.shape[0]
    span = token_count // slots
    for group in range(rows // span):
        slot, live = group_slot(at, step * (rows // span) + group, token_count)
        part = hidden2[group * span : (group + 1) * span] * live
        pooled[pl.ds(slot, 1)] += jnp.sum(part, axis=0, keepdims=True)

    @pl.when(step == pl.num_programs(0) - 1)
    def _():
        row = lax.broadcasted_iota(jnp.int32, (slots, LANES), 0)
        length = jnp.zeros((slots, LANES), jnp.int32)
        for slot in range(slots):
            length += jnp.where(row == slot, at[LENGTHS + slot], 0)
        mean = pooled[...] * (1.0 / jnp.maximum(length[:, :1], 1).astype(jnp.float32))
        pooled[...] = mean
        squares = jnp.sum(mean * mean, axis=-1, keepdims=True)
        units[:, :width] = halved(mean * lax.rsqrt(squares + EPS_NORM))
        first = lax.broadcasted_iota(jnp.int32, (slots, LANES), 1) == 0
        units[:, width:] = halved(jnp.where(first & (length > 0), 1.0, 0.0))


def forward(at, hidden0, context, out_weight, vectors, up, up_bias, down):
    token_count, width = hidden0.shape
    slots = at.shape[0] - LENGTHS
    hidden = 2 * up.shape[2]
    half = functools.partial(stacked, dtype=jnp.bfloat16)
    outs = [
        far_off(width, token_count),
        far_off(token_count, width),
        stacked(token_count, 1),
        pltpu.VMEM((hidden, token_count), jnp.bfloat16),
        pltpu.VMEM((token_count, hidden), jnp.bfloat16),
        far_off(token_count, width),
        stacked(token_count, 1),
        far_off(token_count, width),
        stacked(slots, width),
        half(slots, width + LANES),
    ]
    return kernel_call(
        forward_kernel,
        (token_count // CHUNK,),
        at,
        [far_away(hidden0), far_away(context), out_weight, vectors, near_by(up), up_bias, near_by(down)],
        tiles(hidden0, context)
        + [held(out_weight), held(vectors), HERE, held(up_bias), HERE],
        outs,
        tiles(hidden0, *outs[:8])[1:] + [whole_block(out) for out in outs[8:]],
        [pltpu.VMEM((CHUNK, hidden), jnp.bfloat16)],
        vmem=FORWARD_VMEM,
    )


def norm_back(grad, normed, inverse, gain):
    scaled = grad * gain
    inner = (
        scaled
        - jnp.mean(scaled, axis=-1, keepdims=True)
        - normed * jnp.mean(scaled * normed, axis=-1, keepdims=True)
    )
    return inner * inverse


def loss_kernel(
    at, units, others, pooled, normed2, inverse2, vectors,
    dresid, dresid_half, sums, dpool,
):
    slots, width = pooled.shape
    count = units.shape[0]
    step = pl.program_id(0)

    @pl.when(step == 0)
    def _():
        own, own_flags = units[:, :width], units[:, width:]
        other, other_flags = others[:, :width], others[:, width:]
        lane = lax.broadcasted_iota(jnp.int32, (slots, LANES), 1)
        one_hot = halved(jnp.where(lane == 0, 1.0, 0.0))
        own_row = matmul(one_hot, own_flags, NT)[:1] > 0
        other_row = matmul(one_hot, other_flags, NT)[:1] > 0

        def shares(lines, columns, live):
            logits = matmul(lines, columns, NT) * INV_TEMP
            logits = jnp.where(live, logits, NEGATIVE)
            weights = jnp.exp(logits - jnp.max(logits, axis=-1, keepdims=True))
            return weights / jnp.sum(weights, axis=-1, keepdims=True)

        row = lax.broadcasted_iota(jnp.int32, (slots, count), 0)
        column = lax.broadcasted_iota(jnp.int32, (slots, count), 1)
        target = jnp.where(row == column, 1.0, 0.0)
        row_live = own_flags[:slots, :1].astype(jnp.float32)
        dlogit = halved(LOSS_WEIGHT * (shares(own[:slots], other, other_row) - target) * row_live)
        near = shares(other, own, own_row)[:, :LANES]
        row = lax.broadcasted_iota(jnp.int32, (count, LANES), 0)
        column = lax.broadcasted_iota(jnp.int32, (count, LANES), 1)
        target = jnp.where(row == column, 1.0, 0.0)
        other_live = other_flags[:, :1].astype(jnp.float32)
        dnear = LOSS_WEIGHT * (near - target) * other_live
        dnear = halved(jnp.where(column < slots, dnear, 0.0))
        dunit = INV_TEMP * (matmul(dlogit, other) + matmul(dnear, other, TN)[:slots])
        mean = pooled[...]
        inverse = lax.rsqrt(jnp.sum(mean * mean, axis=-1, keepdims=True) + EPS_NORM)
        along = jnp.sum(mean * dunit, axis=-1, keepdims=True)
        grad = inverse * dunit - inverse * inverse * inverse * mean * along
        slot_row = lax.broadcasted_iota(jnp.int32, (slots, 1), 0)
        length = jnp.zeros((slots, 1), jnp.int32)
        for slot in range(slots):
            length += jnp.where(slot_row == slot, at[LENGTHS + slot], 0)
        dpool[...] = grad * (1.0 / jnp.maximum(length, 1).astype(jnp.float32))
        sums[...] = jnp.zeros_like(sums)

    gain = vectors[G2 : G2 + 1]
    token_count = normed2.shape[0] * pl.num_programs(0)
    span = token_count // slots
    groups = normed2.shape[0] // span
    for group in range(groups):
        here = pl.ds(group * span, span)
        slot, live = group_slot(at, step * groups + group, token_count)
        dhidden = dpool[pl.ds(slot, 1)] * live
        normed = normed2[here].astype(jnp.float32)
        values = norm_back(dhidden, normed, inverse2[here], gain)
        dresid[here] = values
        dresid_half[here] = halved(values)
        for k, terms in enumerate((values, dhidden * normed, dhidden)):
            sums[k : k + 1] += jnp.sum(terms, axis=0, keepdims=True)


def loss_back(at, units, others, pooled, normed2, inverse2, vectors):
    token_count, width = normed2.shape
    half = functools.partial(stacked, dtype=jnp.bfloat16)
    ins = [units, others, pooled, far_away(normed2), inverse2, vectors]
    outs = [
        far_off(token_count, width, dtype=jnp.float32),
        half(token_count, width),
        stacked(3, width),
    ]
    return kernel_call(
        loss_kernel,
        (token_count // CHUNK,),
        at,
        ins,
        [held(a) for a in ins[:3]] + tiles(*ins[3:5]) + [held(vectors)],
        outs,
        tiles(*outs[:2]) + [whole_block(outs[2])],
        [pltpu.VMEM(pooled.shape, jnp.float32)],
    )


def backward_kernel(
    at, dresid2, dresid2_half, slope, up, down, normed1, inverse1, vectors,
    dpre, dpre_sum, dresid, dresid_half, sums,
):
    @pl.when(pl.program_id(0) == 0)
    def _():
        dpre_sum[...] = jnp.zeros_like(dpre_sum)
        sums[...] = jnp.zeros_like(sums)

    half = up.shape[2]
    span = half // BLOCKS
    grad = dresid2_half[...]
    for block in range(2 * BLOCKS):
        here = slice(block * span, (block + 1) * span)
        dactive = matmul(grad, down[here], NT)
        values = dactive * slope[:, here].astype(jnp.float32)
        dpre_sum[:, here] += jnp.sum(values, axis=0, keepdims=True)
        dpre[:, here] = halved(values)
    dhidden = dresid2[...]
    for other in range(2):
        dhidden += matmul(dpre[:, other * half : (other + 1) * half], up[other], NT)
    normed = normed1[...].astype(jnp.float32)
    values = norm_back(dhidden, normed, inverse1[...], vectors[G1 : G1 + 1])
    dresid[...] = values
    rounded = halved(values)
    dresid_half[...] = rounded
    for k, terms in enumerate((values, dhidden * normed, dhidden)):
        sums[k : k + 1] += jnp.sum(terms, axis=0, keepdims=True)


def backward(at, dresid2, dresid2_half, slope, up, down, normed1, inverse1, vectors):
    token_count, width = dresid2.shape
    hidden = 2 * up.shape[2]
    half = functools.partial(stacked, dtype=jnp.bfloat16)
    outs = [
        pltpu.VMEM((token_count, hidden), jnp.bfloat16),
        stacked(1, hidden),
        far_off(token_count, width, dtype=jnp.float32),
        half(token_count, width),
        stacked(3, width),
    ]
    out_specs = tiles(outs[0], *outs[2:4])
    return kernel_call(
        backward_kernel,
        (token_count // CHUNK,),
        at,
        [far_away(dresid2), dresid2_half, near_by(slope), near_by(up), near_by(down), far_away(normed1), inverse1, vectors],
        tiles(dresid2, dresid2_half, slope) + [HERE, HERE] + tiles(normed1, inverse1)
        + [held(vectors)],
        outs,
        out_specs[:1] + [whole_block(outs[1])] + out_specs[1:] + [whole_block(outs[4])],
        vmem=BACKWARD_VMEM,
        long=True,
    )


def leave_kernel(
    at, dresid1, dtriples, qkv, dsums, sums1, sums2, dpre_sum, input_grad, last_own, last_away, total, turned,
):
    step = pl.program_id(0)
    rows = dresid1.shape[0]
    values = dresid1[...]
    for other in range(2):
        values = values + matmul(dtriples[other], qkv[other], NT)
    input_grad[...] = values
    half_steps = pl.num_programs(0) // 2
    here = pl.ds(pl.multiple_of((step % half_steps) * rows, rows), rows)

    @pl.when(step < half_steps)
    def _():
        total[here] = values

    @pl.when(step >= half_steps)
    def _():
        total[here] += values

    @pl.when(step == pl.num_programs(0) - 1)
    def _():
        count = total.shape[0]
        long = total[...]
        span = 2 * count // (at.shape[0] - LENGTHS)
        short = sum(long[k * span : (k + 1) * span] for k in range(count // span))
        short = jnp.concatenate([short, jnp.zeros((count - span, long.shape[1]), jnp.float32)], axis=0)
        columns = jnp.where(at[SLOT_COUNT] == 2, long, short).T
        left, right = columns[:, : count // 2], columns[:, count // 2 :]
        last_own[:, : count // 2] = jnp.where(at[0] == 0, left, right)
        last_away[:, : count // 2] = halved(jnp.where(at[0] == 0, right, left))
        width = long.shape[1]
        first = [jnp.concatenate([dsums[0, k], dsums[1, k]], axis=1) for k in range(2)]
        swapped = [jnp.concatenate([dsums[1, k], dsums[0, k]], axis=1) for k in range(2)]
        heads = [jnp.where(at[0] == 0, a, b) for a, b in zip(first, swapped)]
        vectors = [heads + [sums1[:1], sums2[:1]], [sums1[1:2], sums1[2:3], sums2[1:2], sums2[2:3]]]
        blank = jnp.zeros((LANES - 4, width), jnp.float32)
        vectors = [jnp.concatenate(rows + [blank], axis=0).T for rows in vectors]
        lane = lax.broadcasted_iota(jnp.int32, (width, LANES), 1)
        for other, (out, words) in enumerate(((last_own, False), (last_away, True))):
            row = dpre_sum[:, other * 2 * width : (other + 1) * 2 * width]
            turned[...] = jnp.broadcast_to(row, (LANES, 2 * width)).T
            lines = jnp.where(at[0] == other, vectors[0], vectors[1])
            for k in range(2):
                lines = jnp.where(lane == 4 + k, turned[pl.ds(k, width, 2)], lines)
            out[:, count // 2 :] = halved(two_words(lines)) if words else lines


def left(at, dresid1, dtriples, qkv, dsums, sums1, sums2, dpre_sum):
    token_count, width = dresid1.shape
    triple = qkv.shape[2]
    columns = token_count // 4 + LANES
    small = [dsums, sums1, sums2, dpre_sum]
    outs = [
        stacked(token_count, width),
        stacked(width, columns),
        stacked(width, columns, dtype=jnp.bfloat16),
    ]
    return kernel_call(
        leave_kernel,
        (token_count // CHUNK,),
        at,
        [far_away(dresid1), near_by(dtriples), qkv] + small,
        tiles(dresid1)
        + [pl.BlockSpec((2, CHUNK, triple), lambda i, at: (0, i, 0)), held(qkv)]
        + [held(a) for a in small],
        outs,
        tiles(outs[0]) + [whole_block(out) for out in outs[1:]],
        [
            pltpu.VMEM((token_count // 2, width), jnp.float32),
            pltpu.VMEM((2 * width, LANES), jnp.float32),
        ],
        long=True,
    )


def product_kernel(natural_order, at, left_ref, right_ref, own, away):
    values = left_ref[...]
    if len(right_ref.shape) == 3:
        first, second = matmul(values, right_ref[0]), matmul(values, right_ref[1])
    else:
        both = matmul(values, right_ref[...])
        first, second = both[:, : both.shape[1] // 2], both[:, both.shape[1] // 2 :]
    first, second = halved(first), halved(second)
    if natural_order:
        first, second = jnp.where(at[0] == 0, first, second), jnp.where(at[0] == 0, second, first)
    own[...], away[...] = first, second


def product(at, left_array, right_array, natural_order=False, near=None):
    rows, depth = left_array.shape
    columns = right_array.size // depth // 2
    tile = rows // 6 if rows > 1024 else rows // 3
    outs = [stacked(rows, columns, dtype=jnp.bfloat16)] * 2
    return kernel_call(
        functools.partial(product_kernel, natural_order),
        (rows // tile,),
        at,
        [near_by(left_array) if near == 0 else left_array, near_by(right_array) if near == 1 else right_array],
        [pl.BlockSpec((tile, depth), lambda i, at: (i, 0)), HERE if near == 1 else held(right_array)],
        outs,
        [pl.BlockSpec((tile, columns), lambda i, at: (i, 0))] * 2,
        long=True,
        vmem=PRODUCT_VMEM,
    )


def renew(grad, moment, weight, average, rate):
    moment_new = MOMENTUM * moment + grad
    weight_new = weight - rate * (grad + MOMENTUM * moment_new)
    average_new = AVERAGE * average + (1.0 - AVERAGE) * weight_new
    return (grad, moment_new, weight_new, average_new)


def finish_kernel(kept, first, second, third, out_grad, *refs):
    states, outs = refs[:9], refs[9:]
    quarter = out_grad.shape[1]
    total = kept[...]
    for part in (first, second, third):
        total = total + received(part[...], True)

    def write(at, grad, state, results, rate):
        for result, value in zip(results, renew(grad, *[ref[at] for ref in state], rate), strict=True):
            result[at] = value

    for k in range(4):
        grad = total[:, k * quarter : (k + 1) * quarter] if k < 3 else out_grad[...]
        write((k,), grad, states[:3], outs[:4], RATE)
    lines = total[:, -LANES:].T
    write((Ellipsis,), lines[:4], states[3:6], outs[4:8], RATE)
    write((Ellipsis,), total[:, 3 * quarter : -LANES], states[6:], outs[8:12], POS_RATE)
    rows = kept.shape[0]
    row = lax.broadcasted_iota(jnp.int32, (rows, 2 * rows), 0)
    column = lax.broadcasted_iota(jnp.int32, (rows, 2 * rows), 1)
    bias = jnp.zeros((8, 2 * rows), jnp.float32)
    for k in range(2):
        chosen = jnp.where(column == 2 * row + k, 1.0, 0.0)
        line = jnp.broadcast_to(lines[4 + k : 5 + k], (8, rows))
        bias = bias + jnp.dot(
            line, chosen, precision=lax.Precision.HIGHEST, preferred_element_type=jnp.float32
        )
    outs[12][...] = bias[:1]


def finished(kept, arrived, out_grad, attn_state, vector_state, pos_state):
    pos_state = tuple(part.T for part in pos_state)
    states = attn_state + vector_state + pos_state
    outs = [stacked(*state[0].shape) for state in (attn_state, vector_state, pos_state) for _ in range(4)]
    outs.append(stacked(1, 2 * kept.shape[0]))
    out = pl.pallas_call(
        finish_kernel,
        in_specs=[HERE] * (5 + len(states)),
        out_specs=[HERE] * len(outs),
        out_shape=outs,
        compiler_params=pltpu.CompilerParams(vmem_limit_bytes=20 << 20),
        cost_estimate=COST,
    )(kept, *arrived, out_grad, *states)
    return out[:4], out[4:8], [part.T for part in out[8:12]], out[12]


def local(
    tokens,
    lengths,
    attn_weight,
    attn_moment,
    attn_average,
    up_weight,
    up_moment,
    up_average,
    down_weight,
    down_moment,
    down_average,
    layer_vectors,
    vector_moment,
    vector_average,
    up_bias,
    bias_moment,
    bias_average,
    pos_table,
    pos_moment,
    pos_average,
):
    at = scalars(lengths[0, 0])
    stream = at[0]
    upper = stream == 1
    devices = lax.axis_size("batch")
    rows, hidden_half = up_weight.shape
    quarter = attn_weight.shape[2]
    width = 2 * quarter
    pos_half = pos_table.shape[0]
    slot_count = lengths.shape[2]

    misc = jnp.concatenate([layer_vectors.T, up_bias.reshape(rows, 2)], axis=1)
    misc = jnp.pad(misc, ((0, 0), (0, LANES - misc.shape[1])))
    entry_block = halved(
        jnp.concatenate([attn_weight[0], attn_weight[1], attn_weight[2], pos_table.T, misc], axis=1)
    )
    middle_block = halved(
        jnp.concatenate([up_weight, attn_weight[3], jnp.zeros((rows, LANES), jnp.float32)], axis=1)
    )
    triple = 3 * quarter
    pos_stop = triple + pos_half
    entry_gather = Gather(entry_block, width)
    entry_gather.far()
    down_both = lax.all_gather(
        after(halved(down_weight), entry_gather.blocks), ("stream", "batch"), axis=0, tiled=True
    )
    entry_gather.near((2, 1))
    middle_gather = Gather(
        after(middle_block, *entry_gather.sides), (hidden_half + quarter + LANES) // 2
    )
    middle_gather.far()
    entry_gather.near((1, 2), middle_gather.blocks)
    qkv_blocks, pos_blocks, misc_blocks = entry_gather.placed(
        at,
        (
            (0, triple, 0, "relative", 0, 0),
            (triple, pos_stop, 1, "", 0, pos_half),
            (pos_stop, pos_stop + LANES, 2, "stream", 0, 0),
        ),
        [
            pltpu.VMEM((2, devices, rows, triple), jnp.bfloat16),
            pltpu.VMEM((devices, rows, 2 * pos_half), jnp.bfloat16),
            pltpu.VMEM((2, devices, rows, LANES), jnp.bfloat16),
        ],
    )
    qkv = qkv_blocks.reshape(2, width, triple)
    pos_full = pos_blocks.reshape(width, 2 * pos_half)
    def own_first(pair):
        return jnp.where(upper, pair[::-1], pair)

    hidden0, entry, triples, vectors, bias_lines = entered(
        at, tokens[0], pos_full, qkv, misc_blocks.reshape(2, width, LANES)
    )
    biases = bias_lines.reshape(2, 2, width).transpose(0, 2, 1).reshape(2, 1, hidden_half)
    middle_gather.near((2, 1), triples)
    context_half, context_turned, probs = attend(after(at, *middle_gather.sides), triples)
    middle_gather.near((1, 2), context_half)
    up_blocks, out_blocks, down = middle_gather.placed(
        after(at, context_half),
        (
            (0, hidden_half, 0, "relative", 0, 0),
            (hidden_half, hidden_half + quarter, 1, "", 0, quarter),
        ),
        [
            pltpu.VMEM((2, devices, rows, hidden_half), jnp.bfloat16),
            stacked(devices, rows, width, dtype=jnp.bfloat16),
        ],
        down_both.reshape(2, 2 * hidden_half, quarter),
    )
    up = up_blocks.reshape(2, width, hidden_half)
    out_full = out_blocks.reshape(width, width)
    (entry2, normed1, inverse1, active, slope, normed2, inverse2, block_out, pooled, units) = forward(
        at, hidden0, context_half, out_full, vectors, up, own_first(biases), down
    )

    units = units[None]
    bit = 0
    while 1 << bit < devices:
        step = min(2, devices.bit_length() - 1 - bit)
        arrived = [exchanged(units, "batch", d << bit) for d in range(1, 1 << step)]
        units = jnp.concatenate([units] + arrived, axis=0)
        bit += step
    units = units.reshape(-1, units.shape[2])
    others = exchanged(units, "stream", 1)
    dresid2, dresid2_half, sums2 = loss_back(
        at, units, others, pooled, normed2, inverse2, vectors
    )

    def blocks(values):
        return values.reshape(devices // 4, 2, 2, values.shape[0] // devices, values.shape[1])

    down_own, down_away = product(at, active, dresid2_half, True, near=0)
    down_in = exchanged(down_away, "stream", 1)
    by_rows = down_weight.shape[0] % 32 == 0
    half_rows = down_weight.shape[0] // 2
    down_pair = (blocks(down_own), blocks(down_in))
    if by_rows:
        down_sides = [[down_pair + (half_rows, k, quarter, 0, True)] for k in range(2)]
    else:
        down_sides = [
            [down_pair + (2 * half_rows, 0, LANES, k, True) for k in ks] for ks in ((0, 1), (2,))
        ]
    down_fold = Fold(at, down_sides)
    down_parts = down_fold.first()
    down_first = down_fold.first_sent(down_parts)
    dpre, dpre_sum, dresid1, dresid1_half, sums1 = backward(
        after(at, *down_parts), dresid2, dresid2_half, slope, up, down, normed1, inverse1, vectors
    )
    down_fold.at = after(at, dresid1_half, *down_first)
    down_parts = down_fold.second(down_first)
    down_second, down_kept = down_fold.second_sent(down_parts)
    up_own, up_away = product(after(at, *down_parts), entry2, dpre, near=1)
    up_in = exchanged(up_away, "stream", 1)
    out_own, out_away = product(
        after(at, up_away, *down_second), context_turned, dresid1_half, True
    )
    out_in = exchanged(out_away, "stream", 1)
    down_fold.at = after(at, out_own, *down_second)
    down_last = down_fold.third(down_second, down_kept)
    down_third = down_fold.third_sent(down_last)
    third = hidden_half // 3
    up_pair = (blocks(up_own), blocks(up_in))
    out_pair = (blocks(out_own), blocks(out_in))
    middle_fold = Fold(
        after(at, *down_last),
        [
            [up_pair + (rows, 0, third, 0, False), up_pair + (rows, 0, third, 1, False)],
            [up_pair + (rows, 0, third, 2, False), out_pair + (rows, 0, quarter, 0, False)],
        ],
    )
    middle_parts = middle_fold.first()
    middle_first = middle_fold.first_sent(middle_parts)
    dcontext_half = halved(matmul(after(dresid1_half, *middle_parts), out_full, NT))
    dtriples, dsums = attend_back(at, triples, context_half, dcontext_half, probs)
    qkv_own, qkv_away = product(at, entry, dtriples, near=1)
    qkv_in = exchanged(qkv_away, "stream", 1)
    middle_fold.at = after(at, qkv_away, *middle_first)
    middle_parts = middle_fold.second(middle_first)
    middle_second, middle_kept = middle_fold.second_sent(middle_parts)
    input_grad, last_own, last_away = left(
        after(at, qkv_away, *middle_parts, *down_third), dresid1, dtriples, qkv, dsums, sums1, sums2, dpre_sum
    )
    last_in = exchanged(last_away, "stream", 1)
    qkv_pair = (blocks(qkv_own), blocks(qkv_in))
    last_pair = (blocks(last_own), blocks(last_in))
    entry_fold = Fold(
        at,
        [
            [qkv_pair + (rows, 0, quarter, 0, False), qkv_pair + (rows, 0, quarter, 1, False)],
            [
                qkv_pair + (rows, 0, quarter, 2, False),
                last_pair + (rows, 0, pos_half, 0, False),
                last_pair + (rows, 0, LANES, pos_half // LANES, False),
            ],
        ],
        wide=True,
    )
    entry_parts = entry_fold.first()
    entry_first = entry_fold.first_sent(entry_parts)
    middle_fold.at = after(at, *entry_parts, *middle_second)
    middle_parts = middle_fold.third(middle_second, middle_kept)
    entry_fold.at = after(at, *middle_parts)
    entry_parts = entry_fold.second(entry_first)
    middle_third = middle_fold.third_sent(middle_parts)
    middle_sum = middle_fold.total(middle_parts[0], middle_third, *entry_parts)
    down_sum = down_fold.total(down_last[0], down_third, *entry_parts)
    entry_second, entry_kept = entry_fold.second_sent(entry_parts)
    entry_parts = entry_fold.third(entry_second, entry_kept)
    vector_moment, vector_average = (
        after(part, *entry_parts) for part in (vector_moment, vector_average)
    )
    entry_third = entry_fold.third_sent(entry_parts)

    down_grad = down_sum
    if by_rows:
        down_grad = jnp.concatenate([down_sum[:, :quarter], down_sum[:, quarter:]], axis=0)
    up_all = renew(middle_sum[:, :hidden_half], up_moment, up_weight, up_average, RATE)
    down_all = renew(down_grad, down_moment, down_weight, down_average, RATE)
    out_grad = middle_sum[:, hidden_half : hidden_half + quarter]
    attn_state = (attn_moment, attn_weight, attn_average)
    vector_state = (vector_moment, layer_vectors, vector_average)
    pos_state = (pos_moment, pos_table, pos_average)
    if rows % 16 == 0:
        attn_all, vector_all, pos_all, bias_grad = finished(
            entry_parts[0][0], [part[0] for part in entry_third], out_grad, attn_state, vector_state, pos_state
        )
        bias_grad = bias_grad.reshape(-1)
    else:
        entry_sum = entry_fold.total(entry_parts[0], entry_third)
        attn_grad = jnp.stack(
            [entry_sum[:, k * quarter : (k + 1) * quarter] for k in range(3)] + [out_grad]
        )
        attn_all = renew(attn_grad, *attn_state, RATE)
        vector_all = renew(entry_sum[:, pos_stop : pos_stop + 4].T, *vector_state, RATE)
        pos_all = renew(entry_sum[:, triple:pos_stop].T, *pos_state, POS_RATE)
        bias_grad = entry_sum[:, pos_stop + 4 : pos_stop + 6].reshape(-1)
    bias_all = renew(bias_grad, bias_moment, up_bias, bias_average, RATE)
    return (
        block_out[None],
        input_grad[None],
        *attn_all,
        *up_all,
        *down_all,
        *vector_all,
        *bias_all,
        *pos_all,
    )


def solution(mesh):
    tokens_at, weight_at = P("stream", "batch", None), P("batch", "stream")
    attn_at, rows_at, bias_at = P(None, "batch", "stream"), P("stream", "batch"), P(("stream", "batch"))
    kinds = (attn_at, weight_at, weight_at, rows_at, bias_at, rows_at)
    in_specs = (tokens_at, tokens_at) + tuple(kind for kind in kinds for _ in range(3))
    out_specs = (tokens_at, tokens_at) + tuple(kind for kind in kinds for _ in range(4))
    return jax.shard_map(local, mesh=mesh, in_specs=in_specs, out_specs=out_specs, check_vma=False)
```

```python
import functools
import math

import jax
import jax.numpy as jnp
from jax import lax
from jax.experimental import pallas as pl
from jax.experimental.pallas import tpu as pltpu
from jax.sharding import PartitionSpec as P

HEADS = 12


EPS_NORM = 1e-06
INV_TEMP = 100.0
LOSS_WEIGHT = 256.0
MOMENTUM = 0.5
AVERAGE = 0.5
RATE = 0.0001
POS_RATE = 0.01
NEGATIVE = -1e30
ROOT_HALF = 0.7071067811865476
ROOT_TWO_PI = 2.5066282746310002
LANES = 128
SLOT_COUNT, LENGTHS = 4, 5
CHUNK, BLOCKS = 256, 3
COST = pl.CostEstimate(flops=1000, bytes_accessed=1000, transcendentals=0)
LONG_COST = pl.CostEstimate(flops=10**12, bytes_accessed=10**9, transcendentals=0)
ANYWHERE = pl.BlockSpec(memory_space=pl.ANY)
HERE = pl.BlockSpec(memory_space=pltpu.VMEM)
FORWARD_VMEM, BACKWARD_VMEM, PRODUCT_VMEM, OTHER_VMEM = 22, 17, 12, 20
NN = (((1,), (0,)), ((), ()))
NT = (((1,), (1,)), ((), ()))
TN = (((0,), (0,)), ((), ()))


def halved(values):
    return values.astype(jnp.bfloat16)


def matmul(left, right, dims=NN):
    return lax.dot_general(left, right, dims, preferred_element_type=jnp.float32)


def stacked(*shape, dtype=jnp.float32):
    return jax.ShapeDtypeStruct(shape, dtype)


def far_off(*shape, dtype=jnp.bfloat16):
    return pltpu.HBM(shape, dtype)


def after(value, *earlier):
    return lax.optimization_barrier((value, earlier))[0]


def exchanged(block, axis, mask):
    count = lax.axis_size(axis)
    return lax.ppermute(block, axis, [(place, place ^ mask) for place in range(count)])


def scalars(lengths_row):
    batch = lax.axis_index("batch")
    places = [lax.axis_index("stream"), batch & 1, (batch >> 1) & 1, batch >> 2]
    counted = jnp.sum((lengths_row > 0).astype(jnp.int32))
    return jnp.concatenate([jnp.stack(places + [counted]), lengths_row]).astype(jnp.int32)


class Gather:
    def __init__(self, block, cut):
        self.cut = cut
        self.bits = lax.axis_size("batch").bit_length() - 1
        self.blocks, self.masks = block[None], [0]

    def far(self, *earlier):
        bit = self.bits
        while bit > 2:
            step = min(2, bit - 2)
            bit -= step
            offsets = [d << bit for d in range(1 << step)]
            arrived = [exchanged(self.blocks, "batch", offset) for offset in offsets[1:]]
            own = after(self.blocks, *earlier) if earlier else self.blocks
            self.blocks = jnp.concatenate([own] + arrived, axis=0)
            self.masks = [offset | mask for offset in offsets for mask in self.masks]
        self.sides = [self.blocks[:, :, : self.cut], self.blocks[:, :, self.cut :]]
        self.masks = [self.masks, self.masks]

    def near(self, flips, *earlier):
        for side, flip in enumerate(flips):
            part = self.sides[side]
            own = after(part, *earlier) if earlier else part
            self.sides[side] = jnp.concatenate([own, exchanged(part, "batch", flip)], axis=0)
            self.masks[side] = self.masks[side] + [flip | mask for mask in self.masks[side]]

    def placed(self, at, pieces, shapes, down=None):
        sources, moves = [], []
        for other in range(2):
            for side, part in enumerate(self.sides):
                sources.append(exchanged(part, "stream", 1) if other else part)
                base = self.cut * side
                for start, stop, target, lead, offset, span in pieces:
                    low, high = max(start, base), min(stop, base + part.shape[2])
                    if low >= high:
                        continue
                    for entry, mask in enumerate(self.masks[side]):
                        moves.append(
                            (len(sources) - 1, entry, mask, (low - base, high - base), target, lead,
                             other, offset + low - start, span)
                        )
        return placed(at, sources, moves, shapes, down)


def far_away(array):
    return pltpu.with_memory_space_constraint(array, pltpu.HBM)


def near_by(array):
    return pltpu.with_memory_space_constraint(array, pltpu.VMEM)


def place_kernel(moves, count, with_down, at_ref, *refs):
    sources, rest = refs[:count], refs[count:]
    stream = at_ref[0]
    copies = []
    if with_down:
        down, targets, down_held, sems = rest[0], rest[1:-2], rest[-2], rest[-1]
        half, quarter = down.shape[1] // 2, down.shape[2]
        for other in range(2):
            start = pl.multiple_of((other ^ stream) * half, half)
            for k in range(2):
                copies.append(
                    pltpu.make_async_copy(
                        down.at[k, pl.ds(start, half)],
                        down_held.at[pl.ds(other * half, half), pl.ds(k * quarter, quarter)],
                        sems.at[2 * other + k],
                    )
                )
        for copy in copies:
            copy.start()
    else:
        targets = rest
    batch = at_ref[1] + 2 * at_ref[2] + 4 * at_ref[3]
    for source, entry, mask, columns, target, lead, other, start, span in moves:
        core = stream ^ other
        low = pl.multiple_of(start + core * span, LANES) if span else start
        at = (batch ^ mask, slice(None), pl.ds(low, columns[1] - columns[0]))
        if lead == "relative":
            at = (other,) + at
        elif lead == "stream":
            at = (core,) + at
        targets[target][at] = sources[source][entry, :, columns[0] : columns[1]]
    for copy in copies:
        copy.wait()


def placed(at, sources, moves, shapes, down=None):
    held_here = pl.BlockSpec(memory_space=pltpu.VMEM)
    ins, in_specs, out_specs = list(sources), [held_here] * len(sources), [held_here] * len(shapes)
    scratch = []
    if down is not None:
        ins.append(far_away(down))
        in_specs.append(ANYWHERE)
        shapes = list(shapes) + [pltpu.VMEM((down.shape[1], 2 * down.shape[2]), down.dtype)]
        out_specs.append(held_here)
        scratch.append(pltpu.SemaphoreType.DMA((4,)))
    return pl.pallas_call(
        functools.partial(place_kernel, moves, len(sources), down is not None),
        in_specs=[pl.BlockSpec(memory_space=pltpu.SMEM)] + in_specs,
        out_specs=out_specs,
        out_shape=shapes,
        scratch_shapes=scratch,
        compiler_params=pltpu.CompilerParams(vmem_limit_bytes=24 << 20),
        cost_estimate=COST,
    )(at, *ins)


def two_words(values):
    half = values.shape[-1] // 2
    coarse = values.astype(jnp.bfloat16).astype(jnp.float32)
    lane = lax.broadcasted_iota(jnp.int32, values.shape, values.ndim - 1)
    rest = jnp.concatenate([(values - coarse)[..., half:], (values - coarse)[..., :half]], axis=-1)
    return jnp.where(lane < half, coarse, rest)


def one_word(block):
    half = block.shape[-1] // 2
    return block + jnp.concatenate([block[..., half:], block[..., :half]], axis=-1)


def received(block, wide):
    values = block.astype(jnp.float32)
    if not wide:
        return values
    return jnp.concatenate(
        [values[..., :-LANES], one_word(values[..., -LANES:])], axis=-1
    )


def sent(values, wide):
    if not wide:
        return halved(values)
    return jnp.concatenate(
        [halved(values[..., :-LANES]), halved(two_words(values[..., -LANES:]))], axis=-1
    )


def piece_spec(piece):
    array, _, rows, row_at, columns, column_at, _ = piece
    return pl.BlockSpec(
        (array.shape[0], 2, 2, rows, columns),
        lambda _, at: (0, 0, 0, row_at, column_at),
        pipeline_mode=pl.Buffered(buffer_count=1),
    )


def fold_call(kernel, count, at, ins, in_specs, outs, out_specs, long=False):
    size = sum(math.prod(o.shape) for o in outs) * 8
    return pl.pallas_call(
        kernel,
        grid_spec=pltpu.PrefetchScalarGridSpec(
            num_scalar_prefetch=1, grid=(count,), in_specs=in_specs, out_specs=out_specs
        ),
        out_shape=outs,
        compiler_params=pltpu.CompilerParams(vmem_limit_bytes=17 << 20),
        cost_estimate=LONG_COST if long else COST,
    )(at, *ins)


class Fold:
    def __init__(self, at, sides, wide=False):
        self.at, self.sides, self.wide = at, sides, (False, wide)
        self.count = sides[0][0][0].shape[0]
        self.rows = [side[0][2] for side in sides]
        self.columns = [sum(piece[4] for piece in side) for side in sides]

    def piece_values(self, refs, side, z, bit, which, core):
        columns = []
        for k, piece in enumerate(self.sides[side]):
            values = []
            for turn, ref in ((core, refs[2 * k]), (1 - core, refs[2 * k + 1])):
                place = z ^ (turn * (self.count // 2)) if piece[6] else z
                entry = ref[place, which, bit] if side == 0 else ref[place, bit, which]
                values.append(entry.astype(jnp.float32))
            wide = self.wide[side] and k == len(self.sides[side]) - 1
            columns.append(values[0] + (one_word(values[1]) if wide else values[1]))
        return jnp.concatenate(columns, axis=-1)

    def first_kernel(self, at_ref, *refs):
        place = 0
        for side, pieces in enumerate(self.sides):
            goes, stays = refs[2 * side - 4], refs[2 * side - 3]
            bit = at_ref[1 + side]
            for z in range(self.count):
                for which in range(2):
                    values = self.piece_values(refs[place:], side, z, 1 - bit, which, at_ref[0])
                    goes[z, which] = sent(values, self.wide[side])
                    stays[z, which] = self.piece_values(
                        refs[place:], side, z, bit, which, at_ref[0]
                    )
            place += 2 * len(pieces)

    def first(self):
        ins, in_specs, outs = [], [], []
        for side, pieces in enumerate(self.sides):
            for piece in pieces:
                ins += piece[:2]
                in_specs += [piece_spec(piece)] * 2
            shape = (self.count, 2, self.rows[side], self.columns[side])
            outs += [stacked(*shape, dtype=jnp.bfloat16), pltpu.VMEM(shape, jnp.float32)]
        return fold_call(self.first_kernel, 1, self.at, ins, in_specs, outs, [whole_block(o) for o in outs])

    def first_sent(self, parts):
        self.stays = parts[1::2]
        return [exchanged(part, "batch", 1 << side) for side, part in enumerate(parts[::2])]

    def second_kernel(self, at_ref, *refs):
        outs = refs[-4:]
        for side in range(2):
            stays, arrived = refs[2 * side], refs[2 * side + 1]
            bit = at_ref[2 - side]
            for z in range(self.count):
                for which, out in ((1 - bit, outs[2 * side]), (bit, outs[2 * side + 1])):
                    values = stays[z, which] + received(arrived[z, which], self.wide[side])
                    out[z] = sent(values, self.wide[side]) if out.dtype == jnp.bfloat16 else values

    def second(self, arrived):
        ins, outs = [], []
        for side in range(2):
            ins += [near_by(self.stays[side]), arrived[side]]
            shape = (self.count, self.rows[side], self.columns[side])
            outs += [stacked(*shape, dtype=jnp.bfloat16), pltpu.VMEM(shape, jnp.float32)]
        return fold_call(
            self.second_kernel, 1, self.at, ins, [whole_block(a) for a in ins], outs,
            [whole_block(out) for out in outs],
        )

    def second_sent(self, out):
        return [exchanged(out[0], "batch", 2), exchanged(out[2], "batch", 1)], [out[1], out[3]]

    def third_kernel(self, radix, at_ref, keep0, keep1, in0, in1, *outs):
        mine = at_ref[3] % radix
        for d, out in enumerate(outs):
            which = mine ^ d
            column = 0
            for side, (keep, arrived) in enumerate(((keep0, in0), (keep1, in1))):
                wide = self.wide[side]
                values = keep[which] + received(arrived[which], wide)
                width = values.shape[-1]
                out[0, :, column : column + width] = values if d == 0 else sent(values, wide)
                column += width

    def third(self, arrived, kept):
        radix = min(4, self.count)
        ins = [near_by(part) for part in kept] + arrived
        in_specs = [pl.BlockSpec((radix,) + a.shape[1:], lambda z, at: (z, 0, 0)) for a in ins]
        shape = (self.count // radix, self.rows[0], sum(self.columns))
        outs = [pltpu.VMEM(shape, jnp.float32)] + [stacked(*shape, dtype=jnp.bfloat16)] * (radix - 1)
        out_specs = [pl.BlockSpec((1,) + o.shape[1:], lambda z, at: (z, 0, 0)) for o in outs]
        return fold_call(
            functools.partial(self.third_kernel, radix), self.count // radix, self.at, ins, in_specs, outs, out_specs, True
        )

    def third_sent(self, out):
        return [exchanged(part, "batch", 4 * d) for d, part in enumerate(out) if d > 0]

    def total(self, kept, arrived, *earlier):
        radix = min(4, self.count)
        terms = [kept] + [after(part, *earlier) if earlier else part for part in arrived]
        total = None
        for term in terms:
            value = received(term, self.wide[1]) if term.dtype == jnp.bfloat16 else term
            total = value if total is None else total + value
        bit = 2 + radix.bit_length() - 1
        while total.shape[0] > 1:
            total = total.reshape((total.shape[0] // 2, 2) + total.shape[1:])
            upper = (lax.axis_index("batch") >> bit) & 1
            away = sent(lax.dynamic_index_in_dim(total, 1 - upper, 1, keepdims=False), False)
            total = lax.dynamic_index_in_dim(total, upper, 1, keepdims=False)
            total = total + exchanged(away, "batch", 1 << bit).astype(jnp.float32)
            bit += 1
        return total[0]


def attend_kernel(at, q_ref, k_ref, v_ref, context_ref, turned_ref, prob_ref, bias):
    half = pl.program_id(1)

    @pl.when(pl.program_id(0) == 0)
    def _():
        span = q_ref.shape[0]
        key = lax.broadcasted_iota(jnp.int32, (span, 1), 0) + half * span
        query = lax.broadcasted_iota(jnp.int32, (1, span), 1) + half * span
        bits = (2 * span).bit_length() - 1
        key_slot = (key * at[SLOT_COUNT]) >> bits
        query_slot = (query * at[SLOT_COUNT]) >> bits
        length = jnp.zeros((span, 1), jnp.int32)
        for slot in range(at.shape[0] - LENGTHS):
            length += jnp.where(key_slot == slot, at[LENGTHS + slot], 0)
        present = key - key_slot * bucket_of(at, 2 * span) < length
        code = jnp.where(present, key_slot, -1)
        bias[half] = jnp.where(code == query_slot, 0.0, NEGATIVE)

    rows, lanes = q_ref.shape
    size = lanes // 2
    first = lax.broadcasted_iota(jnp.int32, (rows, lanes), 1) < size
    keys = k_ref[...]
    none = jnp.zeros_like(keys)
    masked = (jnp.where(first, keys, none), jnp.where(first, none, keys))
    values = v_ref[...].T
    queries = q_ref[...] * jnp.bfloat16(1.0 / math.sqrt(size))
    products = [matmul(masked[h], queries, NT) for h in range(2)]
    probs = []
    for h in range(2):
        scores = products[h] + bias[half]
        weights = jnp.exp(scores - jnp.max(scores, axis=0, keepdims=True))
        probs.append(halved(weights * (1.0 / jnp.sum(weights, axis=0, keepdims=True))))
        prob_ref[0, 0, h] = probs[h]
    outs = [matmul(values[h * size : (h + 1) * size], probs[h]) for h in range(2)]
    context = jnp.concatenate(outs, axis=0)
    turned_ref[...] = halved(context)
    context_ref[...] = halved(context.T)


def natural(pairs, i, at):
    return ((i // (pairs // 2)) ^ at[0]) * (pairs // 2) + i % (pairs // 2)


def attend(at, triples):
    tokens, wide = triples.shape[1:]
    width = wide // 3 * 2
    rows, pairs = tokens // 2, width // LANES
    own = pairs // 2

    def part(p):
        return pl.BlockSpec((None, rows, LANES), lambda i, j, at: (i // own, j, p * own + i % own))

    return pl.pallas_call(
        attend_kernel,
        grid_spec=pltpu.PrefetchScalarGridSpec(
            num_scalar_prefetch=1,
            grid=(pairs, 2),
            in_specs=[
                part(0),
                part(1),
                part(2),
            ],
            out_specs=[
                pl.BlockSpec((rows, LANES), lambda i, j, at: (j, natural(pairs, i, at))),
                pl.BlockSpec((LANES, rows), lambda i, j, at: (natural(pairs, i, at), j)),
                pl.BlockSpec((1, 1, 2, rows, rows), lambda i, j, at: (i, j, 0, 0, 0)),
            ],
            scratch_shapes=[pltpu.VMEM((2, rows, rows), jnp.float32)],
        ),
        out_shape=[
            far_off(tokens, width),
            far_off(width, tokens),
            far_off(pairs, 2, 2, rows, rows),
        ],
        compiler_params=pltpu.CompilerParams(vmem_limit_bytes=14 << 20),
        cost_estimate=COST,
    )(at, *[far_away(triples)] * 3)


def attend_back_kernel(at, q_ref, k_ref, v_ref, context_ref, grad_ref, prob_ref, out_ref, sum_ref):
    rows, lanes = q_ref.shape
    size = lanes // 2
    scale = jnp.bfloat16(1.0 / math.sqrt(size))
    first = lax.broadcasted_iota(jnp.int32, (rows, lanes), 1) < size
    queries = q_ref[...] * scale
    keys = (k_ref[...] * scale).T
    values, grads = v_ref[...], grad_ref[...]
    none = jnp.zeros_like(values)
    masked = (jnp.where(first, values, none), jnp.where(first, none, values))
    products = (grads.astype(jnp.float32) * context_ref[...].astype(jnp.float32)).T
    dquery, dkey, dvalue = [], [], []
    for h in range(2):
        here = slice(h * size, (h + 1) * size)
        rowdot = jnp.sum(products[here], axis=0, keepdims=True)
        probs = prob_ref[0, 0, h]
        dprob = matmul(masked[h], grads, NT)
        dscore = halved(probs.astype(jnp.float32) * (dprob - rowdot))
        dkey.append(matmul(dscore, queries))
        dvalue.append(matmul(probs, grads))
        dquery.append(matmul(keys[here], dscore))
    dquery = jnp.concatenate(dquery, axis=0).T
    dkey = jnp.where(first, dkey[0], dkey[1])
    dvalue = jnp.where(first, dvalue[0], dvalue[1])
    pair = pl.program_id(2)
    quarter = out_ref.shape[2] // 3
    low = pl.multiple_of(pair * lanes, lanes)
    for p, part in enumerate((dquery, dkey, dvalue)):
        out_ref[0, :, pl.ds(p * quarter + low, lanes)] = halved(part)

    @pl.when((pl.program_id(1) == 0) & (pair == 0))
    def _():
        sum_ref[...] = jnp.zeros_like(sum_ref)

    sum_ref[0, 0, :, pl.ds(low, lanes)] += jnp.sum(dquery, axis=0, keepdims=True)
    sum_ref[0, 1, :, pl.ds(low, lanes)] += jnp.sum(dvalue, axis=0, keepdims=True)


def attend_back(at, triples, context, grad, probs):
    tokens, width = context.shape
    rows, pairs = tokens // 2, width // LANES
    own = pairs // 2

    def part(p):
        return pl.BlockSpec((None, rows, LANES), lambda r, j, i, at: (r, j, p * own + i))

    whole = pl.BlockSpec((rows, LANES), lambda r, j, i, at: (j, natural(pairs, r * own + i, at)))
    return pl.pallas_call(
        attend_back_kernel,
        grid_spec=pltpu.PrefetchScalarGridSpec(
            num_scalar_prefetch=1,
            grid=(2, 2, own),
            in_specs=[
                part(0),
                part(1),
                part(2),
                whole,
                whole,
                pl.BlockSpec((1, 1, 2, rows, rows), lambda r, j, i, at: (r * own + i, j, 0, 0, 0)),
            ],
            out_specs=[
                pl.BlockSpec((1, rows, triples.shape[2]), lambda r, j, i, at: (r, j, 0)),
                pl.BlockSpec((1, 2, 1, width // 2), lambda r, j, i, at: (r, 0, 0, 0)),
            ],
        ),
        out_shape=[pltpu.VMEM(triples.shape, jnp.bfloat16), stacked(2, 2, 1, width // 2)],
        compiler_params=pltpu.CompilerParams(vmem_limit_bytes=16 << 20),
        cost_estimate=LONG_COST,
    )(at, *[far_away(triples)] * 3, context, grad, probs)


def bucket_of(at, token_count):
    return jnp.where(at[SLOT_COUNT] == 2, token_count // 2, token_count // (at.shape[0] - LENGTHS))


def group_slot(at, group, token_count):
    slots = at.shape[0] - LENGTHS
    span = token_count // slots
    slot = (group * at[SLOT_COUNT]) // slots
    place = lax.broadcasted_iota(jnp.int32, (span, 1), 0) + group * span
    live = place - slot * bucket_of(at, token_count) < at[LENGTHS + slot]
    return slot, live.astype(jnp.float32)


def whole_block(array):
    return pl.BlockSpec(array.shape, lambda *_: (0,) * len(array.shape))


def kernel_call(kernel, grid, at, ins, in_specs, outs, out_specs, scratch=(), long=False, vmem=OTHER_VMEM):
    return pl.pallas_call(
        kernel,
        grid_spec=pltpu.PrefetchScalarGridSpec(
            num_scalar_prefetch=1, grid=grid, in_specs=in_specs, out_specs=out_specs,
            scratch_shapes=scratch,
        ),
        out_shape=outs,
        compiler_params=pltpu.CompilerParams(vmem_limit_bytes=vmem << 20),
        cost_estimate=LONG_COST if long else COST,
    )(at, *ins)


def entry_kernel(
    at, tokens, pos, weight, misc, hidden0, entry, triples, vectors, bias_lines, table, shift
):
    step = pl.program_id(0)
    rows, width = tokens.shape
    quarter = width // 2

    @pl.when(step == 0)
    def _():
        long = pos[...].astype(jnp.float32).T
        count = long.shape[0]
        span = 2 * count // (at.shape[0] - LENGTHS)
        short = jnp.concatenate([long[:span]] * (count // span), axis=0)
        table[...] = jnp.where(at[SLOT_COUNT] == 2, long, short)
        for core in range(2):
            lines = misc[core].astype(jnp.float32).T
            vectors[4 * core : 4 * core + 4] = lines[:4]
            bias_lines[2 * core : 2 * core + 2] = lines[4:6]
        shift[...] = jnp.zeros_like(shift)
        for other in range(2):
            here = pl.ds(pl.multiple_of((other ^ at[0]) * quarter, quarter), quarter)
            shift[other, :, :quarter] = vectors[BQ : BQ + 1, here]
            shift[other, :, 2 * quarter :] = vectors[BV : BV + 1, here]

    half_steps = pl.num_programs(0) // 2
    here = pl.ds(pl.multiple_of((step % half_steps) * rows, rows), rows)
    values = tokens[...].astype(jnp.float32) + table[here]
    hidden0[...] = values
    values = halved(values)
    entry[...] = values.T
    for other in range(2):
        triples[other] = halved(matmul(values, weight[other]) + shift[other])


def entered(at, tokens, pos, qkv, misc):
    token_count, width = tokens.shape
    triple = qkv.shape[2]
    outs = [
        far_off(token_count, width, dtype=jnp.float32),
        far_off(width, token_count),
        far_off(2, token_count, triple),
        stacked(8, width),
        stacked(4, width),
    ]
    return kernel_call(
        entry_kernel,
        (token_count // CHUNK,),
        at,
        [far_away(tokens), near_by(pos), near_by(qkv), near_by(misc)],
        tiles(tokens) + [HERE, HERE, HERE],
        outs,
        tiles(outs[0], outs[1])
        + [pl.BlockSpec((2, CHUNK, triple), lambda i, at: (0, i, 0))]
        + [whole_block(out) for out in outs[3:]],
        [
            pltpu.VMEM((token_count // 2, width), jnp.float32),
            pltpu.VMEM((2, 1, triple), jnp.float32),
        ],
    )


BQ, BV, BO, B2, G1, E1, G2, E2 = range(8)


def normal(values):
    center = values - jnp.mean(values, axis=-1, keepdims=True)
    inverse = lax.rsqrt(jnp.mean(center * center, axis=-1, keepdims=True) + EPS_NORM)
    return center * inverse, inverse


def held(array):
    return pl.BlockSpec(
        array.shape, lambda *_: (0,) * len(array.shape), pipeline_mode=pl.Buffered(buffer_count=1)
    )


def tiles(*arrays):
    return [
        pl.BlockSpec((CHUNK, a.shape[1]), lambda i, at: (i, 0))
        if a.shape[0] == arrays[0].shape[0]
        else pl.BlockSpec((a.shape[0], CHUNK), lambda i, at: (0, i))
        for a in arrays
    ]


def forward_kernel(
    at, hidden0, context, out_weight, vectors, up, up_bias, down,
    entry2, normed1, inverse1, active, slope, normed2, inverse2, block_out, pooled, units, acts,
):
    step = pl.program_id(0)
    rows, width = hidden0.shape
    token_count = rows * pl.num_programs(0)
    resid = hidden0[...] + matmul(context[...], out_weight[...]) + vectors[BO : BO + 1]
    normed, inverse = normal(resid)
    hidden1 = normed * vectors[G1 : G1 + 1] + vectors[E1 : E1 + 1]
    normed1[...], inverse1[...] = halved(normed), inverse
    entry = halved(hidden1)
    entry2[...] = entry.T
    half = up.shape[2]
    span = half // BLOCKS
    for other in range(2):
        for block in range(BLOCKS):
            here = slice(block * span, (block + 1) * span)
            there = slice(other * half + block * span, other * half + (block + 1) * span)
            values = matmul(entry, up[other, :, here]) + up_bias[other, :, here]
            cumulative = 0.5 + 0.5 * lax.erf(values * ROOT_HALF)
            acted = halved(values * cumulative)
            acts[:, there] = acted
            active[there] = acted.T
            density = jnp.exp(-0.5 * values * values) * (1.0 / ROOT_TWO_PI)
            slope[:, there] = halved(cumulative + values * density)
    total = hidden1 + vectors[B2 : B2 + 1] + matmul(acts[...], down[...])
    normed, inverse = normal(total)
    hidden2 = normed * vectors[G2 : G2 + 1] + vectors[E2 : E2 + 1]
    normed2[...], inverse2[...] = halved(normed), inverse
    block_out[...] = halved(hidden2)

    @pl.when(step == 0)
    def _():
        pooled[...] = jnp.zeros_like(pooled)

    slots = pooled.shape[0]
    span = token_count // slots
    for group in range(rows // span):
        slot, live = group_slot(at, step * (rows // span) + group, token_count)
        part = hidden2[group * span : (group + 1) * span] * live
        pooled[pl.ds(slot, 1)] += jnp.sum(part, axis=0, keepdims=True)

    @pl.when(step == pl.num_programs(0) - 1)
    def _():
        row = lax.broadcasted_iota(jnp.int32, (slots, LANES), 0)
        length = jnp.zeros((slots, LANES), jnp.int32)
        for slot in range(slots):
            length += jnp.where(row == slot, at[LENGTHS + slot], 0)
        mean = pooled[...] * (1.0 / jnp.maximum(length[:, :1], 1).astype(jnp.float32))
        pooled[...] = mean
        squares = jnp.sum(mean * mean, axis=-1, keepdims=True)
        units[:, :width] = halved(mean * lax.rsqrt(squares + EPS_NORM))
        first = lax.broadcasted_iota(jnp.int32, (slots, LANES), 1) == 0
        units[:, width:] = halved(jnp.where(first & (length > 0), 1.0, 0.0))


def forward(at, hidden0, context, out_weight, vectors, up, up_bias, down):
    token_count, width = hidden0.shape
    slots = at.shape[0] - LENGTHS
    hidden = 2 * up.shape[2]
    half = functools.partial(stacked, dtype=jnp.bfloat16)
    outs = [
        far_off(width, token_count),
        far_off(token_count, width),
        stacked(token_count, 1),
        pltpu.VMEM((hidden, token_count), jnp.bfloat16),
        pltpu.VMEM((token_count, hidden), jnp.bfloat16),
        pltpu.VMEM((token_count, width), jnp.bfloat16),
        stacked(token_count, 1),
        far_off(token_count, width),
        stacked(slots, width),
        half(slots, width + LANES),
    ]
    return kernel_call(
        forward_kernel,
        (token_count // CHUNK,),
        at,
        [far_away(hidden0), far_away(context), out_weight, vectors, near_by(up), up_bias, near_by(down)],
        tiles(hidden0, context)
        + [held(out_weight), held(vectors), HERE, held(up_bias), HERE],
        outs,
        tiles(hidden0, *outs[:8])[1:] + [whole_block(out) for out in outs[8:]],
        [pltpu.VMEM((CHUNK, hidden), jnp.bfloat16)],
        vmem=FORWARD_VMEM,
    )


def norm_back(grad, normed, inverse, gain):
    scaled = grad * gain
    inner = (
        scaled
        - jnp.mean(scaled, axis=-1, keepdims=True)
        - normed * jnp.mean(scaled * normed, axis=-1, keepdims=True)
    )
    return inner * inverse


def loss_kernel(
    at, units, others, pooled, normed2, inverse2, vectors,
    dresid, dresid_half, sums, dpool,
):
    slots, width = pooled.shape
    count = units.shape[0]
    step = pl.program_id(0)

    @pl.when(step == 0)
    def _():
        own, own_flags = units[:, :width], units[:, width:]
        other, other_flags = others[:, :width], others[:, width:]
        lane = lax.broadcasted_iota(jnp.int32, (slots, LANES), 1)
        one_hot = halved(jnp.where(lane == 0, 1.0, 0.0))
        own_row = matmul(one_hot, own_flags, NT)[:1] > 0
        other_row = matmul(one_hot, other_flags, NT)[:1] > 0

        def shares(lines, columns, live):
            logits = matmul(lines, columns, NT) * INV_TEMP
            logits = jnp.where(live, logits, NEGATIVE)
            weights = jnp.exp(logits - jnp.max(logits, axis=-1, keepdims=True))
            return weights / jnp.sum(weights, axis=-1, keepdims=True)

        row = lax.broadcasted_iota(jnp.int32, (slots, count), 0)
        column = lax.broadcasted_iota(jnp.int32, (slots, count), 1)
        target = jnp.where(row == column, 1.0, 0.0)
        row_live = own_flags[:slots, :1].astype(jnp.float32)
        dlogit = halved(LOSS_WEIGHT * (shares(own[:slots], other, other_row) - target) * row_live)
        near = shares(other, own, own_row)[:, :LANES]
        row = lax.broadcasted_iota(jnp.int32, (count, LANES), 0)
        column = lax.broadcasted_iota(jnp.int32, (count, LANES), 1)
        target = jnp.where(row == column, 1.0, 0.0)
        other_live = other_flags[:, :1].astype(jnp.float32)
        dnear = LOSS_WEIGHT * (near - target) * other_live
        dnear = halved(jnp.where(column < slots, dnear, 0.0))
        dunit = INV_TEMP * (matmul(dlogit, other) + matmul(dnear, other, TN)[:slots])
        mean = pooled[...]
        inverse = lax.rsqrt(jnp.sum(mean * mean, axis=-1, keepdims=True) + EPS_NORM)
        along = jnp.sum(mean * dunit, axis=-1, keepdims=True)
        grad = inverse * dunit - inverse * inverse * inverse * mean * along
        slot_row = lax.broadcasted_iota(jnp.int32, (slots, 1), 0)
        length = jnp.zeros((slots, 1), jnp.int32)
        for slot in range(slots):
            length += jnp.where(slot_row == slot, at[LENGTHS + slot], 0)
        dpool[...] = grad * (1.0 / jnp.maximum(length, 1).astype(jnp.float32))
        sums[...] = jnp.zeros_like(sums)

    gain = vectors[G2 : G2 + 1]
    token_count = normed2.shape[0] * pl.num_programs(0)
    span = token_count // slots
    groups = normed2.shape[0] // span
    for group in range(groups):
        here = pl.ds(group * span, span)
        slot, live = group_slot(at, step * groups + group, token_count)
        dhidden = dpool[pl.ds(slot, 1)] * live
        normed = normed2[here].astype(jnp.float32)
        values = norm_back(dhidden, normed, inverse2[here], gain)
        dresid[here] = values
        dresid_half[here] = halved(values)
        for k, terms in enumerate((values, dhidden * normed, dhidden)):
            sums[k : k + 1] += jnp.sum(terms, axis=0, keepdims=True)


def loss_back(at, units, others, pooled, normed2, inverse2, vectors):
    token_count, width = normed2.shape
    half = functools.partial(stacked, dtype=jnp.bfloat16)
    ins = [units, others, pooled, near_by(normed2), inverse2, vectors]
    outs = [
        pltpu.VMEM((token_count, width), jnp.float32),
        pltpu.VMEM((token_count, width), jnp.bfloat16),
        stacked(3, width),
    ]
    return kernel_call(
        loss_kernel,
        (token_count // CHUNK,),
        at,
        ins,
        [held(a) for a in ins[:3]] + tiles(*ins[3:5]) + [held(vectors)],
        outs,
        tiles(*outs[:2]) + [whole_block(outs[2])],
        [pltpu.VMEM(pooled.shape, jnp.float32)],
        vmem=12,
    )


def backward_kernel(
    at, dresid2, dresid2_half, slope, up, down, normed1, inverse1, vectors,
    dpre, dpre_sum, dresid, dresid_half, sums,
):
    @pl.when(pl.program_id(0) == 0)
    def _():
        dpre_sum[...] = jnp.zeros_like(dpre_sum)
        sums[...] = jnp.zeros_like(sums)

    half = up.shape[2]
    span = half // BLOCKS
    grad = dresid2_half[...]
    for block in range(2 * BLOCKS):
        here = slice(block * span, (block + 1) * span)
        dactive = matmul(grad, down[here], NT)
        values = dactive * slope[:, here].astype(jnp.float32)
        dpre_sum[:, here] += jnp.sum(values, axis=0, keepdims=True)
        dpre[:, here] = halved(values)
    dhidden = dresid2[...]
    for other in range(2):
        dhidden += matmul(dpre[:, other * half : (other + 1) * half], up[other], NT)
    normed = normed1[...].astype(jnp.float32)
    values = norm_back(dhidden, normed, inverse1[...], vectors[G1 : G1 + 1])
    dresid[...] = values
    rounded = halved(values)
    dresid_half[...] = rounded
    for k, terms in enumerate((values, dhidden * normed, dhidden)):
        sums[k : k + 1] += jnp.sum(terms, axis=0, keepdims=True)


def backward(at, dresid2, dresid2_half, slope, up, down, normed1, inverse1, vectors):
    token_count, width = dresid2.shape
    hidden = 2 * up.shape[2]
    half = functools.partial(stacked, dtype=jnp.bfloat16)
    outs = [
        pltpu.VMEM((token_count, hidden), jnp.bfloat16),
        stacked(1, hidden),
        far_off(token_count, width, dtype=jnp.float32),
        half(token_count, width),
        stacked(3, width),
    ]
    out_specs = tiles(outs[0], *outs[2:4])
    return kernel_call(
        backward_kernel,
        (token_count // CHUNK,),
        at,
        [near_by(dresid2), near_by(dresid2_half), near_by(slope), near_by(up), near_by(down), far_away(normed1), inverse1, vectors],
        tiles(dresid2, dresid2_half, slope) + [HERE, HERE] + tiles(normed1, inverse1)
        + [held(vectors)],
        outs,
        out_specs[:1] + [whole_block(outs[1])] + out_specs[1:] + [whole_block(outs[4])],
        vmem=BACKWARD_VMEM,
        long=True,
    )


def leave_kernel(
    at, dresid1, dtriples, qkv, dsums, sums1, sums2, dpre_sum, input_grad, last_own, last_away, total, turned,
):
    step = pl.program_id(0)
    rows = dresid1.shape[0]
    values = dresid1[...]
    for other in range(2):
        values = values + matmul(dtriples[other], qkv[other], NT)
    input_grad[...] = values
    half_steps = pl.num_programs(0) // 2
    here = pl.ds(pl.multiple_of((step % half_steps) * rows, rows), rows)

    @pl.when(step < half_steps)
    def _():
        total[here] = values

    @pl.when(step >= half_steps)
    def _():
        total[here] += values

    @pl.when(step == pl.num_programs(0) - 1)
    def _():
        count = total.shape[0]
        long = total[...]
        span = 2 * count // (at.shape[0] - LENGTHS)
        short = sum(long[k * span : (k + 1) * span] for k in range(count // span))
        short = jnp.concatenate([short, jnp.zeros((count - span, long.shape[1]), jnp.float32)], axis=0)
        columns = jnp.where(at[SLOT_COUNT] == 2, long, short).T
        left, right = columns[:, : count // 2], columns[:, count // 2 :]
        last_own[:, : count // 2] = jnp.where(at[0] == 0, left, right)
        last_away[:, : count // 2] = halved(jnp.where(at[0] == 0, right, left))
        width = long.shape[1]
        first = [jnp.concatenate([dsums[0, k], dsums[1, k]], axis=1) for k in range(2)]
        swapped = [jnp.concatenate([dsums[1, k], dsums[0, k]], axis=1) for k in range(2)]
        heads = [jnp.where(at[0] == 0, a, b) for a, b in zip(first, swapped)]
        vectors = [heads + [sums1[:1], sums2[:1]], [sums1[1:2], sums1[2:3], sums2[1:2], sums2[2:3]]]
        blank = jnp.zeros((LANES - 4, width), jnp.float32)
        vectors = [jnp.concatenate(rows + [blank], axis=0).T for rows in vectors]
        lane = lax.broadcasted_iota(jnp.int32, (width, LANES), 1)
        for other, (out, words) in enumerate(((last_own, False), (last_away, True))):
            row = dpre_sum[:, other * 2 * width : (other + 1) * 2 * width]
            turned[...] = jnp.broadcast_to(row, (LANES, 2 * width)).T
            lines = jnp.where(at[0] == other, vectors[0], vectors[1])
            for k in range(2):
                lines = jnp.where(lane == 4 + k, turned[pl.ds(k, width, 2)], lines)
            out[:, count // 2 :] = halved(two_words(lines)) if words else lines


def left(at, dresid1, dtriples, qkv, dsums, sums1, sums2, dpre_sum):
    token_count, width = dresid1.shape
    triple = qkv.shape[2]
    columns = token_count // 4 + LANES
    small = [dsums, sums1, sums2, dpre_sum]
    outs = [
        stacked(token_count, width),
        stacked(width, columns),
        stacked(width, columns, dtype=jnp.bfloat16),
    ]
    return kernel_call(
        leave_kernel,
        (token_count // CHUNK,),
        at,
        [far_away(dresid1), near_by(dtriples), qkv] + small,
        tiles(dresid1)
        + [pl.BlockSpec((2, CHUNK, triple), lambda i, at: (0, i, 0)), held(qkv)]
        + [held(a) for a in small],
        outs,
        tiles(outs[0]) + [whole_block(out) for out in outs[1:]],
        [
            pltpu.VMEM((token_count // 2, width), jnp.float32),
            pltpu.VMEM((2 * width, LANES), jnp.float32),
        ],
        long=True,
    )


def product_kernel(natural_order, at, left_ref, right_ref, own, away):
    values = left_ref[...]
    if len(right_ref.shape) == 3:
        first, second = matmul(values, right_ref[0]), matmul(values, right_ref[1])
    else:
        both = matmul(values, right_ref[...])
        first, second = both[:, : both.shape[1] // 2], both[:, both.shape[1] // 2 :]
    first, second = halved(first), halved(second)
    if natural_order:
        first, second = jnp.where(at[0] == 0, first, second), jnp.where(at[0] == 0, second, first)
    own[...], away[...] = first, second


def product(at, left_array, right_array, natural_order=False, near=None):
    rows, depth = left_array.shape
    columns = right_array.size // depth // 2
    tile = rows // 6 if rows > 1024 else rows // 3
    outs = [stacked(rows, columns, dtype=jnp.bfloat16)] * 2
    return kernel_call(
        functools.partial(product_kernel, natural_order),
        (rows // tile,),
        at,
        [near_by(left_array) if near in (0, 2) else left_array, near_by(right_array) if near in (1, 2) else right_array],
        [pl.BlockSpec((tile, depth), lambda i, at: (i, 0)), HERE if near in (1, 2) else held(right_array)],
        outs,
        [pl.BlockSpec((tile, columns), lambda i, at: (i, 0))] * 2,
        long=True,
        vmem=PRODUCT_VMEM,
    )


def renew(grad, moment, weight, average, rate):
    moment_new = MOMENTUM * moment + grad
    weight_new = weight - rate * (grad + MOMENTUM * moment_new)
    average_new = AVERAGE * average + (1.0 - AVERAGE) * weight_new
    return (grad, moment_new, weight_new, average_new)


def finish_kernel(kept, first, second, third, out_grad, *refs):
    states, outs = refs[:9], refs[9:]
    quarter = out_grad.shape[1]
    total = kept[...]
    for part in (first, second, third):
        total = total + received(part[...], True)

    def write(at, grad, state, results, rate):
        for result, value in zip(results, renew(grad, *[ref[at] for ref in state], rate), strict=True):
            result[at] = value

    for k in range(4):
        grad = total[:, k * quarter : (k + 1) * quarter] if k < 3 else out_grad[...]
        write((k,), grad, states[:3], outs[:4], RATE)
    lines = total[:, -LANES:].T
    write((Ellipsis,), lines[:4], states[3:6], outs[4:8], RATE)
    write((Ellipsis,), total[:, 3 * quarter : -LANES], states[6:], outs[8:12], POS_RATE)
    rows = kept.shape[0]
    row = lax.broadcasted_iota(jnp.int32, (rows, 2 * rows), 0)
    column = lax.broadcasted_iota(jnp.int32, (rows, 2 * rows), 1)
    bias = jnp.zeros((8, 2 * rows), jnp.float32)
    for k in range(2):
        chosen = jnp.where(column == 2 * row + k, 1.0, 0.0)
        line = jnp.broadcast_to(lines[4 + k : 5 + k], (8, rows))
        bias = bias + jnp.dot(
            line, chosen, precision=lax.Precision.HIGHEST, preferred_element_type=jnp.float32
        )
    outs[12][...] = bias[:1]


def finished(kept, arrived, out_grad, attn_state, vector_state, pos_state):
    pos_state = tuple(part.T for part in pos_state)
    states = attn_state + vector_state + pos_state
    outs = [stacked(*state[0].shape) for state in (attn_state, vector_state, pos_state) for _ in range(4)]
    outs.append(stacked(1, 2 * kept.shape[0]))
    out = pl.pallas_call(
        finish_kernel,
        in_specs=[HERE] * (5 + len(states)),
        out_specs=[HERE] * len(outs),
        out_shape=outs,
        compiler_params=pltpu.CompilerParams(vmem_limit_bytes=20 << 20),
        cost_estimate=COST,
    )(kept, *arrived, out_grad, *states)
    return out[:4], out[4:8], [part.T for part in out[8:12]], out[12]


def local(
    tokens,
    lengths,
    attn_weight,
    attn_moment,
    attn_average,
    up_weight,
    up_moment,
    up_average,
    down_weight,
    down_moment,
    down_average,
    layer_vectors,
    vector_moment,
    vector_average,
    up_bias,
    bias_moment,
    bias_average,
    pos_table,
    pos_moment,
    pos_average,
):
    at = scalars(lengths[0, 0])
    stream = at[0]
    upper = stream == 1
    devices = lax.axis_size("batch")
    rows, hidden_half = up_weight.shape
    quarter = attn_weight.shape[2]
    width = 2 * quarter
    pos_half = pos_table.shape[0]
    slot_count = lengths.shape[2]

    misc = jnp.concatenate([layer_vectors.T, up_bias.reshape(rows, 2)], axis=1)
    misc = jnp.pad(misc, ((0, 0), (0, LANES - misc.shape[1])))
    entry_block = halved(
        jnp.concatenate([attn_weight[0], attn_weight[1], attn_weight[2], pos_table.T, misc], axis=1)
    )
    middle_block = halved(
        jnp.concatenate([up_weight, attn_weight[3], jnp.zeros((rows, LANES), jnp.float32)], axis=1)
    )
    triple = 3 * quarter
    pos_stop = triple + pos_half
    entry_gather = Gather(entry_block, width)
    entry_gather.far()
    down_both = lax.all_gather(
        after(halved(down_weight), entry_gather.blocks), ("stream", "batch"), axis=0, tiled=True
    )
    entry_gather.near((2, 1))
    middle_gather = Gather(
        after(middle_block, *entry_gather.sides), (hidden_half + quarter + LANES) // 2
    )
    middle_gather.far()
    entry_gather.near((1, 2), middle_gather.blocks)
    qkv_blocks, pos_blocks, misc_blocks = entry_gather.placed(
        at,
        (
            (0, triple, 0, "relative", 0, 0),
            (triple, pos_stop, 1, "", 0, pos_half),
            (pos_stop, pos_stop + LANES, 2, "stream", 0, 0),
        ),
        [
            pltpu.VMEM((2, devices, rows, triple), jnp.bfloat16),
            pltpu.VMEM((devices, rows, 2 * pos_half), jnp.bfloat16),
            pltpu.VMEM((2, devices, rows, LANES), jnp.bfloat16),
        ],
    )
    qkv = qkv_blocks.reshape(2, width, triple)
    pos_full = pos_blocks.reshape(width, 2 * pos_half)
    def own_first(pair):
        return jnp.where(upper, pair[::-1], pair)

    hidden0, entry, triples, vectors, bias_lines = entered(
        at, tokens[0], pos_full, qkv, misc_blocks.reshape(2, width, LANES)
    )
    biases = bias_lines.reshape(2, 2, width).transpose(0, 2, 1).reshape(2, 1, hidden_half)
    middle_gather.near((2, 1), triples)
    context_half, context_turned, probs = attend(after(at, *middle_gather.sides), triples)
    middle_gather.near((1, 2), context_half)
    up_blocks, out_blocks, down = middle_gather.placed(
        after(at, context_half),
        (
            (0, hidden_half, 0, "relative", 0, 0),
            (hidden_half, hidden_half + quarter, 1, "", 0, quarter),
        ),
        [
            pltpu.VMEM((2, devices, rows, hidden_half), jnp.bfloat16),
            stacked(devices, rows, width, dtype=jnp.bfloat16),
        ],
        down_both.reshape(2, 2 * hidden_half, quarter),
    )
    up = up_blocks.reshape(2, width, hidden_half)
    out_full = out_blocks.reshape(width, width)
    (entry2, normed1, inverse1, active, slope, normed2, inverse2, block_out, pooled, units) = forward(
        at, hidden0, context_half, out_full, vectors, up, own_first(biases), down
    )

    units = units[None]
    bit = 0
    while 1 << bit < devices:
        step = min(2, devices.bit_length() - 1 - bit)
        arrived = [exchanged(units, "batch", d << bit) for d in range(1, 1 << step)]
        units = jnp.concatenate([units] + arrived, axis=0)
        bit += step
    units = units.reshape(-1, units.shape[2])
    others = exchanged(units, "stream", 1)
    dresid2, dresid2_half, sums2 = loss_back(
        at, units, others, pooled, normed2, inverse2, vectors
    )

    def blocks(values):
        return values.reshape(devices // 4, 2, 2, values.shape[0] // devices, values.shape[1])

    down_own, down_away = product(at, active, dresid2_half, True, near=2)
    down_in = exchanged(down_away, "stream", 1)
    by_rows = down_weight.shape[0] % 32 == 0
    half_rows = down_weight.shape[0] // 2
    down_pair = (blocks(down_own), blocks(down_in))
    if by_rows:
        down_sides = [[down_pair + (half_rows, k, quarter, 0, True)] for k in range(2)]
    else:
        down_sides = [
            [down_pair + (2 * half_rows, 0, LANES, k, True) for k in ks] for ks in ((0, 1), (2,))
        ]
    down_fold = Fold(at, down_sides)
    down_parts = down_fold.first()
    down_first = down_fold.first_sent(down_parts)
    dpre, dpre_sum, dresid1, dresid1_half, sums1 = backward(
        after(at, *down_parts), dresid2, dresid2_half, slope, up, down, normed1, inverse1, vectors
    )
    down_fold.at = after(at, dresid1_half, *down_first)
    down_parts = down_fold.second(down_first)
    down_second, down_kept = down_fold.second_sent(down_parts)
    up_own, up_away = product(after(at, *down_parts), entry2, dpre, near=1)
    up_in = exchanged(up_away, "stream", 1)
    out_own, out_away = product(
        after(at, up_away, *down_second), context_turned, dresid1_half, True
    )
    out_in = exchanged(out_away, "stream", 1)
    down_fold.at = after(at, out_own, *down_second)
    down_last = down_fold.third(down_second, down_kept)
    down_third = down_fold.third_sent(down_last)
    third = hidden_half // 3
    up_pair = (blocks(up_own), blocks(up_in))
    out_pair = (blocks(out_own), blocks(out_in))
    middle_fold = Fold(
        after(at, *down_last),
        [
            [up_pair + (rows, 0, third, 0, False), up_pair + (rows, 0, third, 1, False)],
            [up_pair + (rows, 0, third, 2, False), out_pair + (rows, 0, quarter, 0, False)],
        ],
    )
    middle_parts = middle_fold.first()
    middle_first = middle_fold.first_sent(middle_parts)
    dcontext_half = halved(matmul(after(dresid1_half, *middle_parts), out_full, NT))
    dtriples, dsums = attend_back(at, triples, context_half, dcontext_half, probs)
    qkv_own, qkv_away = product(at, entry, dtriples, near=1)
    qkv_in = exchanged(qkv_away, "stream", 1)
    middle_fold.at = after(at, qkv_away, *middle_first)
    middle_parts = middle_fold.second(middle_first)
    middle_second, middle_kept = middle_fold.second_sent(middle_parts)
    input_grad, last_own, last_away = left(
        after(at, qkv_away, *middle_parts, *down_third), dresid1, dtriples, qkv, dsums, sums1, sums2, dpre_sum
    )
    last_in = exchanged(last_away, "stream", 1)
    qkv_pair = (blocks(qkv_own), blocks(qkv_in))
    last_pair = (blocks(last_own), blocks(last_in))
    entry_fold = Fold(
        at,
        [
            [qkv_pair + (rows, 0, quarter, 0, False), qkv_pair + (rows, 0, quarter, 1, False)],
            [
                qkv_pair + (rows, 0, quarter, 2, False),
                last_pair + (rows, 0, pos_half, 0, False),
                last_pair + (rows, 0, LANES, pos_half // LANES, False),
            ],
        ],
        wide=True,
    )
    entry_parts = entry_fold.first()
    entry_first = entry_fold.first_sent(entry_parts)
    middle_fold.at = after(at, *entry_parts, *middle_second)
    middle_parts = middle_fold.third(middle_second, middle_kept)
    entry_fold.at = after(at, *middle_parts)
    entry_parts = entry_fold.second(entry_first)
    middle_third = middle_fold.third_sent(middle_parts)
    middle_sum = middle_fold.total(middle_parts[0], middle_third, *entry_parts)
    down_sum = down_fold.total(down_last[0], down_third, *entry_parts)
    entry_second, entry_kept = entry_fold.second_sent(entry_parts)
    entry_parts = entry_fold.third(entry_second, entry_kept)
    vector_moment, vector_average = (
        after(part, *entry_parts) for part in (vector_moment, vector_average)
    )
    entry_third = entry_fold.third_sent(entry_parts)

    down_grad = down_sum
    if by_rows:
        down_grad = jnp.concatenate([down_sum[:, :quarter], down_sum[:, quarter:]], axis=0)
    up_all = renew(middle_sum[:, :hidden_half], up_moment, up_weight, up_average, RATE)
    down_all = renew(down_grad, down_moment, down_weight, down_average, RATE)
    out_grad = middle_sum[:, hidden_half : hidden_half + quarter]
    attn_state = (attn_moment, attn_weight, attn_average)
    vector_state = (vector_moment, layer_vectors, vector_average)
    pos_state = (pos_moment, pos_table, pos_average)
    if rows % 16 == 0:
        attn_all, vector_all, pos_all, bias_grad = finished(
            entry_parts[0][0], [part[0] for part in entry_third], out_grad, attn_state, vector_state, pos_state
        )
        bias_grad = bias_grad.reshape(-1)
    else:
        entry_sum = entry_fold.total(entry_parts[0], entry_third)
        attn_grad = jnp.stack(
            [entry_sum[:, k * quarter : (k + 1) * quarter] for k in range(3)] + [out_grad]
        )
        attn_all = renew(attn_grad, *attn_state, RATE)
        vector_all = renew(entry_sum[:, pos_stop : pos_stop + 4].T, *vector_state, RATE)
        pos_all = renew(entry_sum[:, triple:pos_stop].T, *pos_state, POS_RATE)
        bias_grad = entry_sum[:, pos_stop + 4 : pos_stop + 6].reshape(-1)
    bias_all = renew(bias_grad, bias_moment, up_bias, bias_average, RATE)
    return (
        block_out[None],
        input_grad[None],
        *attn_all,
        *up_all,
        *down_all,
        *vector_all,
        *bias_all,
        *pos_all,
    )


def solution(mesh):
    tokens_at, weight_at = P("stream", "batch", None), P("batch", "stream")
    attn_at, rows_at, bias_at = P(None, "batch", "stream"), P("stream", "batch"), P(("stream", "batch"))
    kinds = (attn_at, weight_at, weight_at, rows_at, bias_at, rows_at)
    in_specs = (tokens_at, tokens_at) + tuple(kind for kind in kinds for _ in range(3))
    out_specs = (tokens_at, tokens_at) + tuple(kind for kind in kinds for _ in range(4))
    return jax.shard_map(local, mesh=mesh, in_specs=in_specs, out_specs=out_specs, check_vma=False)
```

```python
import functools
import math

import jax
import jax.numpy as jnp
from jax import lax
from jax.experimental import pallas as pl
from jax.experimental.pallas import tpu as pltpu
from jax.sharding import PartitionSpec as P

HEADS = 12


EPS_NORM = 1e-06
INV_TEMP = 100.0
LOSS_WEIGHT = 256.0
MOMENTUM = 0.5
AVERAGE = 0.5
RATE = 0.0001
POS_RATE = 0.01
NEGATIVE = -1e30
ROOT_HALF = 0.7071067811865476
ROOT_TWO_PI = 2.5066282746310002
LANES = 128
SLOT_COUNT, LENGTHS = 4, 5
CHUNK, BLOCKS = 256, 3
COST = pl.CostEstimate(flops=1000, bytes_accessed=1000, transcendentals=0)
LONG_COST = pl.CostEstimate(flops=10**12, bytes_accessed=10**9, transcendentals=0)
ANYWHERE = pl.BlockSpec(memory_space=pl.ANY)
HERE = pl.BlockSpec(memory_space=pltpu.VMEM)
FORWARD_VMEM, BACKWARD_VMEM, PRODUCT_VMEM, OTHER_VMEM = 22, 17, 12, 20
NN = (((1,), (0,)), ((), ()))
NT = (((1,), (1,)), ((), ()))
TN = (((0,), (0,)), ((), ()))


def halved(values):
    return values.astype(jnp.bfloat16)


def matmul(left, right, dims=NN):
    return lax.dot_general(left, right, dims, preferred_element_type=jnp.float32)


def stacked(*shape, dtype=jnp.float32):
    return jax.ShapeDtypeStruct(shape, dtype)


def far_off(*shape, dtype=jnp.bfloat16):
    return pltpu.HBM(shape, dtype)


def after(value, *earlier):
    return lax.optimization_barrier((value, earlier))[0]


def exchanged(block, axis, mask):
    count = lax.axis_size(axis)
    return lax.ppermute(block, axis, [(place, place ^ mask) for place in range(count)])


def scalars(lengths_row):
    batch = lax.axis_index("batch")
    places = [lax.axis_index("stream"), batch & 1, (batch >> 1) & 1, batch >> 2]
    counted = jnp.sum((lengths_row > 0).astype(jnp.int32))
    return jnp.concatenate([jnp.stack(places + [counted]), lengths_row]).astype(jnp.int32)


class Gather:
    def __init__(self, block, cut):
        self.cut = cut
        self.bits = lax.axis_size("batch").bit_length() - 1
        self.blocks, self.masks = block[None], [0]

    def far(self, *earlier):
        bit = self.bits
        while bit > 2:
            step = min(2, bit - 2)
            bit -= step
            offsets = [d << bit for d in range(1 << step)]
            arrived = [exchanged(self.blocks, "batch", offset) for offset in offsets[1:]]
            own = after(self.blocks, *earlier) if earlier else self.blocks
            self.blocks = jnp.concatenate([own] + arrived, axis=0)
            self.masks = [offset | mask for offset in offsets for mask in self.masks]
        self.sides = [self.blocks[:, :, : self.cut], self.blocks[:, :, self.cut :]]
        self.masks = [self.masks, self.masks]

    def near(self, flips, *earlier):
        for side, flip in enumerate(flips):
            part = self.sides[side]
            own = after(part, *earlier) if earlier else part
            self.sides[side] = jnp.concatenate([own, exchanged(part, "batch", flip)], axis=0)
            self.masks[side] = self.masks[side] + [flip | mask for mask in self.masks[side]]

    def placed(self, at, pieces, shapes, down=None):
        sources, moves = [], []
        for other in range(2):
            for side, part in enumerate(self.sides):
                sources.append(exchanged(part, "stream", 1) if other else part)
                base = self.cut * side
                for start, stop, target, lead, offset, span in pieces:
                    low, high = max(start, base), min(stop, base + part.shape[2])
                    if low >= high:
                        continue
                    for entry, mask in enumerate(self.masks[side]):
                        moves.append(
                            (len(sources) - 1, entry, mask, (low - base, high - base), target, lead,
                             other, offset + low - start, span)
                        )
        return placed(at, sources, moves, shapes, down)


def far_away(array):
    return pltpu.with_memory_space_constraint(array, pltpu.HBM)


def near_by(array):
    return pltpu.with_memory_space_constraint(array, pltpu.VMEM)


def place_kernel(moves, count, with_down, at_ref, *refs):
    sources, rest = refs[:count], refs[count:]
    stream = at_ref[0]
    copies = []
    if with_down:
        down, targets, down_held, sems = rest[0], rest[1:-2], rest[-2], rest[-1]
        half, quarter = down.shape[1] // 2, down.shape[2]
        for other in range(2):
            start = pl.multiple_of((other ^ stream) * half, half)
            for k in range(2):
                copies.append(
                    pltpu.make_async_copy(
                        down.at[k, pl.ds(start, half)],
                        down_held.at[pl.ds(other * half, half), pl.ds(k * quarter, quarter)],
                        sems.at[2 * other + k],
                    )
                )
        for copy in copies:
            copy.start()
    else:
        targets = rest
    batch = at_ref[1] + 2 * at_ref[2] + 4 * at_ref[3]
    for source, entry, mask, columns, target, lead, other, start, span in moves:
        core = stream ^ other
        low = pl.multiple_of(start + core * span, LANES) if span else start
        at = (batch ^ mask, slice(None), pl.ds(low, columns[1] - columns[0]))
        if lead == "relative":
            at = (other,) + at
        elif lead == "stream":
            at = (core,) + at
        targets[target][at] = sources[source][entry, :, columns[0] : columns[1]]
    for copy in copies:
        copy.wait()


def placed(at, sources, moves, shapes, down=None):
    held_here = pl.BlockSpec(memory_space=pltpu.VMEM)
    ins, in_specs, out_specs = list(sources), [held_here] * len(sources), [held_here] * len(shapes)
    scratch = []
    if down is not None:
        ins.append(far_away(down))
        in_specs.append(ANYWHERE)
        shapes = list(shapes) + [pltpu.VMEM((down.shape[1], 2 * down.shape[2]), down.dtype)]
        out_specs.append(held_here)
        scratch.append(pltpu.SemaphoreType.DMA((4,)))
    return pl.pallas_call(
        functools.partial(place_kernel, moves, len(sources), down is not None),
        in_specs=[pl.BlockSpec(memory_space=pltpu.SMEM)] + in_specs,
        out_specs=out_specs,
        out_shape=shapes,
        scratch_shapes=scratch,
        compiler_params=pltpu.CompilerParams(vmem_limit_bytes=24 << 20),
        cost_estimate=COST,
    )(at, *ins)


def two_words(values):
    half = values.shape[-1] // 2
    coarse = values.astype(jnp.bfloat16).astype(jnp.float32)
    lane = lax.broadcasted_iota(jnp.int32, values.shape, values.ndim - 1)
    rest = jnp.concatenate([(values - coarse)[..., half:], (values - coarse)[..., :half]], axis=-1)
    return jnp.where(lane < half, coarse, rest)


def one_word(block):
    half = block.shape[-1] // 2
    return block + jnp.concatenate([block[..., half:], block[..., :half]], axis=-1)


def received(block, wide):
    values = block.astype(jnp.float32)
    if not wide:
        return values
    return jnp.concatenate(
        [values[..., :-LANES], one_word(values[..., -LANES:])], axis=-1
    )


def sent(values, wide):
    if not wide:
        return halved(values)
    return jnp.concatenate(
        [halved(values[..., :-LANES]), halved(two_words(values[..., -LANES:]))], axis=-1
    )


def piece_spec(piece):
    array, _, rows, row_at, columns, column_at, _ = piece
    return pl.BlockSpec(
        (array.shape[0], 2, 2, rows, columns),
        lambda _, at: (0, 0, 0, row_at, column_at),
        pipeline_mode=pl.Buffered(buffer_count=1),
    )


def fold_call(kernel, count, at, ins, in_specs, outs, out_specs, long=False):
    size = sum(math.prod(o.shape) for o in outs) * 8
    return pl.pallas_call(
        kernel,
        grid_spec=pltpu.PrefetchScalarGridSpec(
            num_scalar_prefetch=1, grid=(count,), in_specs=in_specs, out_specs=out_specs
        ),
        out_shape=outs,
        compiler_params=pltpu.CompilerParams(vmem_limit_bytes=17 << 20),
        cost_estimate=LONG_COST if long else COST,
    )(at, *ins)


class Fold:
    def __init__(self, at, sides, wide=False):
        self.at, self.sides, self.wide = at, sides, (False, wide)
        self.count = sides[0][0][0].shape[0]
        self.rows = [side[0][2] for side in sides]
        self.columns = [sum(piece[4] for piece in side) for side in sides]

    def piece_values(self, refs, side, z, bit, which, core):
        columns = []
        for k, piece in enumerate(self.sides[side]):
            values = []
            for turn, ref in ((core, refs[2 * k]), (1 - core, refs[2 * k + 1])):
                place = z ^ (turn * (self.count // 2)) if piece[6] else z
                entry = ref[place, which, bit] if side == 0 else ref[place, bit, which]
                values.append(entry.astype(jnp.float32))
            wide = self.wide[side] and k == len(self.sides[side]) - 1
            columns.append(values[0] + (one_word(values[1]) if wide else values[1]))
        return jnp.concatenate(columns, axis=-1)

    def first_kernel(self, at_ref, *refs):
        place = 0
        for side, pieces in enumerate(self.sides):
            goes, stays = refs[2 * side - 4], refs[2 * side - 3]
            bit = at_ref[1 + side]
            for z in range(self.count):
                for which in range(2):
                    values = self.piece_values(refs[place:], side, z, 1 - bit, which, at_ref[0])
                    goes[z, which] = sent(values, self.wide[side])
                    stays[z, which] = self.piece_values(
                        refs[place:], side, z, bit, which, at_ref[0]
                    )
            place += 2 * len(pieces)

    def first(self):
        ins, in_specs, outs = [], [], []
        for side, pieces in enumerate(self.sides):
            for piece in pieces:
                ins += piece[:2]
                in_specs += [piece_spec(piece)] * 2
            shape = (self.count, 2, self.rows[side], self.columns[side])
            outs += [stacked(*shape, dtype=jnp.bfloat16), pltpu.VMEM(shape, jnp.float32)]
        return fold_call(self.first_kernel, 1, self.at, ins, in_specs, outs, [whole_block(o) for o in outs])

    def first_sent(self, parts):
        self.stays = parts[1::2]
        return [exchanged(part, "batch", 1 << side) for side, part in enumerate(parts[::2])]

    def second_kernel(self, at_ref, *refs):
        outs = refs[-4:]
        for side in range(2):
            stays, arrived = refs[2 * side], refs[2 * side + 1]
            bit = at_ref[2 - side]
            for z in range(self.count):
                for which, out in ((1 - bit, outs[2 * side]), (bit, outs[2 * side + 1])):
                    values = stays[z, which] + received(arrived[z, which], self.wide[side])
                    out[z] = sent(values, self.wide[side]) if out.dtype == jnp.bfloat16 else values

    def second(self, arrived):
        ins, outs = [], []
        for side in range(2):
            ins += [near_by(self.stays[side]), arrived[side]]
            shape = (self.count, self.rows[side], self.columns[side])
            outs += [stacked(*shape, dtype=jnp.bfloat16), pltpu.VMEM(shape, jnp.float32)]
        return fold_call(
            self.second_kernel, 1, self.at, ins, [whole_block(a) for a in ins], outs,
            [whole_block(out) for out in outs],
        )

    def second_sent(self, out):
        return [exchanged(out[0], "batch", 2), exchanged(out[2], "batch", 1)], [out[1], out[3]]

    def third_kernel(self, radix, at_ref, keep0, keep1, in0, in1, *outs):
        mine = at_ref[3] % radix
        for d, out in enumerate(outs):
            which = mine ^ d
            column = 0
            for side, (keep, arrived) in enumerate(((keep0, in0), (keep1, in1))):
                wide = self.wide[side]
                values = keep[which] + received(arrived[which], wide)
                width = values.shape[-1]
                out[0, :, column : column + width] = values if d == 0 else sent(values, wide)
                column += width

    def third(self, arrived, kept):
        radix = min(4, self.count)
        ins = [near_by(part) for part in kept] + arrived
        in_specs = [pl.BlockSpec((radix,) + a.shape[1:], lambda z, at: (z, 0, 0)) for a in ins]
        shape = (self.count // radix, self.rows[0], sum(self.columns))
        outs = [pltpu.VMEM(shape, jnp.float32)] + [stacked(*shape, dtype=jnp.bfloat16)] * (radix - 1)
        out_specs = [pl.BlockSpec((1,) + o.shape[1:], lambda z, at: (z, 0, 0)) for o in outs]
        return fold_call(
            functools.partial(self.third_kernel, radix), self.count // radix, self.at, ins, in_specs, outs, out_specs, True
        )

    def third_sent(self, out):
        return [exchanged(part, "batch", 4 * d) for d, part in enumerate(out) if d > 0]

    def total(self, kept, arrived, *earlier):
        radix = min(4, self.count)
        terms = [kept] + [after(part, *earlier) if earlier else part for part in arrived]
        total = None
        for term in terms:
            value = received(term, self.wide[1]) if term.dtype == jnp.bfloat16 else term
            total = value if total is None else total + value
        bit = 2 + radix.bit_length() - 1
        while total.shape[0] > 1:
            total = total.reshape((total.shape[0] // 2, 2) + total.shape[1:])
            upper = (lax.axis_index("batch") >> bit) & 1
            away = sent(lax.dynamic_index_in_dim(total, 1 - upper, 1, keepdims=False), False)
            total = lax.dynamic_index_in_dim(total, upper, 1, keepdims=False)
            total = total + exchanged(away, "batch", 1 << bit).astype(jnp.float32)
            bit += 1
        return total[0]


def attend_kernel(at, q_ref, k_ref, v_ref, context_ref, turned_ref, prob_ref, bias):
    half = pl.program_id(1)

    @pl.when(pl.program_id(0) == 0)
    def _():
        span = q_ref.shape[0]
        key = lax.broadcasted_iota(jnp.int32, (span, 1), 0) + half * span
        query = lax.broadcasted_iota(jnp.int32, (1, span), 1) + half * span
        bits = (2 * span).bit_length() - 1
        key_slot = (key * at[SLOT_COUNT]) >> bits
        query_slot = (query * at[SLOT_COUNT]) >> bits
        length = jnp.zeros((span, 1), jnp.int32)
        for slot in range(at.shape[0] - LENGTHS):
            length += jnp.where(key_slot == slot, at[LENGTHS + slot], 0)
        present = key - key_slot * bucket_of(at, 2 * span) < length
        code = jnp.where(present, key_slot, -1)
        bias[half] = jnp.where(code == query_slot, 0.0, NEGATIVE)

    rows, lanes = q_ref.shape
    size = lanes // 2
    first = lax.broadcasted_iota(jnp.int32, (rows, lanes), 1) < size
    keys = k_ref[...]
    none = jnp.zeros_like(keys)
    masked = (jnp.where(first, keys, none), jnp.where(first, none, keys))
    values = v_ref[...].T
    queries = q_ref[...] * jnp.bfloat16(1.0 / math.sqrt(size))
    products = [matmul(masked[h], queries, NT) for h in range(2)]
    probs = []
    for h in range(2):
        scores = products[h] + bias[half]
        weights = jnp.exp(scores - jnp.max(scores, axis=0, keepdims=True))
        probs.append(halved(weights * (1.0 / jnp.sum(weights, axis=0, keepdims=True))))
        prob_ref[0, 0, h] = probs[h]
    outs = [matmul(values[h * size : (h + 1) * size], probs[h]) for h in range(2)]
    context = jnp.concatenate(outs, axis=0)
    turned_ref[...] = halved(context)
    context_ref[...] = halved(context.T)


def natural(pairs, i, at):
    return ((i // (pairs // 2)) ^ at[0]) * (pairs // 2) + i % (pairs // 2)


def attend(at, triples):
    tokens, wide = triples.shape[1:]
    width = wide // 3 * 2
    rows, pairs = tokens // 2, width // LANES
    own = pairs // 2

    def part(p):
        return pl.BlockSpec((None, rows, LANES), lambda i, j, at: (i // own, j, p * own + i % own))

    return pl.pallas_call(
        attend_kernel,
        grid_spec=pltpu.PrefetchScalarGridSpec(
            num_scalar_prefetch=1,
            grid=(pairs, 2),
            in_specs=[
                part(0),
                part(1),
                part(2),
            ],
            out_specs=[
                pl.BlockSpec((rows, LANES), lambda i, j, at: (j, natural(pairs, i, at))),
                pl.BlockSpec((LANES, rows), lambda i, j, at: (natural(pairs, i, at), j)),
                pl.BlockSpec((1, 1, 2, rows, rows), lambda i, j, at: (i, j, 0, 0, 0)),
            ],
            scratch_shapes=[pltpu.VMEM((2, rows, rows), jnp.float32)],
        ),
        out_shape=[
            far_off(tokens, width),
            far_off(width, tokens),
            far_off(pairs, 2, 2, rows, rows),
        ],
        compiler_params=pltpu.CompilerParams(vmem_limit_bytes=14 << 20),
        cost_estimate=COST,
    )(at, *[far_away(triples)] * 3)


def attend_back_kernel(at, q_ref, k_ref, v_ref, context_ref, grad_ref, prob_ref, out_ref, sum_ref):
    rows, lanes = q_ref.shape
    size = lanes // 2
    scale = jnp.bfloat16(1.0 / math.sqrt(size))
    first = lax.broadcasted_iota(jnp.int32, (rows, lanes), 1) < size
    queries = q_ref[...] * scale
    keys = (k_ref[...] * scale).T
    values, grads = v_ref[...], grad_ref[...]
    none = jnp.zeros_like(values)
    masked = (jnp.where(first, values, none), jnp.where(first, none, values))
    products = (grads.astype(jnp.float32) * context_ref[...].astype(jnp.float32)).T
    dquery, dkey, dvalue = [], [], []
    for h in range(2):
        here = slice(h * size, (h + 1) * size)
        rowdot = jnp.sum(products[here], axis=0, keepdims=True)
        probs = prob_ref[0, 0, h]
        dprob = matmul(masked[h], grads, NT)
        dscore = halved(probs.astype(jnp.float32) * (dprob - rowdot))
        dkey.append(matmul(dscore, queries))
        dvalue.append(matmul(probs, grads))
        dquery.append(matmul(keys[here], dscore))
    dquery = jnp.concatenate(dquery, axis=0).T
    dkey = jnp.where(first, dkey[0], dkey[1])
    dvalue = jnp.where(first, dvalue[0], dvalue[1])
    pair = pl.program_id(2)
    quarter = out_ref.shape[2] // 3
    low = pl.multiple_of(pair * lanes, lanes)
    for p, part in enumerate((dquery, dkey, dvalue)):
        out_ref[0, :, pl.ds(p * quarter + low, lanes)] = halved(part)

    @pl.when((pl.program_id(1) == 0) & (pair == 0))
    def _():
        sum_ref[...] = jnp.zeros_like(sum_ref)

    sum_ref[0, 0, :, pl.ds(low, lanes)] += jnp.sum(dquery, axis=0, keepdims=True)
    sum_ref[0, 1, :, pl.ds(low, lanes)] += jnp.sum(dvalue, axis=0, keepdims=True)


def attend_back(at, triples, context, grad, probs):
    tokens, width = context.shape
    rows, pairs = tokens // 2, width // LANES
    own = pairs // 2

    def part(p):
        return pl.BlockSpec((None, rows, LANES), lambda r, j, i, at: (r, j, p * own + i))

    whole = pl.BlockSpec((rows, LANES), lambda r, j, i, at: (j, natural(pairs, r * own + i, at)))
    return pl.pallas_call(
        attend_back_kernel,
        grid_spec=pltpu.PrefetchScalarGridSpec(
            num_scalar_prefetch=1,
            grid=(2, 2, own),
            in_specs=[
                part(0),
                part(1),
                part(2),
                whole,
                whole,
                pl.BlockSpec((1, 1, 2, rows, rows), lambda r, j, i, at: (r * own + i, j, 0, 0, 0)),
            ],
            out_specs=[
                pl.BlockSpec((1, rows, triples.shape[2]), lambda r, j, i, at: (r, j, 0)),
                pl.BlockSpec((1, 2, 1, width // 2), lambda r, j, i, at: (r, 0, 0, 0)),
            ],
        ),
        out_shape=[pltpu.VMEM(triples.shape, jnp.bfloat16), stacked(2, 2, 1, width // 2)],
        compiler_params=pltpu.CompilerParams(vmem_limit_bytes=16 << 20),
        cost_estimate=LONG_COST,
    )(at, *[far_away(triples)] * 3, context, grad, probs)


def bucket_of(at, token_count):
    return jnp.where(at[SLOT_COUNT] == 2, token_count // 2, token_count // (at.shape[0] - LENGTHS))


def group_slot(at, group, token_count):
    slots = at.shape[0] - LENGTHS
    span = token_count // slots
    slot = (group * at[SLOT_COUNT]) // slots
    place = lax.broadcasted_iota(jnp.int32, (span, 1), 0) + group * span
    live = place - slot * bucket_of(at, token_count) < at[LENGTHS + slot]
    return slot, live.astype(jnp.float32)


def whole_block(array):
    return pl.BlockSpec(array.shape, lambda *_: (0,) * len(array.shape))


def kernel_call(kernel, grid, at, ins, in_specs, outs, out_specs, scratch=(), long=False, vmem=OTHER_VMEM):
    return pl.pallas_call(
        kernel,
        grid_spec=pltpu.PrefetchScalarGridSpec(
            num_scalar_prefetch=1, grid=grid, in_specs=in_specs, out_specs=out_specs,
            scratch_shapes=scratch,
        ),
        out_shape=outs,
        compiler_params=pltpu.CompilerParams(vmem_limit_bytes=vmem << 20),
        cost_estimate=LONG_COST if long else COST,
    )(at, *ins)


def entry_kernel(
    at, tokens, pos, weight, misc, hidden0, entry, triples, vectors, bias_lines, table, shift
):
    step = pl.program_id(0)
    rows, width = tokens.shape
    quarter = width // 2

    @pl.when(step == 0)
    def _():
        long = pos[...].astype(jnp.float32).T
        count = long.shape[0]
        span = 2 * count // (at.shape[0] - LENGTHS)
        short = jnp.concatenate([long[:span]] * (count // span), axis=0)
        table[...] = jnp.where(at[SLOT_COUNT] == 2, long, short)
        for core in range(2):
            lines = misc[core].astype(jnp.float32).T
            vectors[4 * core : 4 * core + 4] = lines[:4]
            bias_lines[2 * core : 2 * core + 2] = lines[4:6]
        shift[...] = jnp.zeros_like(shift)
        for other in range(2):
            here = pl.ds(pl.multiple_of((other ^ at[0]) * quarter, quarter), quarter)
            shift[other, :, :quarter] = vectors[BQ : BQ + 1, here]
            shift[other, :, 2 * quarter :] = vectors[BV : BV + 1, here]

    half_steps = pl.num_programs(0) // 2
    here = pl.ds(pl.multiple_of((step % half_steps) * rows, rows), rows)
    values = tokens[...].astype(jnp.float32) + table[here]
    hidden0[...] = values
    values = halved(values)
    entry[...] = values.T
    for other in range(2):
        triples[other] = halved(matmul(values, weight[other]) + shift[other])


def entered(at, tokens, pos, qkv, misc):
    token_count, width = tokens.shape
    triple = qkv.shape[2]
    outs = [
        pltpu.VMEM((token_count, width), jnp.float32),
        far_off(width, token_count),
        far_off(2, token_count, triple),
        stacked(8, width),
        stacked(4, width),
    ]
    return kernel_call(
        entry_kernel,
        (token_count // CHUNK,),
        at,
        [far_away(tokens), near_by(pos), near_by(qkv), near_by(misc)],
        tiles(tokens) + [HERE, HERE, HERE],
        outs,
        tiles(outs[0], outs[1])
        + [pl.BlockSpec((2, CHUNK, triple), lambda i, at: (0, i, 0))]
        + [whole_block(out) for out in outs[3:]],
        [
            pltpu.VMEM((token_count // 2, width), jnp.float32),
            pltpu.VMEM((2, 1, triple), jnp.float32),
        ],
    )


BQ, BV, BO, B2, G1, E1, G2, E2 = range(8)


def normal(values):
    center = values - jnp.mean(values, axis=-1, keepdims=True)
    inverse = lax.rsqrt(jnp.mean(center * center, axis=-1, keepdims=True) + EPS_NORM)
    return center * inverse, inverse


def held(array):
    return pl.BlockSpec(
        array.shape, lambda *_: (0,) * len(array.shape), pipeline_mode=pl.Buffered(buffer_count=1)
    )


def tiles(*arrays):
    return [
        pl.BlockSpec((CHUNK, a.shape[1]), lambda i, at: (i, 0))
        if a.shape[0] == arrays[0].shape[0]
        else pl.BlockSpec((a.shape[0], CHUNK), lambda i, at: (0, i))
        for a in arrays
    ]


def forward_kernel(
    at, hidden0, context, out_weight, vectors, up, up_bias, down,
    entry2, normed1, inverse1, active, slope, normed2, inverse2, block_out, pooled, units, acts,
):
    step = pl.program_id(0)
    rows, width = hidden0.shape
    token_count = rows * pl.num_programs(0)
    resid = hidden0[...] + matmul(context[...], out_weight[...]) + vectors[BO : BO + 1]
    normed, inverse = normal(resid)
    hidden1 = normed * vectors[G1 : G1 + 1] + vectors[E1 : E1 + 1]
    normed1[...], inverse1[...] = halved(normed), inverse
    entry = halved(hidden1)
    entry2[...] = entry.T
    half = up.shape[2]
    span = half // BLOCKS
    for other in range(2):
        for block in range(BLOCKS):
            here = slice(block * span, (block + 1) * span)
            there = slice(other * half + block * span, other * half + (block + 1) * span)
            values = matmul(entry, up[other, :, here]) + up_bias[other, :, here]
            cumulative = 0.5 + 0.5 * lax.erf(values * ROOT_HALF)
            acted = halved(values * cumulative)
            acts[:, there] = acted
            active[there] = acted.T
            density = jnp.exp(-0.5 * values * values) * (1.0 / ROOT_TWO_PI)
            slope[:, there] = halved(cumulative + values * density)
    total = hidden1 + vectors[B2 : B2 + 1] + matmul(acts[...], down[...])
    normed, inverse = normal(total)
    hidden2 = normed * vectors[G2 : G2 + 1] + vectors[E2 : E2 + 1]
    normed2[...], inverse2[...] = halved(normed), inverse
    block_out[...] = halved(hidden2)

    @pl.when(step == 0)
    def _():
        pooled[...] = jnp.zeros_like(pooled)

    slots = pooled.shape[0]
    span = token_count // slots
    for group in range(rows // span):
        slot, live = group_slot(at, step * (rows // span) + group, token_count)
        part = hidden2[group * span : (group + 1) * span] * live
        pooled[pl.ds(slot, 1)] += jnp.sum(part, axis=0, keepdims=True)

    @pl.when(step == pl.num_programs(0) - 1)
    def _():
        row = lax.broadcasted_iota(jnp.int32, (slots, LANES), 0)
        length = jnp.zeros((slots, LANES), jnp.int32)
        for slot in range(slots):
            length += jnp.where(row == slot, at[LENGTHS + slot], 0)
        mean = pooled[...] * (1.0 / jnp.maximum(length[:, :1], 1).astype(jnp.float32))
        pooled[...] = mean
        squares = jnp.sum(mean * mean, axis=-1, keepdims=True)
        units[:, :width] = halved(mean * lax.rsqrt(squares + EPS_NORM))
        first = lax.broadcasted_iota(jnp.int32, (slots, LANES), 1) == 0
        units[:, width:] = halved(jnp.where(first & (length > 0), 1.0, 0.0))


def forward(at, hidden0, context, out_weight, vectors, up, up_bias, down):
    token_count, width = hidden0.shape
    slots = at.shape[0] - LENGTHS
    hidden = 2 * up.shape[2]
    half = functools.partial(stacked, dtype=jnp.bfloat16)
    outs = [
        far_off(width, token_count),
        far_off(token_count, width),
        stacked(token_count, 1),
        pltpu.VMEM((hidden, token_count), jnp.bfloat16),
        pltpu.VMEM((token_count, hidden), jnp.bfloat16),
        pltpu.VMEM((token_count, width), jnp.bfloat16),
        stacked(token_count, 1),
        far_off(token_count, width),
        stacked(slots, width),
        half(slots, width + LANES),
    ]
    return kernel_call(
        forward_kernel,
        (token_count // CHUNK,),
        at,
        [near_by(hidden0), far_away(context), out_weight, vectors, near_by(up), up_bias, near_by(down)],
        tiles(hidden0, context)
        + [held(out_weight), held(vectors), HERE, held(up_bias), HERE],
        outs,
        tiles(hidden0, *outs[:8])[1:] + [whole_block(out) for out in outs[8:]],
        [pltpu.VMEM((CHUNK, hidden), jnp.bfloat16)],
        vmem=FORWARD_VMEM,
    )


def norm_back(grad, normed, inverse, gain):
    scaled = grad * gain
    inner = (
        scaled
        - jnp.mean(scaled, axis=-1, keepdims=True)
        - normed * jnp.mean(scaled * normed, axis=-1, keepdims=True)
    )
    return inner * inverse


def loss_kernel(
    at, units, others, pooled, normed2, inverse2, vectors,
    dresid, dresid_half, sums, dpool,
):
    slots, width = pooled.shape
    count = units.shape[0]
    step = pl.program_id(0)

    @pl.when(step == 0)
    def _():
        own, own_flags = units[:, :width], units[:, width:]
        other, other_flags = others[:, :width], others[:, width:]
        lane = lax.broadcasted_iota(jnp.int32, (slots, LANES), 1)
        one_hot = halved(jnp.where(lane == 0, 1.0, 0.0))
        own_row = matmul(one_hot, own_flags, NT)[:1] > 0
        other_row = matmul(one_hot, other_flags, NT)[:1] > 0

        def shares(lines, columns, live):
            logits = matmul(lines, columns, NT) * INV_TEMP
            logits = jnp.where(live, logits, NEGATIVE)
            weights = jnp.exp(logits - jnp.max(logits, axis=-1, keepdims=True))
            return weights / jnp.sum(weights, axis=-1, keepdims=True)

        row = lax.broadcasted_iota(jnp.int32, (slots, count), 0)
        column = lax.broadcasted_iota(jnp.int32, (slots, count), 1)
        target = jnp.where(row == column, 1.0, 0.0)
        row_live = own_flags[:slots, :1].astype(jnp.float32)
        dlogit = halved(LOSS_WEIGHT * (shares(own[:slots], other, other_row) - target) * row_live)
        near = shares(other, own, own_row)[:, :LANES]
        row = lax.broadcasted_iota(jnp.int32, (count, LANES), 0)
        column = lax.broadcasted_iota(jnp.int32, (count, LANES), 1)
        target = jnp.where(row == column, 1.0, 0.0)
        other_live = other_flags[:, :1].astype(jnp.float32)
        dnear = LOSS_WEIGHT * (near - target) * other_live
        dnear = halved(jnp.where(column < slots, dnear, 0.0))
        dunit = INV_TEMP * (matmul(dlogit, other) + matmul(dnear, other, TN)[:slots])
        mean = pooled[...]
        inverse = lax.rsqrt(jnp.sum(mean * mean, axis=-1, keepdims=True) + EPS_NORM)
        along = jnp.sum(mean * dunit, axis=-1, keepdims=True)
        grad = inverse * dunit - inverse * inverse * inverse * mean * along
        slot_row = lax.broadcasted_iota(jnp.int32, (slots, 1), 0)
        length = jnp.zeros((slots, 1), jnp.int32)
        for slot in range(slots):
            length += jnp.where(slot_row == slot, at[LENGTHS + slot], 0)
        dpool[...] = grad * (1.0 / jnp.maximum(length, 1).astype(jnp.float32))
        sums[...] = jnp.zeros_like(sums)

    gain = vectors[G2 : G2 + 1]
    token_count = normed2.shape[0] * pl.num_programs(0)
    span = token_count // slots
    groups = normed2.shape[0] // span
    for group in range(groups):
        here = pl.ds(group * span, span)
        slot, live = group_slot(at, step * groups + group, token_count)
        dhidden = dpool[pl.ds(slot, 1)] * live
        normed = normed2[here].astype(jnp.float32)
        values = norm_back(dhidden, normed, inverse2[here], gain)
        dresid[here] = values
        dresid_half[here] = halved(values)
        for k, terms in enumerate((values, dhidden * normed, dhidden)):
            sums[k : k + 1] += jnp.sum(terms, axis=0, keepdims=True)


def loss_back(at, units, others, pooled, normed2, inverse2, vectors):
    token_count, width = normed2.shape
    half = functools.partial(stacked, dtype=jnp.bfloat16)
    ins = [units, others, pooled, near_by(normed2), inverse2, vectors]
    outs = [
        pltpu.VMEM((token_count, width), jnp.float32),
        pltpu.VMEM((token_count, width), jnp.bfloat16),
        stacked(3, width),
    ]
    return kernel_call(
        loss_kernel,
        (token_count // CHUNK,),
        at,
        ins,
        [held(a) for a in ins[:3]] + tiles(*ins[3:5]) + [held(vectors)],
        outs,
        tiles(*outs[:2]) + [whole_block(outs[2])],
        [pltpu.VMEM(pooled.shape, jnp.float32)],
        vmem=12,
    )


def backward_kernel(
    at, dresid2, dresid2_half, slope, up, down, normed1, inverse1, vectors,
    dpre, dpre_sum, dresid, dresid_half, sums,
):
    @pl.when(pl.program_id(0) == 0)
    def _():
        dpre_sum[...] = jnp.zeros_like(dpre_sum)
        sums[...] = jnp.zeros_like(sums)

    half = up.shape[2]
    span = half // BLOCKS
    grad = dresid2_half[...]
    for block in range(2 * BLOCKS):
        here = slice(block * span, (block + 1) * span)
        dactive = matmul(grad, down[here], NT)
        values = dactive * slope[:, here].astype(jnp.float32)
        dpre_sum[:, here] += jnp.sum(values, axis=0, keepdims=True)
        dpre[:, here] = halved(values)
    dhidden = dresid2[...]
    for other in range(2):
        dhidden += matmul(dpre[:, other * half : (other + 1) * half], up[other], NT)
    normed = normed1[...].astype(jnp.float32)
    values = norm_back(dhidden, normed, inverse1[...], vectors[G1 : G1 + 1])
    dresid[...] = values
    rounded = halved(values)
    dresid_half[...] = rounded
    for k, terms in enumerate((values, dhidden * normed, dhidden)):
        sums[k : k + 1] += jnp.sum(terms, axis=0, keepdims=True)


def backward(at, dresid2, dresid2_half, slope, up, down, normed1, inverse1, vectors):
    token_count, width = dresid2.shape
    hidden = 2 * up.shape[2]
    half = functools.partial(stacked, dtype=jnp.bfloat16)
    outs = [
        pltpu.VMEM((token_count, hidden), jnp.bfloat16),
        stacked(1, hidden),
        far_off(token_count, width, dtype=jnp.float32),
        half(token_count, width),
        stacked(3, width),
    ]
    out_specs = tiles(outs[0], *outs[2:4])
    return kernel_call(
        backward_kernel,
        (token_count // CHUNK,),
        at,
        [near_by(dresid2), near_by(dresid2_half), near_by(slope), near_by(up), near_by(down), far_away(normed1), inverse1, vectors],
        tiles(dresid2, dresid2_half, slope) + [HERE, HERE] + tiles(normed1, inverse1)
        + [held(vectors)],
        outs,
        out_specs[:1] + [whole_block(outs[1])] + out_specs[1:] + [whole_block(outs[4])],
        vmem=BACKWARD_VMEM,
        long=True,
    )


def leave_kernel(
    at, dresid1, dtriples, qkv, dsums, sums1, sums2, dpre_sum, input_grad, last_own, last_away, total, turned,
):
    step = pl.program_id(0)
    rows = dresid1.shape[0]
    values = dresid1[...]
    for other in range(2):
        values = values + matmul(dtriples[other], qkv[other], NT)
    input_grad[...] = values
    half_steps = pl.num_programs(0) // 2
    here = pl.ds(pl.multiple_of((step % half_steps) * rows, rows), rows)

    @pl.when(step < half_steps)
    def _():
        total[here] = values

    @pl.when(step >= half_steps)
    def _():
        total[here] += values

    @pl.when(step == pl.num_programs(0) - 1)
    def _():
        count = total.shape[0]
        long = total[...]
        span = 2 * count // (at.shape[0] - LENGTHS)
        short = sum(long[k * span : (k + 1) * span] for k in range(count // span))
        short = jnp.concatenate([short, jnp.zeros((count - span, long.shape[1]), jnp.float32)], axis=0)
        columns = jnp.where(at[SLOT_COUNT] == 2, long, short).T
        left, right = columns[:, : count // 2], columns[:, count // 2 :]
        last_own[:, : count // 2] = jnp.where(at[0] == 0, left, right)
        last_away[:, : count // 2] = halved(jnp.where(at[0] == 0, right, left))
        width = long.shape[1]
        first = [jnp.concatenate([dsums[0, k], dsums[1, k]], axis=1) for k in range(2)]
        swapped = [jnp.concatenate([dsums[1, k], dsums[0, k]], axis=1) for k in range(2)]
        heads = [jnp.where(at[0] == 0, a, b) for a, b in zip(first, swapped)]
        vectors = [heads + [sums1[:1], sums2[:1]], [sums1[1:2], sums1[2:3], sums2[1:2], sums2[2:3]]]
        blank = jnp.zeros((LANES - 4, width), jnp.float32)
        vectors = [jnp.concatenate(rows + [blank], axis=0).T for rows in vectors]
        lane = lax.broadcasted_iota(jnp.int32, (width, LANES), 1)
        for other, (out, words) in enumerate(((last_own, False), (last_away, True))):
            row = dpre_sum[:, other * 2 * width : (other + 1) * 2 * width]
            turned[...] = jnp.broadcast_to(row, (LANES, 2 * width)).T
            lines = jnp.where(at[0] == other, vectors[0], vectors[1])
            for k in range(2):
                lines = jnp.where(lane == 4 + k, turned[pl.ds(k, width, 2)], lines)
            out[:, count // 2 :] = halved(two_words(lines)) if words else lines


def left(at, dresid1, dtriples, qkv, dsums, sums1, sums2, dpre_sum):
    token_count, width = dresid1.shape
    triple = qkv.shape[2]
    columns = token_count // 4 + LANES
    small = [dsums, sums1, sums2, dpre_sum]
    outs = [
        stacked(token_count, width),
        stacked(width, columns),
        stacked(width, columns, dtype=jnp.bfloat16),
    ]
    return kernel_call(
        leave_kernel,
        (token_count // CHUNK,),
        at,
        [far_away(dresid1), near_by(dtriples), qkv] + small,
        tiles(dresid1)
        + [pl.BlockSpec((2, CHUNK, triple), lambda i, at: (0, i, 0)), held(qkv)]
        + [held(a) for a in small],
        outs,
        tiles(outs[0]) + [whole_block(out) for out in outs[1:]],
        [
            pltpu.VMEM((token_count // 2, width), jnp.float32),
            pltpu.VMEM((2 * width, LANES), jnp.float32),
        ],
        long=True,
    )


def product_kernel(natural_order, at, left_ref, right_ref, own, away):
    values = left_ref[...]
    if len(right_ref.shape) == 3:
        first, second = matmul(values, right_ref[0]), matmul(values, right_ref[1])
    else:
        both = matmul(values, right_ref[...])
        first, second = both[:, : both.shape[1] // 2], both[:, both.shape[1] // 2 :]
    first, second = halved(first), halved(second)
    if natural_order:
        first, second = jnp.where(at[0] == 0, first, second), jnp.where(at[0] == 0, second, first)
    own[...], away[...] = first, second


def product(at, left_array, right_array, natural_order=False, near=None):
    rows, depth = left_array.shape
    columns = right_array.size // depth // 2
    tile = rows // 6 if rows > 1024 else rows // 3
    outs = [stacked(rows, columns, dtype=jnp.bfloat16)] * 2
    return kernel_call(
        functools.partial(product_kernel, natural_order),
        (rows // tile,),
        at,
        [near_by(left_array) if near in (0, 2) else left_array, near_by(right_array) if near in (1, 2) else right_array],
        [pl.BlockSpec((tile, depth), lambda i, at: (i, 0)), HERE if near in (1, 2) else held(right_array)],
        outs,
        [pl.BlockSpec((tile, columns), lambda i, at: (i, 0))] * 2,
        long=True,
        vmem=PRODUCT_VMEM,
    )


def renew(grad, moment, weight, average, rate):
    moment_new = MOMENTUM * moment + grad
    weight_new = weight - rate * (grad + MOMENTUM * moment_new)
    average_new = AVERAGE * average + (1.0 - AVERAGE) * weight_new
    return (grad, moment_new, weight_new, average_new)


def finish_kernel(kept, first, second, third, out_grad, *refs):
    states, outs = refs[:9], refs[9:]
    quarter = out_grad.shape[1]
    total = kept[...]
    for part in (first, second, third):
        total = total + received(part[...], True)

    def write(at, grad, state, results, rate):
        for result, value in zip(results, renew(grad, *[ref[at] for ref in state], rate), strict=True):
            result[at] = value

    for k in range(4):
        grad = total[:, k * quarter : (k + 1) * quarter] if k < 3 else out_grad[...]
        write((k,), grad, states[:3], outs[:4], RATE)
    lines = total[:, -LANES:].T
    write((Ellipsis,), lines[:4], states[3:6], outs[4:8], RATE)
    write((Ellipsis,), total[:, 3 * quarter : -LANES], states[6:], outs[8:12], POS_RATE)
    rows = kept.shape[0]
    row = lax.broadcasted_iota(jnp.int32, (rows, 2 * rows), 0)
    column = lax.broadcasted_iota(jnp.int32, (rows, 2 * rows), 1)
    bias = jnp.zeros((8, 2 * rows), jnp.float32)
    for k in range(2):
        chosen = jnp.where(column == 2 * row + k, 1.0, 0.0)
        line = jnp.broadcast_to(lines[4 + k : 5 + k], (8, rows))
        bias = bias + jnp.dot(
            line, chosen, precision=lax.Precision.HIGHEST, preferred_element_type=jnp.float32
        )
    outs[12][...] = bias[:1]


def finished(kept, arrived, out_grad, attn_state, vector_state, pos_state):
    pos_state = tuple(part.T for part in pos_state)
    states = attn_state + vector_state + pos_state
    outs = [stacked(*state[0].shape) for state in (attn_state, vector_state, pos_state) for _ in range(4)]
    outs.append(stacked(1, 2 * kept.shape[0]))
    out = pl.pallas_call(
        finish_kernel,
        in_specs=[HERE] * (5 + len(states)),
        out_specs=[HERE] * len(outs),
        out_shape=outs,
        compiler_params=pltpu.CompilerParams(vmem_limit_bytes=20 << 20),
        cost_estimate=COST,
    )(kept, *arrived, out_grad, *states)
    return out[:4], out[4:8], [part.T for part in out[8:12]], out[12]


def local(
    tokens,
    lengths,
    attn_weight,
    attn_moment,
    attn_average,
    up_weight,
    up_moment,
    up_average,
    down_weight,
    down_moment,
    down_average,
    layer_vectors,
    vector_moment,
    vector_average,
    up_bias,
    bias_moment,
    bias_average,
    pos_table,
    pos_moment,
    pos_average,
):
    at = scalars(lengths[0, 0])
    stream = at[0]
    upper = stream == 1
    devices = lax.axis_size("batch")
    rows, hidden_half = up_weight.shape
    quarter = attn_weight.shape[2]
    width = 2 * quarter
    pos_half = pos_table.shape[0]
    slot_count = lengths.shape[2]

    misc = jnp.concatenate([layer_vectors.T, up_bias.reshape(rows, 2)], axis=1)
    misc = jnp.pad(misc, ((0, 0), (0, LANES - misc.shape[1])))
    entry_block = halved(
        jnp.concatenate([attn_weight[0], attn_weight[1], attn_weight[2], pos_table.T, misc], axis=1)
    )
    middle_block = halved(
        jnp.concatenate([up_weight, attn_weight[3], jnp.zeros((rows, LANES), jnp.float32)], axis=1)
    )
    triple = 3 * quarter
    pos_stop = triple + pos_half
    entry_gather = Gather(entry_block, width)
    entry_gather.far()
    down_both = lax.all_gather(
        after(halved(down_weight), entry_gather.blocks), ("stream", "batch"), axis=0, tiled=True
    )
    entry_gather.near((2, 1))
    middle_gather = Gather(
        after(middle_block, *entry_gather.sides), (hidden_half + quarter + LANES) // 2
    )
    middle_gather.far()
    entry_gather.near((1, 2), middle_gather.blocks)
    qkv_blocks, pos_blocks, misc_blocks = entry_gather.placed(
        at,
        (
            (0, triple, 0, "relative", 0, 0),
            (triple, pos_stop, 1, "", 0, pos_half),
            (pos_stop, pos_stop + LANES, 2, "stream", 0, 0),
        ),
        [
            pltpu.VMEM((2, devices, rows, triple), jnp.bfloat16),
            pltpu.VMEM((devices, rows, 2 * pos_half), jnp.bfloat16),
            pltpu.VMEM((2, devices, rows, LANES), jnp.bfloat16),
        ],
    )
    qkv = qkv_blocks.reshape(2, width, triple)
    pos_full = pos_blocks.reshape(width, 2 * pos_half)
    def own_first(pair):
        return jnp.where(upper, pair[::-1], pair)

    hidden0, entry, triples, vectors, bias_lines = entered(
        at, tokens[0], pos_full, qkv, misc_blocks.reshape(2, width, LANES)
    )
    biases = bias_lines.reshape(2, 2, width).transpose(0, 2, 1).reshape(2, 1, hidden_half)
    middle_gather.near((2, 1), triples)
    context_half, context_turned, probs = attend(after(at, *middle_gather.sides), triples)
    middle_gather.near((1, 2), context_half)
    up_blocks, out_blocks, down = middle_gather.placed(
        after(at, context_half),
        (
            (0, hidden_half, 0, "relative", 0, 0),
            (hidden_half, hidden_half + quarter, 1, "", 0, quarter),
        ),
        [
            pltpu.VMEM((2, devices, rows, hidden_half), jnp.bfloat16),
            stacked(devices, rows, width, dtype=jnp.bfloat16),
        ],
        down_both.reshape(2, 2 * hidden_half, quarter),
    )
    up = up_blocks.reshape(2, width, hidden_half)
    out_full = out_blocks.reshape(width, width)
    (entry2, normed1, inverse1, active, slope, normed2, inverse2, block_out, pooled, units) = forward(
        at, hidden0, context_half, out_full, vectors, up, own_first(biases), down
    )

    units = units[None]
    bit = 0
    while 1 << bit < devices:
        step = min(2, devices.bit_length() - 1 - bit)
        arrived = [exchanged(units, "batch", d << bit) for d in range(1, 1 << step)]
        units = jnp.concatenate([units] + arrived, axis=0)
        bit += step
    units = units.reshape(-1, units.shape[2])
    others = exchanged(units, "stream", 1)
    dresid2, dresid2_half, sums2 = loss_back(
        at, units, others, pooled, normed2, inverse2, vectors
    )

    def blocks(values):
        return values.reshape(devices // 4, 2, 2, values.shape[0] // devices, values.shape[1])

    down_own, down_away = product(at, active, dresid2_half, True, near=2)
    down_in = exchanged(down_away, "stream", 1)
    by_rows = down_weight.shape[0] % 32 == 0
    half_rows = down_weight.shape[0] // 2
    down_pair = (blocks(down_own), blocks(down_in))
    if by_rows:
        down_sides = [[down_pair + (half_rows, k, quarter, 0, True)] for k in range(2)]
    else:
        down_sides = [
            [down_pair + (2 * half_rows, 0, LANES, k, True) for k in ks] for ks in ((0, 1), (2,))
        ]
    down_fold = Fold(at, down_sides)
    down_parts = down_fold.first()
    down_first = down_fold.first_sent(down_parts)
    dpre, dpre_sum, dresid1, dresid1_half, sums1 = backward(
        after(at, *down_parts), dresid2, dresid2_half, slope, up, down, normed1, inverse1, vectors
    )
    down_fold.at = after(at, dresid1_half, *down_first)
    down_parts = down_fold.second(down_first)
    down_second, down_kept = down_fold.second_sent(down_parts)
    up_own, up_away = product(after(at, *down_parts), entry2, dpre, near=1)
    up_in = exchanged(up_away, "stream", 1)
    out_own, out_away = product(
        after(at, up_away, *down_second), context_turned, dresid1_half, True
    )
    out_in = exchanged(out_away, "stream", 1)
    down_fold.at = after(at, out_own, *down_second)
    down_last = down_fold.third(down_second, down_kept)
    down_third = down_fold.third_sent(down_last)
    third = hidden_half // 3
    up_pair = (blocks(up_own), blocks(up_in))
    out_pair = (blocks(out_own), blocks(out_in))
    middle_fold = Fold(
        after(at, *down_last),
        [
            [up_pair + (rows, 0, third, 0, False), up_pair + (rows, 0, third, 1, False)],
            [up_pair + (rows, 0, third, 2, False), out_pair + (rows, 0, quarter, 0, False)],
        ],
    )
    middle_parts = middle_fold.first()
    middle_first = middle_fold.first_sent(middle_parts)
    dcontext_half = halved(matmul(after(dresid1_half, *middle_parts), out_full, NT))
    dtriples, dsums = attend_back(at, triples, context_half, dcontext_half, probs)
    qkv_own, qkv_away = product(at, entry, dtriples, near=1)
    qkv_in = exchanged(qkv_away, "stream", 1)
    middle_fold.at = after(at, qkv_away, *middle_first)
    middle_parts = middle_fold.second(middle_first)
    middle_second, middle_kept = middle_fold.second_sent(middle_parts)
    input_grad, last_own, last_away = left(
        after(at, qkv_away, *middle_parts, *down_third), dresid1, dtriples, qkv, dsums, sums1, sums2, dpre_sum
    )
    last_in = exchanged(last_away, "stream", 1)
    qkv_pair = (blocks(qkv_own), blocks(qkv_in))
    last_pair = (blocks(last_own), blocks(last_in))
    entry_fold = Fold(
        at,
        [
            [qkv_pair + (rows, 0, quarter, 0, False), qkv_pair + (rows, 0, quarter, 1, False)],
            [
                qkv_pair + (rows, 0, quarter, 2, False),
                last_pair + (rows, 0, pos_half, 0, False),
                last_pair + (rows, 0, LANES, pos_half // LANES, False),
            ],
        ],
        wide=True,
    )
    entry_parts = entry_fold.first()
    entry_first = entry_fold.first_sent(entry_parts)
    middle_fold.at = after(at, *entry_parts, *middle_second)
    middle_parts = middle_fold.third(middle_second, middle_kept)
    entry_fold.at = after(at, *middle_parts)
    entry_parts = entry_fold.second(entry_first)
    middle_third = middle_fold.third_sent(middle_parts)
    middle_sum = middle_fold.total(middle_parts[0], middle_third, *entry_parts)
    down_sum = down_fold.total(down_last[0], down_third, *entry_parts)
    entry_second, entry_kept = entry_fold.second_sent(entry_parts)
    entry_parts = entry_fold.third(entry_second, entry_kept)
    vector_moment, vector_average = (
        after(part, *entry_parts) for part in (vector_moment, vector_average)
    )
    entry_third = entry_fold.third_sent(entry_parts)

    down_grad = down_sum
    if by_rows:
        down_grad = jnp.concatenate([down_sum[:, :quarter], down_sum[:, quarter:]], axis=0)
    up_all = renew(middle_sum[:, :hidden_half], up_moment, up_weight, up_average, RATE)
    down_all = renew(down_grad, down_moment, down_weight, down_average, RATE)
    out_grad = middle_sum[:, hidden_half : hidden_half + quarter]
    attn_state = (attn_moment, attn_weight, attn_average)
    vector_state = (vector_moment, layer_vectors, vector_average)
    pos_state = (pos_moment, pos_table, pos_average)
    if rows % 16 == 0:
        attn_all, vector_all, pos_all, bias_grad = finished(
            entry_parts[0][0], [part[0] for part in entry_third], out_grad, attn_state, vector_state, pos_state
        )
        bias_grad = bias_grad.reshape(-1)
    else:
        entry_sum = entry_fold.total(entry_parts[0], entry_third)
        attn_grad = jnp.stack(
            [entry_sum[:, k * quarter : (k + 1) * quarter] for k in range(3)] + [out_grad]
        )
        attn_all = renew(attn_grad, *attn_state, RATE)
        vector_all = renew(entry_sum[:, pos_stop : pos_stop + 4].T, *vector_state, RATE)
        pos_all = renew(entry_sum[:, triple:pos_stop].T, *pos_state, POS_RATE)
        bias_grad = entry_sum[:, pos_stop + 4 : pos_stop + 6].reshape(-1)
    bias_all = renew(bias_grad, bias_moment, up_bias, bias_average, RATE)
    return (
        block_out[None],
        input_grad[None],
        *attn_all,
        *up_all,
        *down_all,
        *vector_all,
        *bias_all,
        *pos_all,
    )


def solution(mesh):
    tokens_at, weight_at = P("stream", "batch", None), P("batch", "stream")
    attn_at, rows_at, bias_at = P(None, "batch", "stream"), P("stream", "batch"), P(("stream", "batch"))
    kinds = (attn_at, weight_at, weight_at, rows_at, bias_at, rows_at)
    in_specs = (tokens_at, tokens_at) + tuple(kind for kind in kinds for _ in range(3))
    out_specs = (tokens_at, tokens_at) + tuple(kind for kind in kinds for _ in range(4))
    return jax.shard_map(local, mesh=mesh, in_specs=in_specs, out_specs=out_specs, check_vma=False)
```
